512 devices in a mesh: seq: 128 (over x, z_lo, y, core), head: 4 (over z_hi).
Axes of the slice: x: 4, y: 8, z: 8 (z_hi: 4, z_lo: 2; z = z_hi * 2 + z_lo), core: 2. Of those that a mesh axis runs over, the one named last changes fastest.
Arguments:
- queries: bfloat16 [8192, 12, 128], P('seq', 'head'), may hold values from -6 to 6
- keys: bfloat16 [8192, 12, 128], P('seq', 'head'), may hold values from -6 to 6
- values: bfloat16 [8192, 12, 128], P('seq', 'head'), may hold values from -6 to 6
- out_weight: bfloat16 [768, 768], P('head'), may hold values from -0.21875 to 0.21875
- offsets: int32 [12], P('head'), may hold values from 0 to 127
- out_grad: bfloat16 [8192, 1536], P('seq', 'head'), may hold values from -6 to 6
Outputs:
- output: bfloat16 [8192, 1536], P('seq', 'head')
- query_grad: bfloat16 [8192, 12, 128], P('seq', 'head')
- key_grad: bfloat16 [8192, 12, 128], P('seq', 'head')
- value_grad: bfloat16 [8192, 12, 128], P('seq', 'head')
- weight_grad: float32 [768, 768], P('head')
The draws below stay inside these ranges and needn't reach their ends.
All inputs are finite; a program needn't handle non-finite values.
Results may differ from the reference program's by a relative error of at most 0.029.
Values may be sent and summed in bfloat16 or wider, within the bound.
No kernel may reach another device: no remote copies, remote signals or barrier semaphores. Data moves between devices by JAX's collectives and lax.ppermute only.
A program may use at most 64 MiB of HBM per device.

```python
import jax
import jax.numpy as jnp
from jax import lax

WIDTH = 768
HEADS = 12
HEAD_DIM = 64
ROWS = 128
TOKENS = 16384
LEVELS = 8
N_SEQ = 128


def pair_layout(flat):
    return flat.reshape(TOKENS // 2, 2, HEADS, HEAD_DIM).transpose(0, 2, 1, 3).reshape(TOKENS // 2, HEADS, 2 * HEAD_DIM)


def draw_queries(key, part):
    key = jax.random.fold_in(key, 11)
    drawn = jnp.clip(jax.random.normal(key, (TOKENS, HEADS * HEAD_DIM)), -4.0, 4.0)
    return pair_layout(drawn.astype(jnp.float32)).astype(jnp.bfloat16)


def draw_keys(key, part):
    key = jax.random.fold_in(key, 12)
    drawn = jnp.clip(jax.random.normal(key, (TOKENS, HEADS * HEAD_DIM)), -4.0, 4.0)
    return pair_layout(drawn.astype(jnp.float32)).astype(jnp.bfloat16)


def place_ends(array, rng, smallest, high):
    shape = array.shape
    spot = [jax.random.randint(jax.random.fold_in(rng, axis), (), 0, shape[axis]) for axis in range(len(shape))]
    array = array.at[tuple(spot)].set(smallest)
    longest = shape.index(max(shape))
    spot[longest] = (spot[longest] + 1) % shape[longest]
    return array.at[tuple(spot)].set(high)


def block_levels(stream_key, extent, pieces, least, largest):
    loudness = 1.0
    for axis_at, shards_of in pieces:
        steps = jax.random.uniform(jax.random.fold_in(jax.random.fold_in(stream_key, 6), axis_at), (shards_of,), jnp.float32, least / len(pieces), largest / len(pieces))
        loudness = loudness * jnp.repeat(jnp.exp(steps), extent[axis_at] // shards_of).reshape((-1,) + (1,) * (len(extent) - 1 - axis_at))
    return loudness


def centred(own_key, shape, scale, most, pieces=(), held_as=jnp.bfloat16):
    factor_of = block_levels(own_key, shape, pieces, -0.22, 0.18) if pieces else 1.0
    entries = jax.random.normal(own_key, shape, jnp.float32) * scale * factor_of
    return jnp.minimum(jnp.maximum(entries, -most), most).astype(held_as)


def setup_inputs(seed: int = 0) -> dict:
    seeds = jax.random.split(jax.random.key(seed), 7)
    return {
        "queries": draw_queries(jax.random.fold_in(seeds[6], 71), 0),
        "keys": draw_keys(jax.random.fold_in(seeds[6], 71), 0),
        "values": centred(seeds[2], (TOKENS // 2, HEADS, 2 * HEAD_DIM), 1.0, 6.0, ((0, 128), (1, 4))),
        "out_weight": centred(seeds[3], (HEADS * HEAD_DIM, WIDTH), (HEADS * HEAD_DIM) ** -0.5, 0.21875, ((0, 4),)),
        "offsets": place_ends(jax.random.randint(seeds[4], (HEADS,), 0, N_SEQ), jax.random.fold_in(seeds[4], 1), 0, N_SEQ - 1).astype(jnp.int32),
        "out_grad": centred(seeds[5], (TOKENS // 2, 2 * WIDTH), 1.0, 6.0, ((0, 128), (1, 4))),
    }


def pick(block, stride, shift):
    rows = block.reshape((block.shape[0] // stride, stride) + block.shape[1:])
    return lax.dynamic_index_in_dim(rows, shift, 1, keepdims=False)


def place(part, stride, shift, fill):
    whole = jnp.full((part.shape[0], stride) + part.shape[1:], fill, part.dtype)
    whole = lax.dynamic_update_index_in_dim(whole, part, shift, 1)
    return whole.reshape((part.shape[0] * stride,) + part.shape[1:])


def to_bf16_f32(values_in):
    return lax.optimization_barrier(values_in.astype(jnp.bfloat16)).astype(jnp.float32)


def unpack_pairs(packed):
    pairs = packed.shape[0]
    return packed.reshape(pairs, HEADS, 2, HEAD_DIM).transpose(0, 2, 1, 3).reshape(pairs * 2, HEADS * HEAD_DIM)


def pack_pairs(flat):
    pairs = flat.shape[0] // 2
    return flat.reshape(pairs, 2, HEADS, HEAD_DIM).transpose(0, 2, 1, 3).reshape(pairs, HEADS, 2 * HEAD_DIM)


def head_forward(query, key_rows, value_rows, offset):
    scale = HEAD_DIM ** -0.5
    outs = []
    lses = []
    for level in range(LEVELS):
        stride = 2 ** level
        shift = (offset % stride).astype(jnp.int32)
        groups = N_SEQ // stride
        q_seg = pick(query, stride, shift).reshape(groups, ROWS, HEAD_DIM).astype(jnp.float32)
        k_seg = pick(key_rows, stride, shift).reshape(groups, ROWS, HEAD_DIM).astype(jnp.float32)
        v_seg = pick(value_rows, stride, shift).reshape(groups, ROWS, HEAD_DIM).astype(jnp.float32)
        scores = jnp.einsum('gqd,gkd->gqk', q_seg, k_seg) * scale
        top = jnp.max(scores, axis=2, keepdims=True)
        expd = jnp.exp(scores - top)
        total = jnp.sum(expd, axis=2, keepdims=True)
        probs = to_bf16_f32(expd / total)
        part = jnp.einsum('gqk,gkd->gqd', probs, v_seg)
        lse = (top + jnp.log(total))[..., 0].reshape(-1)
        outs.append(place(part.reshape(-1, HEAD_DIM), stride, shift, 0.0))
        lses.append(place(lse, stride, shift, -jnp.inf))
    stacked = jnp.stack(lses)
    top = jnp.max(stacked, axis=0)
    lse_all = top + jnp.log(jnp.sum(jnp.exp(stacked - top), axis=0))
    combined = outs[0] * jnp.exp(lses[0] - lse_all)[:, None]
    for level in range(1, LEVELS):
        combined = combined + outs[level] * jnp.exp(lses[level] - lse_all)[:, None]
    return combined.astype(jnp.bfloat16), lse_all


def head_backward(query, key_rows, value_rows, offset, grad_rows, attn_rows, lse_all):
    scale = HEAD_DIM ** -0.5
    delta = jnp.sum(grad_rows.astype(jnp.float32) * attn_rows.astype(jnp.float32), axis=1)
    dq_sum = jnp.zeros((TOKENS, HEAD_DIM), jnp.float32)
    dk_sum = jnp.zeros((TOKENS, HEAD_DIM), jnp.float32)
    dv_sum = jnp.zeros((TOKENS, HEAD_DIM), jnp.float32)
    for level in range(LEVELS):
        stride = 2 ** level
        shift = (offset % stride).astype(jnp.int32)
        groups = N_SEQ // stride
        q_seg = pick(query, stride, shift).reshape(groups, ROWS, HEAD_DIM).astype(jnp.float32)
        k_seg = pick(key_rows, stride, shift).reshape(groups, ROWS, HEAD_DIM).astype(jnp.float32)
        v_seg = pick(value_rows, stride, shift).reshape(groups, ROWS, HEAD_DIM).astype(jnp.float32)
        g_seg = pick(grad_rows, stride, shift).reshape(groups, ROWS, HEAD_DIM).astype(jnp.float32)
        lse_seg = pick(lse_all, stride, shift).reshape(groups, ROWS, 1)
        delta_seg = pick(delta, stride, shift).reshape(groups, ROWS, 1)
        scores = jnp.einsum('gqd,gkd->gqk', q_seg, k_seg) * scale
        probs = jnp.exp(scores - lse_seg)
        rounded = to_bf16_f32(probs)
        dv_part = jnp.einsum('gqk,gqd->gkd', rounded, g_seg)
        dprob = jnp.einsum('gqd,gkd->gqk', g_seg, v_seg)
        dscore = to_bf16_f32(probs * (dprob - delta_seg) * scale)
        dq_part = jnp.einsum('gqk,gkd->gqd', dscore, k_seg)
        dk_part = jnp.einsum('gqk,gqd->gkd', dscore, q_seg)
        dq_sum = dq_sum + place(dq_part.reshape(-1, HEAD_DIM), stride, shift, 0.0)
        dk_sum = dk_sum + place(dk_part.reshape(-1, HEAD_DIM), stride, shift, 0.0)
        dv_sum = dv_sum + place(dv_part.reshape(-1, HEAD_DIM), stride, shift, 0.0)
    return dq_sum.astype(jnp.bfloat16), dk_sum.astype(jnp.bfloat16), dv_sum.astype(jnp.bfloat16)


def reference(queries, keys, values, out_weight, offsets, out_grad):
    flat_q = unpack_pairs(queries)
    flat_k = unpack_pairs(keys)
    flat_v = unpack_pairs(values)
    grad_flat = out_grad.reshape(TOKENS, WIDTH)
    heads_out = []
    heads_lse = []
    for head in range(HEADS):
        cols = slice(head * HEAD_DIM, (head + 1) * HEAD_DIM)
        attn_head, lse_head = head_forward(flat_q[:, cols], flat_k[:, cols], flat_v[:, cols], offsets[head])
        heads_out.append(attn_head)
        heads_lse.append(lse_head)
    attn = jnp.concatenate(heads_out, axis=1)
    output = jnp.dot(attn, out_weight, preferred_element_type=jnp.float32).astype(jnp.bfloat16)
    d_attn = jnp.dot(grad_flat, out_weight.T, preferred_element_type=jnp.float32).astype(jnp.bfloat16)
    weight_grad = jnp.dot(attn.T, grad_flat, preferred_element_type=jnp.float32)
    dq_list = []
    dk_list = []
    dv_list = []
    for head in range(HEADS):
        cols = slice(head * HEAD_DIM, (head + 1) * HEAD_DIM)
        dq_head, dk_head, dv_head = head_backward(flat_q[:, cols], flat_k[:, cols], flat_v[:, cols], offsets[head], d_attn[:, cols], attn[:, cols], heads_lse[head])
        dq_list.append(dq_head)
        dk_list.append(dk_head)
        dv_list.append(dv_head)
    query_grad = pack_pairs(jnp.concatenate(dq_list, axis=1))
    key_grad = pack_pairs(jnp.concatenate(dk_list, axis=1))
    value_grad = pack_pairs(jnp.concatenate(dv_list, axis=1))
    output = output.reshape(TOKENS // 2, 2 * WIDTH)
    return output, query_grad, key_grad, value_grad, weight_grad
```

```python
import math

import jax
import jax.numpy as jnp
import numpy as np
from jax import lax
from jax.experimental import pallas as pl
from jax.experimental.pallas import tpu as pltpu
from jax.sharding import PartitionSpec as P

FAR, LINE, CORE = 8, 8, 2
ROWS = 128
LOCAL = 3
SIZE = 64
LANES = LOCAL * 2 * SIZE
WIDTH = 768
HALF = WIDTH // 2
SCALE = SIZE**-0.5
NEAR = 32
PICKED = 16
BLOCK = NEAR + PICKED
REACH = LINE * BLOCK
PARTNER_AT = ROWS + REACH
OTHER_AT = PARTNER_AT + NEAR
KEYS = OTHER_AT + REACH
SHARE = 192
SEND = REACH + NEAR + SHARE
PART = SHARE // LINE
FINAL = PART // FAR

NT = (((1,), (1,)), ((), ()))
TN = (((0,), (0,)), ((), ()))
NN = (((1,), (0,)), ((), ()))
BF16 = jnp.bfloat16
F32 = jnp.float32


def dot(a, b, dims=NN):
    return lax.dot_general(a, b, dims, preferred_element_type=F32)


def depth_of(row):
    return 7 if row == 0 else 7 - row.bit_length()


def far_rows():
    rows = [(1, i) for i in range(4)] + [(d, i) for d in (2, 3) for i in range(2)]
    return rows + [(d, 0) for d in range(4, 8)]


def key_table():
    table = [(-1, depth_of(row)) for row in range(ROWS)]
    for core in range(CORE):
        if core:
            table += [(0, depth_of(NEAR + row)) for row in range(NEAR)]
        for line in range(LINE):
            distance = 2 * line + core
            for row in range(NEAR):
                table.append((distance.bit_length() - 1, depth_of(row)) if distance else None)
            table += [(3 + far.bit_length(), depth_of(row)) for far, row in far_rows()]
            table += [None] * (PICKED - 12)
    return table


def shared_levels():
    table = key_table()
    bias = np.full((KEYS, ROWS), -1e30, np.float32)
    for key, entry in enumerate(table):
        if entry is None:
            continue
        for query in range(ROWS):
            count = min(entry[1], depth_of(query)) - entry[0]
            if count > 0:
                bias[key, query] = math.log(count)
    return bias


def reversed_bits(row):
    out = row * 0
    for bit in range(7):
        out = out | ((row >> bit) & 1) << (6 - bit)
    return out


def token_of(row):
    return jnp.where(row < SIZE, 2 * row, 2 * row - (ROWS - 1))


def one_hot(match):
    return jnp.where(match, 1.0, 0.0).astype(BF16)


def order_from(offset, row_axis):
    row = lax.broadcasted_iota(jnp.int32, (ROWS, ROWS), row_axis)
    token = token_of(lax.broadcasted_iota(jnp.int32, (ROWS, ROWS), 1 - row_axis))
    return one_hot(((reversed_bits(row) + offset) & (ROWS - 1)) == token)


def lane_iota(shape):
    return lax.broadcasted_iota(jnp.int32, shape, len(shape) - 1)


def beside(first, second):
    low = lane_iota(first.shape) < SIZE
    even = jnp.where(low, first, pltpu.roll(second, SIZE, 1))
    odd = jnp.where(low, pltpu.roll(first, SIZE, 1), second)
    return jnp.concatenate([even, odd], axis=0).astype(BF16)


def start_kernel(offsets, keys, values, grad, ordered, far_out, partner_out, grad_out):
    for head in range(LOCAL):
        lanes = pl.ds(head * 2 * SIZE, 2 * SIZE)
        both = beside(keys[:, head, :].astype(F32), values[:, head, :].astype(F32))
        ordered[:, lanes] = dot(order_from(offsets[head], 0), both).astype(BF16)
    for slot in range(FAR):
        far_out[slot] = ordered[0:8, :]
    partner_out[...] = ordered[NEAR : 2 * NEAR, :]
    for slot in range(4):
        grad_out[slot] = grad[...]


def far_place(row, far):
    distance = jnp.where(row < 4, 1, jnp.where(row < 6, 2, jnp.where(row < 8, 3, row - 4)))
    index = jnp.where(row < 4, row, jnp.where(row < 8, row & 1, 0))
    return jnp.where(row < 12, (far ^ distance) * 8 + index, -1)


def line_kernel(rank, ordered, far_in, line_out):
    row = lax.broadcasted_iota(jnp.int32, (PICKED, FAR * 8), 0)
    column = lax.broadcasted_iota(jnp.int32, (PICKED, FAR * 8), 1)
    choose = one_hot(far_place(row, rank[0]) == column)
    picked = dot(choose, far_in[...].reshape(FAR * 8, LANES)).astype(BF16)
    for slot in range(LINE):
        line_out[slot, 0:NEAR, :] = ordered[0:NEAR, :]
        line_out[slot, NEAR:BLOCK, :] = picked


def main_kernel(
    rank, offsets, queries, weight, grads, ordered, line_in, partner_in, other_in, bias,
    output_part, query_grad, send, keep_line, keep_own, keep_weight,
    held, full_grad, attn, weight_term,
):
    line, core = rank[1], rank[2]
    held[0:ROWS, :] = ordered[...]
    held[PARTNER_AT:OTHER_AT, :] = partner_in[...]
    for step in range(LINE):
        slot = line ^ step
        held[ROWS + step * BLOCK : ROWS + (step + 1) * BLOCK, :] = line_in[slot]
        held[OTHER_AT + step * BLOCK : OTHER_AT + (step + 1) * BLOCK, :] = other_in[slot]
    for parity in range(2):
        for half in range(2):
            full_grad[parity * SIZE : (parity + 1) * SIZE, half * HALF : (half + 1) * HALF] = grads[2 * parity + half]
    for head in range(LOCAL):
        lanes = pl.ds(head * 2 * SIZE, 2 * SIZE)
        to_order = order_from(offsets[head], 0)
        to_token = order_from(offsets[head], 1)
        pairs = queries[:, head, :].astype(F32)
        query = dot(to_order, beside(pairs, jnp.zeros_like(pairs))).astype(BF16)
        head_weight = weight[head * SIZE : (head + 1) * SIZE, :]
        grad = dot(full_grad[...], head_weight, NT).astype(BF16)
        grad = dot(to_order, jnp.concatenate([jnp.zeros_like(grad), grad], axis=1)).astype(BF16)
        beside_grad = jnp.concatenate([query, grad], axis=0)
        both = held[:, lanes]
        products = dot(both, beside_grad, NT)
        scores = products[:, :ROWS] * SCALE + bias[...]
        top = jnp.max(scores, axis=0, keepdims=True)
        expd = jnp.exp(scores - top)
        probs = expd / jnp.sum(expd, axis=0, keepdims=True)
        rounded = probs.astype(BF16)
        attn_head = dot(both, rounded, TN)[SIZE:, :].astype(BF16)
        grad_side = grad.astype(F32).T
        delta = jnp.sum(grad_side[SIZE:, :] * attn_head.astype(F32), axis=0, keepdims=True)
        dscore = (probs * (products[:, ROWS:] - delta) * SCALE).astype(BF16)
        dquery = dot(both, dscore, TN)[:SIZE, :].astype(BF16)
        attn[:, head * SIZE : (head + 1) * SIZE] = dot(to_token, attn_head, NT).astype(BF16)
        by_token = dot(to_token, jnp.concatenate([dquery, jnp.zeros_like(dquery)], axis=0), NT)
        query_grad[:, head, :] = (by_token[:SIZE] + pltpu.roll(by_token[SIZE:], SIZE, 1)).astype(BF16)
        dboth = dot(jnp.concatenate([dscore, rounded], axis=1), beside_grad)
        keep_own[:, lanes] = dboth[0:ROWS]
        send[REACH : REACH + NEAR, lanes] = dboth[PARTNER_AT:OTHER_AT].astype(BF16)
        for step in range(LINE):
            slot = line ^ step
            keep_line[slot, :, lanes] = dboth[ROWS + step * BLOCK : ROWS + (step + 1) * BLOCK]
            at = pl.multiple_of(slot * BLOCK, 16)
            send[pl.ds(at, BLOCK), lanes] = dboth[OTHER_AT + step * BLOCK : OTHER_AT + (step + 1) * BLOCK].astype(BF16)
    part = dot(attn[...], weight[...])
    output_part[:, :WIDTH] = part[:SIZE]
    output_part[:, WIDTH:] = part[SIZE:]
    weight_term[...] = dot(attn[...], full_grad[...], TN)
    rows = SHARE // 2
    mine = pl.ds(pl.multiple_of(core * rows, 8), rows)
    theirs = pl.ds(pl.multiple_of((1 - core) * rows, 8), rows)
    for half in range(2):
        columns = pl.ds(half * HALF, HALF)
        keep_weight[half * rows : (half + 1) * rows, :] = weight_term[mine, columns]
        at = REACH + NEAR + half * rows
        send[at : at + rows, :] = weight_term[theirs, columns].astype(BF16)


def line_return_kernel(received, keep_line, keep_weight, line_out):
    for slot in range(LINE):
        rows = slice(slot * BLOCK, (slot + 1) * BLOCK)
        line_out[slot, 0:BLOCK, :] = (keep_line[slot] + received[rows, :].astype(F32)).astype(BF16)
        part = slice(slot * PART, (slot + 1) * PART)
        at = REACH + NEAR + slot * PART
        line_out[slot, BLOCK:, :] = (keep_weight[part, :] + received[at : at + PART, :].astype(F32)).astype(BF16)


def far_return_kernel(rank, line_in, near_sum, far_out):
    total = line_in[0].astype(F32)
    for slot in range(1, LINE):
        total = total + line_in[slot].astype(F32)
    near_sum[...] = total[:NEAR]
    shape = (FAR * 8, PICKED + PART)
    place = lax.broadcasted_iota(jnp.int32, shape, 0)
    column = lax.broadcasted_iota(jnp.int32, shape, 1)
    slot, row = place >> 3, place & 7
    term = PICKED + slot * FINAL + row - 4
    choose = ((row < 4) & (column < 12) & (far_place(column, rank[0]) == place)) | (
        (row >= 4) & (row < 4 + FINAL) & (column == term)
    )
    picked = dot(one_hot(choose), total[NEAR:].astype(BF16)).astype(BF16)
    far_out[...] = picked.reshape(FAR, 8, LANES)


def spread_kernel(far_in, far_sum, spread_out):
    total = far_in[0].astype(F32)
    for slot in range(1, FAR):
        total = total + far_in[slot].astype(F32)
    far_sum[...] = total
    part = total[4:8].astype(BF16)
    spread_out[...] = jnp.broadcast_to(part[None], spread_out.shape)


def finish_kernel(offsets, keep_own, received, near_sum, far_sum, spread_in, key_grad, value_grad, weight_grad, own):
    own[...] = keep_own[...]
    own[NEAR : 2 * NEAR, :] += received[REACH : REACH + NEAR, :].astype(F32)
    own[0:NEAR, :] += near_sum[...]
    row = lax.broadcasted_iota(jnp.int32, (8, LANES), 0)
    own[0:8, :] += jnp.where(row < 4, far_sum[...], 0.0)
    for head in range(LOCAL):
        to_token = order_from(offsets[head], 1)
        both = own[:, head * 2 * SIZE : (head + 1) * 2 * SIZE].astype(BF16)
        both = dot(to_token, both)
        even, odd = both[:SIZE], both[SIZE:]
        low = lane_iota(even.shape) < SIZE
        key_grad[:, head, :] = jnp.where(low, even, pltpu.roll(odd, SIZE, 1)).astype(BF16)
        value_grad[:, head, :] = jnp.where(low, pltpu.roll(even, SIZE, 1), odd).astype(BF16)
    place = lax.broadcasted_iota(jnp.int32, (2 * SHARE, ROWS), 0)
    device = lax.broadcasted_iota(jnp.int32, (2 * SHARE, ROWS), 1)
    start = (device & 1) * SHARE + (device >> 1 & 7) * PART + (device >> 4) * FINAL
    total = jnp.zeros((2 * SHARE, HALF), F32)
    for term in range(FINAL):
        total = total + dot(one_hot(place == start + term), spread_in[:, term, :])
    rows = SHARE // 2
    for core in range(CORE):
        for half in range(2):
            at = core * SHARE + half * rows
            weight_grad[core * rows : (core + 1) * rows, half * HALF : (half + 1) * HALF] = total[at : at + rows]


def call(kernel, outs, args, scalars, scratch=()):
    smem = pl.BlockSpec(memory_space=pltpu.SMEM)
    vmem = pl.BlockSpec(memory_space=pltpu.VMEM)
    return pl.pallas_call(
        kernel,
        out_shape=[jax.ShapeDtypeStruct(shape, dtype) for shape, dtype in outs],
        in_specs=[smem] * scalars + [vmem] * (len(args) - scalars),
        out_specs=[vmem] * len(outs),
        scratch_shapes=list(scratch),
        compiler_params=pltpu.CompilerParams(vmem_limit_bytes=48 * 2**20),
    )(*args)


def start(offsets, keys, values, grad):
    outs = [((ROWS, LANES), BF16), ((FAR, 8, LANES), BF16), ((NEAR, LANES), BF16), ((4, SIZE, HALF), BF16)]
    return call(start_kernel, outs, (offsets, keys, values, grad), 1)


def line_pieces(rank, ordered, far_in):
    return call(line_kernel, [((LINE, BLOCK, LANES), BF16)], (rank, ordered, far_in), 1)[0]


def attention(rank, offsets, queries, weight, grads, ordered, line_in, partner_in, other_in):
    outs = [
        ((SIZE, 2 * WIDTH), F32),
        ((SIZE, LOCAL, 2 * SIZE), BF16),
        ((SEND, LANES), BF16),
        ((LINE, BLOCK, LANES), F32),
        ((ROWS, LANES), F32),
        ((SHARE, HALF), F32),
    ]
    scratch = [
        pltpu.VMEM((KEYS, LANES), BF16),
        pltpu.VMEM((ROWS, WIDTH), BF16),
        pltpu.VMEM((ROWS, LOCAL * SIZE), BF16),
        pltpu.VMEM((SHARE, WIDTH), F32),
    ]
    args = (rank, offsets, queries, weight, grads, ordered, line_in, partner_in, other_in, jnp.asarray(shared_levels()))
    return call(main_kernel, outs, args, 2, scratch)


def line_return(received, keep_line, keep_weight):
    return call(line_return_kernel, [((LINE, BLOCK + PART, LANES), BF16)], (received, keep_line, keep_weight), 0)[0]


def far_return(rank, line_in):
    outs = [((NEAR, LANES), F32), ((FAR, 8, LANES), BF16)]
    return call(far_return_kernel, outs, (rank, line_in), 1)


def spread_pieces(far_in):
    outs = [((8, LANES), F32), ((ROWS, 4, LANES), BF16)]
    return call(spread_kernel, outs, (far_in,), 0)


def finish(offsets, keep_own, received, near_sum, far_sum, spread_in):
    outs = [((SIZE, LOCAL, 2 * SIZE), BF16)] * 2 + [((SHARE, WIDTH), F32)]
    args = (offsets, keep_own, received, near_sum, far_sum, spread_in)
    return call(finish_kernel, outs, args, 1, [pltpu.VMEM((ROWS, LANES), F32)])


def trade(pieces, groups):
    return lax.all_to_all(pieces, "seq", 0, 0, axis_index_groups=groups, tiled=True)


def swap_cores(block):
    return lax.ppermute(block, "seq", [(i, i ^ 1) for i in range(FAR * LINE * CORE)])


def shards(queries, keys, values, out_weight, offsets, out_grad):
    index = lax.axis_index("seq")
    rank = jnp.stack([index >> 4, index >> 1 & 7, index & 1]).astype(jnp.int32)
    far_groups = [[far * 16 + low for far in range(FAR)] for low in range(16)]
    line_groups = [[far * 16 + line * 2 + core for line in range(LINE)] for far in range(FAR) for core in range(CORE)]
    ordered, far_out, partner_out, grad_out = start(offsets, keys, values, out_grad)
    partner_in = swap_cores(partner_out)
    far_in = trade(far_out, far_groups)
    line_in = trade(line_pieces(rank, ordered, far_in), line_groups)
    other_in = swap_cores(line_in)
    grads = lax.all_to_all(grad_out, "head", 0, 0, tiled=True)
    output_part, query_grad, send, keep_line, keep_own, keep_weight = attention(
        rank, offsets, queries, out_weight, grads, ordered, line_in, partner_in, other_in
    )
    output = lax.psum_scatter(output_part, "head", scatter_dimension=1, tiled=True).astype(BF16)
    received = swap_cores(send)
    line_back = trade(line_return(received, keep_line, keep_weight), line_groups)
    near_sum, far_back = far_return(rank, line_back)
    far_sum, spread_out = spread_pieces(trade(far_back, far_groups))
    spread_in = lax.all_to_all(spread_out, "seq", 0, 0, tiled=True)
    key_grad, value_grad, weight_grad = finish(offsets, keep_own, received, near_sum, far_sum, spread_in)
    return (output, query_grad, key_grad, value_grad, weight_grad)


def solution(mesh):
    return jax.shard_map(
        shards,
        mesh=mesh,
        in_specs=(
            P("seq", "head", None),
            P("seq", "head", None),
            P("seq", "head", None),
            P("head", None),
            P("head"),
            P("seq", "head"),
        ),
        out_specs=(
            P("seq", "head"),
            P("seq", "head", None),
            P("seq", "head", None),
            P("seq", "head", None),
            P("head", None),
        ),
        check_vma=False,
    )
```

```python
import math

import jax
import jax.numpy as jnp
import numpy as np
from jax import lax
from jax.experimental import pallas as pl
from jax.experimental.pallas import tpu as pltpu
from jax.sharding import PartitionSpec as P

FAR, LINE, CORE = 8, 8, 2
ROWS = 128
LOCAL = 3
SIZE = 64
LANES = LOCAL * 2 * SIZE
WIDTH = 768
HALF = WIDTH // 2
SCALE = SIZE**-0.5
NEAR = 32
PICKED = 16
BLOCK = NEAR + PICKED
REACH = LINE * BLOCK
PARTNER_AT = ROWS + REACH
OTHER_AT = PARTNER_AT + NEAR
KEYS = OTHER_AT + REACH
SHARE = 192
SEND = REACH + NEAR + SHARE
PART = SHARE // LINE

NT = (((1,), (1,)), ((), ()))
TN = (((0,), (0,)), ((), ()))
NN = (((1,), (0,)), ((), ()))
BF16 = jnp.bfloat16
F32 = jnp.float32


def dot(a, b, dims=NN):
    return lax.dot_general(a, b, dims, preferred_element_type=F32)


def depth_of(row):
    return 7 if row == 0 else 7 - row.bit_length()


def far_rows():
    rows = [(1, i) for i in range(4)] + [(d, i) for d in (2, 3) for i in range(2)]
    return rows + [(d, 0) for d in range(4, 8)]


def key_table():
    table = [(-1, depth_of(row)) for row in range(ROWS)]
    for core in range(CORE):
        if core:
            table += [(0, depth_of(NEAR + row)) for row in range(NEAR)]
        for line in range(LINE):
            distance = 2 * line + core
            for row in range(NEAR):
                table.append((distance.bit_length() - 1, depth_of(row)) if distance else None)
            table += [(3 + far.bit_length(), depth_of(row)) for far, row in far_rows()]
            table += [None] * (PICKED - 12)
    return table


def shared_levels():
    table = key_table()
    bias = np.full((KEYS, ROWS), -1e30, np.float32)
    for key, entry in enumerate(table):
        if entry is None:
            continue
        for query in range(ROWS):
            count = min(entry[1], depth_of(query)) - entry[0]
            if count > 0:
                bias[key, query] = math.log(count)
    return bias


def reversed_bits(row):
    out = row * 0
    for bit in range(7):
        out = out | ((row >> bit) & 1) << (6 - bit)
    return out


def token_of(row):
    return jnp.where(row < SIZE, 2 * row, 2 * row - (ROWS - 1))


def one_hot(match):
    return jnp.where(match, 1.0, 0.0).astype(BF16)


def order_from(offset, row_axis):
    row = lax.broadcasted_iota(jnp.int32, (ROWS, ROWS), row_axis)
    token = token_of(lax.broadcasted_iota(jnp.int32, (ROWS, ROWS), 1 - row_axis))
    return one_hot(((reversed_bits(row) + offset) & (ROWS - 1)) == token)


def lane_iota(shape):
    return lax.broadcasted_iota(jnp.int32, shape, len(shape) - 1)


def beside(first, second):
    low = lane_iota(first.shape) < SIZE
    even = jnp.where(low, first, pltpu.roll(second, SIZE, 1))
    odd = jnp.where(low, pltpu.roll(first, SIZE, 1), second)
    return jnp.concatenate([even, odd], axis=0).astype(BF16)


def start_kernel(offsets, keys, values, grad, ordered, far_out, partner_out, grad_out):
    for head in range(LOCAL):
        lanes = pl.ds(head * 2 * SIZE, 2 * SIZE)
        both = beside(keys[head].astype(F32), values[head].astype(F32))
        ordered[:, lanes] = dot(order_from(offsets[head], 0), both).astype(BF16)
    for slot in range(FAR):
        far_out[slot] = ordered[0:8, :]
    partner_out[...] = ordered[NEAR : 2 * NEAR, :]
    for slot in range(4):
        grad_out[slot] = grad[...]


def far_place(row, far):
    distance = jnp.where(row < 4, 1, jnp.where(row < 6, 2, jnp.where(row < 8, 3, row - 4)))
    index = jnp.where(row < 4, row, jnp.where(row < 8, row & 1, 0))
    return jnp.where(row < 12, (far ^ distance) * 8 + index, -1)


def line_kernel(rank, ordered, far_in, line_out):
    row = lax.broadcasted_iota(jnp.int32, (PICKED, FAR * 8), 0)
    column = lax.broadcasted_iota(jnp.int32, (PICKED, FAR * 8), 1)
    choose = one_hot(far_place(row, rank[0]) == column)
    picked = dot(choose, far_in[...].reshape(FAR * 8, LANES)).astype(BF16)
    for slot in range(LINE):
        line_out[slot, 0:NEAR, :] = ordered[0:NEAR, :]
        line_out[slot, NEAR:BLOCK, :] = picked


def main_kernel(
    rank, offsets, queries, weight, grads, ordered, line_in, partner_in, other_in, bias,
    output_part, query_grad, send, keep_line, keep_own, keep_weight,
    held, full_grad, attn, weight_term,
):
    line, core = rank[1], rank[2]
    held[0:ROWS, :] = ordered[...]
    held[PARTNER_AT:OTHER_AT, :] = partner_in[...]
    for step in range(LINE):
        slot = line ^ step
        held[ROWS + step * BLOCK : ROWS + (step + 1) * BLOCK, :] = line_in[slot]
        held[OTHER_AT + step * BLOCK : OTHER_AT + (step + 1) * BLOCK, :] = other_in[slot]
    for parity in range(2):
        for half in range(2):
            full_grad[parity * SIZE : (parity + 1) * SIZE, half * HALF : (half + 1) * HALF] = grads[2 * parity + half]
    for head in range(LOCAL):
        lanes = pl.ds(head * 2 * SIZE, 2 * SIZE)
        to_order = order_from(offsets[head], 0)
        to_token = order_from(offsets[head], 1)
        pairs = queries[head].astype(F32)
        query = dot(to_order, beside(pairs, jnp.zeros_like(pairs))).astype(BF16)
        head_weight = weight[head * SIZE : (head + 1) * SIZE, :]
        grad = dot(full_grad[...], head_weight, NT).astype(BF16)
        grad = dot(to_order, jnp.concatenate([jnp.zeros_like(grad), grad], axis=1)).astype(BF16)
        beside_grad = jnp.concatenate([query, grad], axis=0)
        both = held[:, lanes]
        products = dot(both, beside_grad, NT)
        scores = products[:, :ROWS] * SCALE + bias[...]
        top = jnp.max(scores, axis=0, keepdims=True)
        expd = jnp.exp(scores - top)
        probs = expd / jnp.sum(expd, axis=0, keepdims=True)
        rounded = probs.astype(BF16)
        attn_head = dot(both, rounded, TN)[SIZE:, :].astype(BF16)
        grad_side = grad.astype(F32).T
        delta = jnp.sum(grad_side[SIZE:, :] * attn_head.astype(F32), axis=0, keepdims=True)
        dscore = (probs * (products[:, ROWS:] - delta) * SCALE).astype(BF16)
        dquery = dot(both, dscore, TN)[:SIZE, :].astype(BF16)
        attn[:, head * SIZE : (head + 1) * SIZE] = dot(to_token, attn_head, NT).astype(BF16)
        by_token = dot(to_token, jnp.concatenate([dquery, jnp.zeros_like(dquery)], axis=0), NT)
        query_grad[head] = (by_token[:SIZE] + pltpu.roll(by_token[SIZE:], SIZE, 1)).astype(BF16)
        dboth = dot(jnp.concatenate([dscore, rounded], axis=1), beside_grad)
        keep_own[:, lanes] = dboth[0:ROWS]
        send[REACH : REACH + NEAR, lanes] = dboth[PARTNER_AT:OTHER_AT].astype(BF16)
        for step in range(LINE):
            slot = line ^ step
            keep_line[slot, :, lanes] = dboth[ROWS + step * BLOCK : ROWS + (step + 1) * BLOCK]
            at = pl.multiple_of(slot * BLOCK, 16)
            send[pl.ds(at, BLOCK), lanes] = dboth[OTHER_AT + step * BLOCK : OTHER_AT + (step + 1) * BLOCK].astype(BF16)
    part = dot(attn[...], weight[...])
    for parity in range(2):
        for half in range(2):
            piece = part[parity * SIZE : (parity + 1) * SIZE, half * HALF : (half + 1) * HALF]
            output_part[2 * parity + half] = piece.astype(BF16)
    weight_term[...] = dot(attn[...], full_grad[...], TN)
    rows = SHARE // 2
    mine = pl.ds(pl.multiple_of(core * rows, 8), rows)
    theirs = pl.ds(pl.multiple_of((1 - core) * rows, 8), rows)
    for half in range(2):
        columns = pl.ds(half * HALF, HALF)
        keep_weight[half * rows : (half + 1) * rows, :] = weight_term[mine, columns]
        at = REACH + NEAR + half * rows
        send[at : at + rows, :] = weight_term[theirs, columns].astype(BF16)


def line_return_kernel(received, keep_line, keep_weight, line_out):
    for slot in range(LINE):
        rows = slice(slot * BLOCK, (slot + 1) * BLOCK)
        line_out[slot, 0:BLOCK, :] = (keep_line[slot] + received[rows, :].astype(F32)).astype(BF16)
        part = slice(slot * PART, (slot + 1) * PART)
        at = REACH + NEAR + slot * PART
        line_out[slot, BLOCK:, :] = (keep_weight[part, :] + received[at : at + PART, :].astype(F32)).astype(BF16)


def far_return_kernel(rank, line_in, near_sum, far_out):
    total = line_in[0].astype(F32)
    for slot in range(1, LINE):
        total = total + line_in[slot].astype(F32)
    near_sum[...] = total[:NEAR]
    place = lax.broadcasted_iota(jnp.int32, (FAR * 8, PICKED), 0)
    row = lax.broadcasted_iota(jnp.int32, (FAR * 8, PICKED), 1)
    choose = one_hot(far_place(row, rank[0]) == place)
    picked = dot(choose, total[NEAR:BLOCK].astype(BF16))
    for slot in range(FAR):
        far_out[slot, 0:8, :] = picked[slot * 8 : (slot + 1) * 8].astype(BF16)
        far_out[slot, 8:, :] = total[BLOCK:].astype(BF16)


def spread_kernel(far_in, far_sum, spread_out):
    total = far_in[0].astype(F32)
    for slot in range(1, FAR):
        total = total + far_in[slot].astype(F32)
    far_sum[...] = total[:8]
    part = total[8:].astype(BF16)
    for slot in range(LINE * CORE):
        spread_out[slot] = part


def finish_kernel(offsets, keep_own, received, near_sum, far_sum, key_grad, value_grad, own):
    own[...] = keep_own[...]
    own[NEAR : 2 * NEAR, :] += received[REACH : REACH + NEAR, :].astype(F32)
    own[0:NEAR, :] += near_sum[...]
    own[0:8, :] += far_sum[...]
    for head in range(LOCAL):
        to_token = order_from(offsets[head], 1)
        both = own[:, head * 2 * SIZE : (head + 1) * 2 * SIZE].astype(BF16)
        both = dot(to_token, both)
        even, odd = both[:SIZE], both[SIZE:]
        low = lane_iota(even.shape) < SIZE
        key_grad[head] = jnp.where(low, even, pltpu.roll(odd, SIZE, 1)).astype(BF16)
        value_grad[head] = jnp.where(low, pltpu.roll(even, SIZE, 1), odd).astype(BF16)


def weight_kernel(spread_in, weight_grad):
    for line in range(LINE):
        half, row = line // 4, line % 4 * PART
        for core in range(CORE):
            at = core * SHARE // 2 + row
            weight_grad[at : at + PART, half * HALF : (half + 1) * HALF] = spread_in[2 * line + core].astype(F32)


def call(kernel, outs, args, scalars, scratch=()):
    smem = pl.BlockSpec(memory_space=pltpu.SMEM)
    vmem = pl.BlockSpec(memory_space=pltpu.VMEM)
    return pl.pallas_call(
        kernel,
        out_shape=[jax.ShapeDtypeStruct(shape, dtype) for shape, dtype in outs],
        in_specs=[smem] * scalars + [vmem] * (len(args) - scalars),
        out_specs=[vmem] * len(outs),
        scratch_shapes=list(scratch),
        compiler_params=pltpu.CompilerParams(vmem_limit_bytes=48 * 2**20),
    )(*args)


def start(offsets, keys, values, grad):
    outs = [((ROWS, LANES), BF16), ((FAR, 8, LANES), BF16), ((NEAR, LANES), BF16), ((4, SIZE, HALF), BF16)]
    return call(start_kernel, outs, (offsets, keys, values, grad), 1)


def line_pieces(rank, ordered, far_in):
    return call(line_kernel, [((LINE, BLOCK, LANES), BF16)], (rank, ordered, far_in), 1)[0]


def attention(rank, offsets, queries, weight, grads, ordered, line_in, partner_in, other_in):
    outs = [
        ((4, SIZE, HALF), BF16),
        ((LOCAL, SIZE, 2 * SIZE), BF16),
        ((SEND, LANES), BF16),
        ((LINE, BLOCK, LANES), F32),
        ((ROWS, LANES), F32),
        ((SHARE, HALF), F32),
    ]
    scratch = [
        pltpu.VMEM((KEYS, LANES), BF16),
        pltpu.VMEM((ROWS, WIDTH), BF16),
        pltpu.VMEM((ROWS, LOCAL * SIZE), BF16),
        pltpu.VMEM((SHARE, WIDTH), F32),
    ]
    args = (rank, offsets, queries, weight, grads, ordered, line_in, partner_in, other_in, jnp.asarray(shared_levels()))
    return call(main_kernel, outs, args, 2, scratch)


def line_return(received, keep_line, keep_weight):
    return call(line_return_kernel, [((LINE, BLOCK + PART, LANES), BF16)], (received, keep_line, keep_weight), 0)[0]


def far_return(rank, line_in):
    outs = [((NEAR, LANES), F32), ((FAR, 8 + PART, LANES), BF16)]
    return call(far_return_kernel, outs, (rank, line_in), 1)


def spread_pieces(far_in):
    outs = [((8, LANES), F32), ((LINE * CORE, PART, LANES), BF16)]
    return call(spread_kernel, outs, (far_in,), 0)


def finish(offsets, keep_own, received, near_sum, far_sum):
    outs = [((LOCAL, SIZE, 2 * SIZE), BF16)] * 2
    args = (offsets, keep_own, received, near_sum, far_sum)
    return call(finish_kernel, outs, args, 1, [pltpu.VMEM((ROWS, LANES), F32)])


def weight_rows(spread_in):
    return call(weight_kernel, [((SHARE, WIDTH), F32)], (spread_in,), 0)[0]


def trade(pieces, groups):
    return lax.all_to_all(pieces, "seq", 0, 0, axis_index_groups=groups, tiled=True)


def swap_cores(block):
    return lax.ppermute(block, "seq", [(i, i ^ 1) for i in range(FAR * LINE * CORE)])


def shards(queries, keys, values, out_weight, offsets, out_grad):
    index = lax.axis_index("seq")
    rank = jnp.stack([index >> 4, index >> 1 & 7, index & 1]).astype(jnp.int32)
    far_groups = [[far * 16 + low for far in range(FAR)] for low in range(16)]
    line_groups = [[far * 16 + line * 2 + core for line in range(LINE)] for far in range(FAR) for core in range(CORE)]
    near_groups = [[far * 16 + low for low in range(16)] for far in range(FAR)]
    queries, keys, values = (array.transpose(1, 0, 2) for array in (queries, keys, values))
    ordered, far_out, partner_out, grad_out = start(offsets, keys, values, out_grad)
    partner_in = swap_cores(partner_out)
    far_in = trade(far_out, far_groups)
    line_in = trade(line_pieces(rank, ordered, far_in), line_groups)
    other_in = swap_cores(line_in)
    grads = lax.all_to_all(grad_out, "head", 0, 0, tiled=True)
    output_part, query_grad, send, keep_line, keep_own, keep_weight = attention(
        rank, offsets, queries, out_weight, grads, ordered, line_in, partner_in, other_in
    )
    received = swap_cores(send)
    output_terms = lax.all_to_all(output_part, "head", 0, 0, tiled=True)
    output = jnp.sum(output_terms.astype(F32), axis=0).astype(BF16)
    line_back = trade(line_return(received, keep_line, keep_weight), line_groups)
    near_sum, far_back = far_return(rank, line_back)
    far_sum, spread_out = spread_pieces(trade(far_back, far_groups))
    weight_grad = weight_rows(trade(spread_out, near_groups))
    key_grad, value_grad = finish(offsets, keep_own, received, near_sum, far_sum)
    query_grad, key_grad, value_grad = (grad.transpose(1, 0, 2) for grad in (query_grad, key_grad, value_grad))
    return (output, query_grad, key_grad, value_grad, weight_grad)


def solution(mesh):
    return jax.shard_map(
        shards,
        mesh=mesh,
        in_specs=(
            P("seq", "head", None),
            P("seq", "head", None),
            P("seq", "head", None),
            P("head", None),
            P("head"),
            P("seq", "head"),
        ),
        out_specs=(
            P("seq", "head"),
            P("seq", "head", None),
            P("seq", "head", None),
            P("seq", "head", None),
            P("head", None),
        ),
        check_vma=False,
    )
```

```python
import math

import jax
import jax.numpy as jnp
import numpy as np
from jax import lax
from jax.experimental import pallas as pl
from jax.experimental.pallas import tpu as pltpu
from jax.sharding import PartitionSpec as P

FAR, LINE, CORE = 8, 8, 2
ROWS = 128
LOCAL = 3
SIZE = 64
LANES = LOCAL * 2 * SIZE
WIDTH = 768
HALF = WIDTH // 2
SCALE = SIZE**-0.5
NEAR = 32
EACH = 4
PICKED = 96
SLOTS = LINE * NEAR
LINE_AT = ROWS
FAR_AT = LINE_AT + SLOTS - NEAR
PARTNER_AT = FAR_AT + PICKED
OTHER_AT = PARTNER_AT + NEAR
OTHER_FAR_AT = OTHER_AT + SLOTS
KEYS = OTHER_FAR_AT + PICKED
SHARE = 192
PART = SHARE // FAR
SEND_FAR = SLOTS + NEAR
SEND_WEIGHT = SEND_FAR + PICKED
SEND = SEND_WEIGHT + SHARE

NT = (((1,), (1,)), ((), ()))
TN = (((0,), (0,)), ((), ()))
NN = (((1,), (0,)), ((), ()))
BF16 = jnp.bfloat16
F32 = jnp.float32


def dot(a, b, dims=NN):
    return lax.dot_general(a, b, dims, preferred_element_type=F32)


def depth_of(row):
    return 7 if row == 0 else 7 - row.bit_length()


def far_table():
    table = [(1, row) for line in range(LINE) for row in range(4)]
    table += [(far, row) for far in (2, 3) for line in range(LINE) for row in range(2)]
    return table + [(far, 0) for far in range(4, 8) for line in range(LINE)]


def key_table():
    table = [(-1, depth_of(row)) for row in range(ROWS)]
    for core in range(CORE):
        if core:
            table += [(0, depth_of(NEAR + row)) for row in range(NEAR)]
        for line in range(1 - core, LINE):
            table += [(line.bit_length(), depth_of(row)) for row in range(NEAR)]
        table += [(3 + far.bit_length(), depth_of(row)) for far, row in far_table()]
    return table


def shared_levels():
    table = key_table()
    bias = np.full((KEYS, ROWS), -1e30, np.float32)
    for key, entry in enumerate(table):
        for query in range(ROWS):
            count = min(entry[1], depth_of(query)) - entry[0]
            if count > 0:
                bias[key, query] = math.log(count)
    return bias


def reversed_bits(row):
    out = row * 0
    for bit in range(7):
        out = out | ((row >> bit) & 1) << (6 - bit)
    return out


def token_of(row):
    return jnp.where(row < SIZE, 2 * row, 2 * row - (ROWS - 1))


def one_hot(match):
    return jnp.where(match, 1.0, 0.0).astype(BF16)


def order_from(offset, row_axis):
    row = lax.broadcasted_iota(jnp.int32, (ROWS, ROWS), row_axis)
    token = token_of(lax.broadcasted_iota(jnp.int32, (ROWS, ROWS), 1 - row_axis))
    return one_hot(((reversed_bits(row) + offset) & (ROWS - 1)) == token)


def lane_iota(shape):
    return lax.broadcasted_iota(jnp.int32, shape, len(shape) - 1)


def beside(first, second):
    low = lane_iota(first.shape) < SIZE
    even = jnp.where(low, first, pltpu.roll(second, SIZE, 1))
    odd = jnp.where(low, pltpu.roll(first, SIZE, 1), second)
    return jnp.concatenate([even, odd], axis=0).astype(BF16)


def start_kernel(offsets, keys, values, grad, ordered, line_out, partner_out, grad_out, keys_here, values_here, grad_here, done):
    copies = [
        pltpu.make_async_copy(source, target, done.at[at])
        for at, (source, target) in enumerate(((keys, keys_here), (values, values_here), (grad, grad_here)))
    ]
    for copy in copies:
        copy.start()
    orders = [order_from(offsets[head], 0) for head in range(LOCAL)]
    for copy in copies:
        copy.wait()
    for head in range(LOCAL):
        lanes = pl.ds(head * 2 * SIZE, 2 * SIZE)
        both = beside(keys_here[head].astype(F32), values_here[head].astype(F32))
        ordered[:, lanes] = dot(orders[head], both).astype(BF16)
    for slot in range(LINE):
        line_out[slot] = ordered[0:NEAR, :]
    partner_out[...] = ordered[NEAR : 2 * NEAR, :]
    for slot in range(4):
        grad_out[slot] = grad_here[...]


def far_place(row, far):
    second, third = row - 32, row - 64
    distance = jnp.where(row < 32, 1, jnp.where(row < 64, 2 + (second >> 4), 4 + (third >> 3)))
    line = jnp.where(row < 32, row >> 2, jnp.where(row < 64, (second >> 1) & 7, third & 7))
    index = jnp.where(row < 32, row & 3, jnp.where(row < 64, second & 1, 0))
    return ((far ^ distance) * LINE + line) * EACH + index


def far_choice(far, row_axis):
    shape = (PICKED, FAR * NEAR) if row_axis == 0 else (FAR * NEAR, PICKED)
    row = lax.broadcasted_iota(jnp.int32, shape, row_axis)
    return one_hot(far_place(row, far) == lax.broadcasted_iota(jnp.int32, shape, 1 - row_axis))


def far_kernel(line_in, far_out):
    low = lax.broadcasted_iota(jnp.int32, (8, LANES), 0) < EACH
    for pair in range(LINE // 2):
        first, second = (line_in[2 * pair + slot, 0:16, :].astype(F32)[:8] for slot in range(2))
        rows = jnp.where(low, first, pltpu.roll(second, EACH, 0)).astype(BF16)
        for slot in range(FAR):
            far_out[slot, pair * 8 : (pair + 1) * 8, :] = rows


def main_kernel(
    rank, offsets, queries, weight, grads, ordered, line_in, far_in, partner_in, other_in, other_far_in, bias,
    output_part, query_grad, send, keep_line, keep_far, keep_own, keep_weight,
    held, full_grad, attn, weight_term,
):
    far, line, core = rank[0], rank[1], rank[2]
    held[0:ROWS, :] = ordered[...]
    held[PARTNER_AT:OTHER_AT, :] = partner_in[...]
    choice = far_choice(far, 0)
    held[FAR_AT:PARTNER_AT, :] = dot(choice, far_in[...].reshape(FAR * NEAR, LANES)).astype(BF16)
    held[OTHER_FAR_AT:, :] = dot(choice, other_far_in[...].reshape(FAR * NEAR, LANES)).astype(BF16)
    for step in range(LINE):
        slot = line ^ step
        if step:
            at = LINE_AT + (step - 1) * NEAR
            held[at : at + NEAR, :] = line_in[slot]
        at = OTHER_AT + step * NEAR
        held[at : at + NEAR, :] = other_in[slot]
    for parity in range(2):
        for half in range(2):
            full_grad[parity * SIZE : (parity + 1) * SIZE, half * HALF : (half + 1) * HALF] = grads[2 * parity + half]
    for head in range(LOCAL):
        lanes = pl.ds(head * 2 * SIZE, 2 * SIZE)
        to_order = order_from(offsets[head], 0)
        to_token = order_from(offsets[head], 1)
        pairs = queries[head].astype(F32)
        query = dot(to_order, beside(pairs, jnp.zeros_like(pairs))).astype(BF16)
        head_weight = weight[head * SIZE : (head + 1) * SIZE, :]
        grad = dot(full_grad[...], head_weight, NT).astype(BF16)
        grad = dot(to_order, jnp.concatenate([jnp.zeros_like(grad), grad], axis=1)).astype(BF16)
        beside_grad = jnp.concatenate([query, grad], axis=0)
        both = held[:, lanes]
        products = dot(both, beside_grad, NT)
        scores = products[:, :ROWS] * SCALE + bias[...]
        top = jnp.max(scores, axis=0, keepdims=True)
        expd = jnp.exp(scores - top)
        probs = expd / jnp.sum(expd, axis=0, keepdims=True)
        rounded = probs.astype(BF16)
        attn_head = dot(both, rounded, TN)[SIZE:, :].astype(BF16)
        grad_side = grad.astype(F32).T
        delta = jnp.sum(grad_side[SIZE:, :] * attn_head.astype(F32), axis=0, keepdims=True)
        dscore = (probs * (products[:, ROWS:] - delta) * SCALE).astype(BF16)
        dquery = dot(both, dscore, TN)[:SIZE, :].astype(BF16)
        attn[:, head * SIZE : (head + 1) * SIZE] = dot(to_token, attn_head, NT).astype(BF16)
        by_token = dot(to_token, jnp.concatenate([dquery, jnp.zeros_like(dquery)], axis=0), NT)
        query_grad[head] = (by_token[:SIZE] + pltpu.roll(by_token[SIZE:], SIZE, 1)).astype(BF16)
        dboth = dot(jnp.concatenate([dscore, rounded], axis=1), beside_grad)
        keep_own[:, lanes] = dboth[0:ROWS]
        keep_far[:, lanes] = dboth[FAR_AT:PARTNER_AT]
        send[SLOTS:SEND_FAR, lanes] = dboth[PARTNER_AT:OTHER_AT].astype(BF16)
        send[SEND_FAR:SEND_WEIGHT, lanes] = dboth[OTHER_FAR_AT:].astype(BF16)
        for step in range(LINE):
            slot = line ^ step
            at = LINE_AT + (step - 1) * NEAR
            keep_line[slot, :, lanes] = dboth[at : at + NEAR] if step else jnp.zeros((NEAR, 2 * SIZE), F32)
            at = OTHER_AT + step * NEAR
            rows = pl.ds(pl.multiple_of(slot * NEAR, NEAR), NEAR)
            send[rows, lanes] = dboth[at : at + NEAR].astype(BF16)
    part = dot(attn[...], weight[...])
    for parity in range(2):
        for half in range(2):
            piece = part[parity * SIZE : (parity + 1) * SIZE, half * HALF : (half + 1) * HALF]
            output_part[2 * parity + half] = piece.astype(BF16)
    weight_term[...] = dot(attn[...], full_grad[...], TN)
    rows = SHARE // 2
    mine = pl.ds(pl.multiple_of(core * rows, 8), rows)
    theirs = pl.ds(pl.multiple_of((1 - core) * rows, 8), rows)
    for half in range(2):
        columns = pl.ds(half * HALF, HALF)
        keep_weight[half * rows : (half + 1) * rows, :] = weight_term[mine, columns]
        at = SEND_WEIGHT + half * rows
        send[at : at + rows, :] = weight_term[theirs, columns].astype(BF16)


def far_return_kernel(rank, received, keep_far, keep_weight, far_out):
    picked = (keep_far[...] + received[SEND_FAR:SEND_WEIGHT, :].astype(F32)).astype(BF16)
    rows = dot(far_choice(rank[0], 1), picked).astype(BF16)
    weight = (keep_weight[...] + received[SEND_WEIGHT:, :].astype(F32)).astype(BF16)
    for slot in range(FAR):
        far_out[slot, 0:NEAR, :] = rows[slot * NEAR : (slot + 1) * NEAR]
        far_out[slot, NEAR:, :] = weight[slot * PART : (slot + 1) * PART]


def line_return_kernel(received, keep_line, far_in, line_out):
    total = far_in[0].astype(F32)
    for slot in range(1, FAR):
        total = total + far_in[slot].astype(F32)
    low = lax.broadcasted_iota(jnp.int32, (8, LANES), 0) < EACH
    for slot in range(LINE):
        rows = keep_line[slot] + received[slot * NEAR : (slot + 1) * NEAR, :].astype(F32)
        both = total[slot // 2 * 8 : slot // 2 * 8 + 8]
        first = jnp.where(low, pltpu.roll(both, EACH, 0) if slot % 2 else both, 0.0)
        line_out[slot, 0:NEAR, :] = jnp.concatenate([rows[:8] + first, rows[8:]], axis=0).astype(BF16)
        line_out[slot, NEAR:, :] = total[NEAR:].astype(BF16)


def spread_kernel(line_in, near_sum, spread_out):
    total = line_in[0].astype(F32)
    for slot in range(1, LINE):
        total = total + line_in[slot].astype(F32)
    near_sum[...] = total[:NEAR]
    part = total[NEAR:].astype(BF16)
    for slot in range(FAR * CORE):
        spread_out[slot] = part


def finish_kernel(offsets, keep_own, received, near_sum, key_grad, value_grad, own):
    own[...] = keep_own[...]
    own[NEAR : 2 * NEAR, :] += received[SLOTS:SEND_FAR, :].astype(F32)
    own[0:NEAR, :] += near_sum[...]
    for head in range(LOCAL):
        to_token = order_from(offsets[head], 1)
        both = own[:, head * 2 * SIZE : (head + 1) * 2 * SIZE].astype(BF16)
        both = dot(to_token, both)
        even, odd = both[:SIZE], both[SIZE:]
        low = lane_iota(even.shape) < SIZE
        key_grad[head] = jnp.where(low, even, pltpu.roll(odd, SIZE, 1)).astype(BF16)
        value_grad[head] = jnp.where(low, pltpu.roll(even, SIZE, 1), odd).astype(BF16)


def weight_kernel(spread_in, weight_grad):
    for far in range(FAR):
        half, row = far // 4, far % 4 * PART
        for core in range(CORE):
            at = core * SHARE // 2 + row
            weight_grad[at : at + PART, half * HALF : (half + 1) * HALF] = spread_in[CORE * far + core].astype(F32)


def call(kernel, outs, args, scalars, scratch=(), space=pltpu.VMEM):
    return pl.pallas_call(
        kernel,
        out_shape=[jax.ShapeDtypeStruct(shape, dtype) for shape, dtype in outs],
        in_specs=[pl.BlockSpec(memory_space=pltpu.SMEM)] * scalars
        + [pl.BlockSpec(memory_space=space)] * (len(args) - scalars),
        out_specs=[pl.BlockSpec(memory_space=pltpu.VMEM)] * len(outs),
        scratch_shapes=list(scratch),
        compiler_params=pltpu.CompilerParams(vmem_limit_bytes=48 * 2**20),
    )(*args)


def start(offsets, keys, values, grad):
    outs = [((ROWS, LANES), BF16), ((LINE, NEAR, LANES), BF16), ((NEAR, LANES), BF16), ((4, SIZE, HALF), BF16)]
    scratch = [pltpu.VMEM((LOCAL, SIZE, 2 * SIZE), BF16)] * 2 + [pltpu.VMEM((SIZE, HALF), BF16), pltpu.SemaphoreType.DMA((3,))]
    return call(start_kernel, outs, (offsets, keys, values, grad), 1, scratch, pltpu.HBM)


def far_pieces(line_in):
    return call(far_kernel, [((FAR, NEAR, LANES), BF16)], (line_in,), 0)[0]


def attention(rank, offsets, *arrays):
    outs = [
        ((4, SIZE, HALF), BF16),
        ((LOCAL, SIZE, 2 * SIZE), BF16),
        ((SEND, LANES), BF16),
        ((LINE, NEAR, LANES), F32),
        ((PICKED, LANES), F32),
        ((ROWS, LANES), F32),
        ((SHARE, HALF), F32),
    ]
    scratch = [
        pltpu.VMEM((KEYS, LANES), BF16),
        pltpu.VMEM((ROWS, WIDTH), BF16),
        pltpu.VMEM((ROWS, LOCAL * SIZE), BF16),
        pltpu.VMEM((SHARE, WIDTH), F32),
    ]
    return call(main_kernel, outs, (rank, offsets) + arrays + (jnp.asarray(shared_levels()),), 2, scratch)


def far_return(rank, received, keep_far, keep_weight):
    args = (rank, received, keep_far, keep_weight)
    return call(far_return_kernel, [((FAR, NEAR + PART, LANES), BF16)], args, 1)[0]


def line_return(received, keep_line, far_in):
    return call(line_return_kernel, [((LINE, NEAR + PART, LANES), BF16)], (received, keep_line, far_in), 0)[0]


def spread_pieces(line_in):
    outs = [((NEAR, LANES), F32), ((FAR * CORE, PART, LANES), BF16)]
    return call(spread_kernel, outs, (line_in,), 0)


def finish(offsets, keep_own, received, near_sum):
    outs = [((LOCAL, SIZE, 2 * SIZE), BF16)] * 2
    return call(finish_kernel, outs, (offsets, keep_own, received, near_sum), 1, [pltpu.VMEM((ROWS, LANES), F32)])


def weight_rows(spread_in):
    return call(weight_kernel, [((SHARE, WIDTH), F32)], (spread_in,), 0)[0]


def trade(pieces, groups):
    return lax.all_to_all(pieces, "seq", 0, 0, axis_index_groups=groups, tiled=True)


def swap_cores(block):
    return lax.ppermute(block, "seq", [(i, i ^ 1) for i in range(FAR * LINE * CORE)])


def shards(queries, keys, values, out_weight, offsets, out_grad):
    index = lax.axis_index("seq")
    rank = jnp.stack([index >> 4, index >> 1 & 7, index & 1]).astype(jnp.int32)
    far_groups = [[far * 16 + low for far in range(FAR)] for low in range(16)]
    line_groups = [[far * 16 + line * 2 + core for line in range(LINE)] for far in range(FAR) for core in range(CORE)]
    side_groups = [[far * 16 + line * 2 + core for far in range(FAR) for core in range(CORE)] for line in range(LINE)]
    queries, keys, values = (array.transpose(1, 0, 2) for array in (queries, keys, values))
    ordered, line_out, partner_out, grad_out = start(offsets, keys, values, out_grad)
    partner_in = swap_cores(partner_out)
    line_in = trade(line_out, line_groups)
    other_in = swap_cores(line_in)
    far_in = trade(far_pieces(line_in), far_groups)
    other_far_in = swap_cores(far_in)
    grads = lax.all_to_all(grad_out, "head", 0, 0, tiled=True)
    output_part, query_grad, send, keep_line, keep_far, keep_own, keep_weight = attention(
        rank, offsets, queries, out_weight, grads, ordered, line_in, far_in, partner_in, other_in, other_far_in
    )
    received = swap_cores(send)
    output_terms = lax.all_to_all(output_part, "head", 0, 0, tiled=True)
    far_out = far_return(rank, received, keep_far, keep_weight)
    far_out, output_terms = lax.optimization_barrier((far_out, output_terms))
    output = jnp.sum(output_terms.astype(F32), axis=0).astype(BF16)
    line_back = trade(line_return(received, keep_line, trade(far_out, far_groups)), line_groups)
    near_sum, spread_out = spread_pieces(line_back)
    weight_grad = weight_rows(trade(spread_out, side_groups))
    key_grad, value_grad = finish(offsets, keep_own, received, near_sum)
    query_grad, key_grad, value_grad = (grad.transpose(1, 0, 2) for grad in (query_grad, key_grad, value_grad))
    return (output, query_grad, key_grad, value_grad, weight_grad)


def solution(mesh):
    return jax.shard_map(
        shards,
        mesh=mesh,
        in_specs=(
            P("seq", "head", None),
            P("seq", "head", None),
            P("seq", "head", None),
            P("head", None),
            P("head"),
            P("seq", "head"),
        ),
        out_specs=(
            P("seq", "head"),
            P("seq", "head", None),
            P("seq", "head", None),
            P("seq", "head", None),
            P("head", None),
        ),
        check_vma=False,
    )
```

```python
import math

import jax
import jax.numpy as jnp
import numpy as np
from jax import lax
from jax.experimental import pallas as pl
from jax.experimental.pallas import tpu as pltpu
from jax.sharding import PartitionSpec as P

FAR, LINE, CORE = 8, 8, 2
ROWS = 128
LOCAL = 3
SIZE = 64
LANES = LOCAL * 2 * SIZE
WIDTH = 768
HALF = WIDTH // 2
SCALE = SIZE**-0.5
NEAR = 32
EACH = 4
PICKED = 96
SLOTS = LINE * NEAR
LINE_AT = ROWS
FAR_AT = LINE_AT + SLOTS - NEAR
PARTNER_AT = FAR_AT + PICKED
OTHER_AT = PARTNER_AT + NEAR
OTHER_FAR_AT = OTHER_AT + SLOTS
KEYS = OTHER_FAR_AT + PICKED
SHARE = 192
PART = SHARE // FAR
SEND_FAR = SLOTS + NEAR
SEND_WEIGHT = SEND_FAR + PICKED
SEND = SEND_WEIGHT + SHARE

NT = (((1,), (1,)), ((), ()))
TN = (((0,), (0,)), ((), ()))
NN = (((1,), (0,)), ((), ()))
BF16 = jnp.bfloat16
F32 = jnp.float32


def dot(a, b, dims=NN):
    return lax.dot_general(a, b, dims, preferred_element_type=F32)


def depth_of(row):
    return 7 if row == 0 else 7 - row.bit_length()


def far_table():
    table = [(1, row) for line in range(LINE) for row in range(4)]
    table += [(far, row) for far in (2, 3) for line in range(LINE) for row in range(2)]
    return table + [(far, 0) for far in range(4, 8) for line in range(LINE)]


def key_table():
    table = [(-1, depth_of(row)) for row in range(ROWS)]
    for core in range(CORE):
        if core:
            table += [(0, depth_of(NEAR + row)) for row in range(NEAR)]
        for line in range(1 - core, LINE):
            table += [(line.bit_length(), depth_of(row)) for row in range(NEAR)]
        table += [(3 + far.bit_length(), depth_of(row)) for far, row in far_table()]
    return table


def shared_levels():
    table = key_table()
    bias = np.full((KEYS, ROWS), -1e30, np.float32)
    for key, entry in enumerate(table):
        for query in range(ROWS):
            count = min(entry[1], depth_of(query)) - entry[0]
            if count > 0:
                bias[key, query] = math.log(count)
    return bias


def reversed_bits(row):
    out = row * 0
    for bit in range(7):
        out = out | ((row >> bit) & 1) << (6 - bit)
    return out


def token_of(row):
    return jnp.where(row < SIZE, 2 * row, 2 * row - (ROWS - 1))


def one_hot(match):
    return jnp.where(match, 1.0, 0.0).astype(BF16)


def order_from(offset, row_axis):
    row = lax.broadcasted_iota(jnp.int32, (ROWS, ROWS), row_axis)
    token = token_of(lax.broadcasted_iota(jnp.int32, (ROWS, ROWS), 1 - row_axis))
    return one_hot(((reversed_bits(row) + offset) & (ROWS - 1)) == token)


def lane_iota(shape):
    return lax.broadcasted_iota(jnp.int32, shape, len(shape) - 1)


def beside(first, second):
    low = lane_iota(first.shape) < SIZE
    even = jnp.where(low, first, pltpu.roll(second, SIZE, 1))
    odd = jnp.where(low, pltpu.roll(first, SIZE, 1), second)
    return jnp.concatenate([even, odd], axis=0).astype(BF16)


def start_kernel(offsets, keys, values, grad, ordered, line_out, grad_out, keys_here, values_here, grad_here, done):
    copies = [
        pltpu.make_async_copy(source, target, done.at[at])
        for at, (source, target) in enumerate(((keys, keys_here), (values, values_here), (grad, grad_here)))
    ]
    for copy in copies:
        copy.start()
    orders = [order_from(offsets[head], 0) for head in range(LOCAL)]
    for copy in copies:
        copy.wait()
    for head in range(LOCAL):
        lanes = pl.ds(head * 2 * SIZE, 2 * SIZE)
        both = beside(keys_here[head].astype(F32), values_here[head].astype(F32))
        ordered[:, lanes] = dot(orders[head], both).astype(BF16)
    for slot in range(LINE):
        line_out[slot] = ordered[0:NEAR, :]
    for slot in range(4):
        grad_out[slot] = grad_here[...]


def far_place(row, far):
    second, third = row - 32, row - 64
    distance = jnp.where(row < 32, 1, jnp.where(row < 64, 2 + (second >> 4), 4 + (third >> 3)))
    line = jnp.where(row < 32, row >> 2, jnp.where(row < 64, (second >> 1) & 7, third & 7))
    index = jnp.where(row < 32, row & 3, jnp.where(row < 64, second & 1, 0))
    return ((far ^ distance) * LINE + line) * EACH + index


def far_choice(far, row_axis):
    shape = (PICKED, FAR * NEAR) if row_axis == 0 else (FAR * NEAR, PICKED)
    row = lax.broadcasted_iota(jnp.int32, shape, row_axis)
    return one_hot(far_place(row, far) == lax.broadcasted_iota(jnp.int32, shape, 1 - row_axis))


def far_kernel(ordered, line_in, far_out, partner_out):
    for slot in range(LINE):
        partner_out[slot * NEAR : (slot + 1) * NEAR, :] = line_in[slot]
    partner_out[SLOTS:, :] = ordered[NEAR : 2 * NEAR, :]
    low = lax.broadcasted_iota(jnp.int32, (8, LANES), 0) < EACH
    for pair in range(LINE // 2):
        first, second = (line_in[2 * pair + slot, 0:16, :].astype(F32)[:8] for slot in range(2))
        rows = jnp.where(low, first, pltpu.roll(second, EACH, 0)).astype(BF16)
        for slot in range(FAR):
            far_out[slot, pair * 8 : (pair + 1) * 8, :] = rows


def main_kernel(
    rank, offsets, queries, weight, grads, ordered, line_in, far_in, other_in, other_far_in, bias,
    output_keep, output_send, query_grad, send, keep_line, keep_far, keep_own, keep_weight,
    held, full_grad, attn, weight_term, parts,
):
    far, line, core = rank[0], rank[1], rank[2]
    held[0:ROWS, :] = ordered[...]
    held[PARTNER_AT:OTHER_AT, :] = other_in[SLOTS:, :]
    choice = far_choice(far, 0)
    held[FAR_AT:PARTNER_AT, :] = dot(choice, far_in[...].reshape(FAR * NEAR, LANES)).astype(BF16)
    held[OTHER_FAR_AT:, :] = dot(choice, other_far_in[...].reshape(FAR * NEAR, LANES)).astype(BF16)
    for step in range(LINE):
        slot = line ^ step
        if step:
            at = LINE_AT + (step - 1) * NEAR
            held[at : at + NEAR, :] = line_in[slot]
        at = OTHER_AT + step * NEAR
        held[at : at + NEAR, :] = other_in[pl.ds(pl.multiple_of(slot * NEAR, NEAR), NEAR), :]
    for parity in range(2):
        for half in range(2):
            full_grad[parity * SIZE : (parity + 1) * SIZE, half * HALF : (half + 1) * HALF] = grads[2 * parity + half]
    heads = range(LOCAL)
    lanes = [pl.ds(head * 2 * SIZE, 2 * SIZE) for head in heads]
    to_order = [order_from(offsets[head], 0) for head in heads]
    to_token = [order_from(offsets[head], 1) for head in heads]
    grad = dot(full_grad[...], weight[...], NT).astype(BF16)
    pairs = [queries[head].astype(F32) for head in heads]
    query = [dot(to_order[head], beside(pairs[head], jnp.zeros_like(pairs[head]))).astype(BF16) for head in heads]
    zeros = jnp.zeros((ROWS, SIZE), BF16)
    grad = [jnp.concatenate([zeros, grad[:, head * SIZE : (head + 1) * SIZE]], axis=1) for head in heads]
    grad = [dot(to_order[head], grad[head]).astype(BF16) for head in heads]
    blocks = [jnp.concatenate([query[head], grad[head]], axis=0) for head in heads]
    products = [dot(held[:, lanes[head]], blocks[head], NT) for head in heads]
    scores = [products[head][:, :ROWS] * SCALE + bias[...] for head in heads]
    top = [jnp.max(scores[head], axis=0, keepdims=True) for head in heads]
    expd = [jnp.exp(scores[head] - top[head]) for head in heads]
    share = [1.0 / jnp.sum(expd[head], axis=0, keepdims=True) for head in heads]
    probs = [expd[head] * share[head] for head in heads]
    rounded = [probs[head].astype(BF16) for head in heads]
    attn_head = [dot(held[:, lanes[head]], rounded[head], TN)[SIZE:, :].astype(BF16) for head in heads]
    grad_side = [grad[head].astype(F32).T[SIZE:, :] for head in heads]
    delta = [jnp.sum(grad_side[head] * attn_head[head].astype(F32), axis=0, keepdims=True) for head in heads]
    dscore = [(probs[head] * (products[head][:, ROWS:] - delta[head]) * SCALE).astype(BF16) for head in heads]
    dquery = [dot(held[:, lanes[head]], dscore[head], TN)[:SIZE, :].astype(BF16) for head in heads]
    dboth = [dot(jnp.concatenate([dscore[head], rounded[head]], axis=1), blocks[head]) for head in heads]
    for head in heads:
        attn[:, head * SIZE : (head + 1) * SIZE] = dot(to_token[head], attn_head[head], NT).astype(BF16)
        by_token = dot(to_token[head], jnp.concatenate([dquery[head], jnp.zeros_like(dquery[head])], axis=0), NT)
        query_grad[head] = (by_token[:SIZE] + pltpu.roll(by_token[SIZE:], SIZE, 1)).astype(BF16)
        keep_own[:, lanes[head]] = dboth[head][0:ROWS]
        keep_far[:, lanes[head]] = dboth[head][FAR_AT:PARTNER_AT]
        send[SLOTS:SEND_FAR, lanes[head]] = dboth[head][PARTNER_AT:OTHER_AT].astype(BF16)
        send[SEND_FAR:SEND_WEIGHT, lanes[head]] = dboth[head][OTHER_FAR_AT:].astype(BF16)
        for step in range(LINE):
            slot = line ^ step
            at = LINE_AT + (step - 1) * NEAR
            keep_line[slot, :, lanes[head]] = dboth[head][at : at + NEAR] if step else jnp.zeros((NEAR, 2 * SIZE), F32)
            at = OTHER_AT + step * NEAR
            rows = pl.ds(pl.multiple_of(slot * NEAR, NEAR), NEAR)
            send[rows, lanes[head]] = dboth[head][at : at + NEAR].astype(BF16)
    part = dot(attn[...], weight[...])
    for parity in range(2):
        for half in range(2):
            piece = part[parity * SIZE : (parity + 1) * SIZE, half * HALF : (half + 1) * HALF]
            parts[2 * parity + half] = piece
    mine = rank[3]
    for step, way in ((0, 0), (1, 3)):
        output_keep[step] = parts[mine ^ way]
        output_send[step] = parts[mine ^ way ^ 1].astype(BF16)
    weight_term[...] = dot(attn[...], full_grad[...], TN)
    rows = SHARE // 2
    mine = pl.ds(pl.multiple_of(core * rows, 8), rows)
    theirs = pl.ds(pl.multiple_of((1 - core) * rows, 8), rows)
    for half in range(2):
        columns = pl.ds(half * HALF, HALF)
        keep_weight[half * rows : (half + 1) * rows, :] = weight_term[mine, columns]
        at = SEND_WEIGHT + half * rows
        send[at : at + rows, :] = weight_term[theirs, columns].astype(BF16)


def far_return_kernel(rank, received, keep_far, keep_weight, far_out):
    picked = (keep_far[...] + received[SEND_FAR:SEND_WEIGHT, :].astype(F32)).astype(BF16)
    rows = dot(far_choice(rank[0], 1), picked).astype(BF16)
    weight = (keep_weight[...] + received[SEND_WEIGHT:, :].astype(F32)).astype(BF16)
    for slot in range(FAR):
        far_out[slot, 0:NEAR, :] = rows[slot * NEAR : (slot + 1) * NEAR]
        far_out[slot, NEAR:, :] = weight[slot * PART : (slot + 1) * PART]


def line_return_kernel(received, keep_line, far_in, line_out):
    total = far_in[0].astype(F32)
    for slot in range(1, FAR):
        total = total + far_in[slot].astype(F32)
    low = lax.broadcasted_iota(jnp.int32, (8, LANES), 0) < EACH
    for slot in range(LINE):
        rows = keep_line[slot] + received[slot * NEAR : (slot + 1) * NEAR, :].astype(F32)
        both = total[slot // 2 * 8 : slot // 2 * 8 + 8]
        first = jnp.where(low, pltpu.roll(both, EACH, 0) if slot % 2 else both, 0.0)
        line_out[slot, 0:NEAR, :] = jnp.concatenate([rows[:8] + first, rows[8:]], axis=0).astype(BF16)
        line_out[slot, NEAR:, :] = total[NEAR:].astype(BF16)


def spread_kernel(line_in, near_sum, spread_out):
    total = line_in[0].astype(F32)
    for slot in range(1, LINE):
        total = total + line_in[slot].astype(F32)
    near_sum[...] = total[:NEAR]
    part = total[NEAR:].astype(BF16)
    for slot in range(FAR * CORE):
        spread_out[slot] = part


def finish_kernel(offsets, keep_own, received, near_sum, key_grad, value_grad, own):
    own[...] = keep_own[...]
    own[NEAR : 2 * NEAR, :] += received[SLOTS:SEND_FAR, :].astype(F32)
    own[0:NEAR, :] += near_sum[...]
    for head in range(LOCAL):
        to_token = order_from(offsets[head], 1)
        both = own[:, head * 2 * SIZE : (head + 1) * 2 * SIZE].astype(BF16)
        both = dot(to_token, both)
        even, odd = both[:SIZE], both[SIZE:]
        low = lane_iota(even.shape) < SIZE
        key_grad[head] = jnp.where(low, even, pltpu.roll(odd, SIZE, 1)).astype(BF16)
        value_grad[head] = jnp.where(low, pltpu.roll(even, SIZE, 1), odd).astype(BF16)


def weight_kernel(spread_in, weight_grad):
    for far in range(FAR):
        half, row = far // 4, far % 4 * PART
        for core in range(CORE):
            at = core * SHARE // 2 + row
            weight_grad[at : at + PART, half * HALF : (half + 1) * HALF] = spread_in[CORE * far + core].astype(F32)


def call(kernel, outs, args, scalars, scratch=(), space=pltpu.VMEM):
    return pl.pallas_call(
        kernel,
        out_shape=[jax.ShapeDtypeStruct(shape, dtype) for shape, dtype in outs],
        in_specs=[pl.BlockSpec(memory_space=pltpu.SMEM)] * scalars
        + [pl.BlockSpec(memory_space=space)] * (len(args) - scalars),
        out_specs=[pl.BlockSpec(memory_space=pltpu.VMEM)] * len(outs),
        scratch_shapes=list(scratch),
        compiler_params=pltpu.CompilerParams(vmem_limit_bytes=48 * 2**20),
    )(*args)


def start(offsets, keys, values, grad):
    outs = [((ROWS, LANES), BF16), ((LINE, NEAR, LANES), BF16), ((4, SIZE, HALF), BF16)]
    scratch = [pltpu.VMEM((LOCAL, SIZE, 2 * SIZE), BF16)] * 2 + [pltpu.VMEM((SIZE, HALF), BF16), pltpu.SemaphoreType.DMA((3,))]
    keys, values, grad = (pltpu.with_memory_space_constraint(array, pltpu.HBM) for array in (keys, values, grad))
    return call(start_kernel, outs, (offsets, keys, values, grad), 1, scratch, pltpu.HBM)


def far_pieces(ordered, line_in):
    return call(far_kernel, [((FAR, NEAR, LANES), BF16), ((SLOTS + NEAR, LANES), BF16)], (ordered, line_in), 0)


def attention(rank, offsets, *arrays):
    outs = [
        ((2, SIZE, HALF), F32),
        ((2, SIZE, HALF), BF16),
        ((LOCAL, SIZE, 2 * SIZE), BF16),
        ((SEND, LANES), BF16),
        ((LINE, NEAR, LANES), F32),
        ((PICKED, LANES), F32),
        ((ROWS, LANES), F32),
        ((SHARE, HALF), F32),
    ]
    scratch = [
        pltpu.VMEM((KEYS, LANES), BF16),
        pltpu.VMEM((ROWS, WIDTH), BF16),
        pltpu.VMEM((ROWS, LOCAL * SIZE), BF16),
        pltpu.VMEM((SHARE, WIDTH), F32),
        pltpu.VMEM((4, SIZE, HALF), F32),
    ]
    return call(main_kernel, outs, (rank, offsets) + arrays + (jnp.asarray(shared_levels()),), 2, scratch)


def far_return(rank, received, keep_far, keep_weight):
    args = (rank, received, keep_far, keep_weight)
    return call(far_return_kernel, [((FAR, NEAR + PART, LANES), BF16)], args, 1)[0]


def line_return(received, keep_line, far_in):
    return call(line_return_kernel, [((LINE, NEAR + PART, LANES), BF16)], (received, keep_line, far_in), 0)[0]


def spread_pieces(line_in):
    outs = [((NEAR, LANES), F32), ((FAR * CORE, PART, LANES), BF16)]
    return call(spread_kernel, outs, (line_in,), 0)


def finish(offsets, keep_own, received, near_sum):
    outs = [((LOCAL, SIZE, 2 * SIZE), BF16)] * 2
    return call(finish_kernel, outs, (offsets, keep_own, received, near_sum), 1, [pltpu.VMEM((ROWS, LANES), F32)])


def weight_rows(spread_in):
    return call(weight_kernel, [((SHARE, WIDTH), F32)], (spread_in,), 0)[0]


def trade(pieces, groups):
    return lax.all_to_all(pieces, "seq", 0, 0, axis_index_groups=groups, tiled=True)


def swap_cores(block):
    return lax.ppermute(block, "seq", [(i, i ^ 1) for i in range(FAR * LINE * CORE)])


def swap_heads(block, way):
    return lax.ppermute(block, "head", [(i, i ^ way) for i in range(4)])


def shards(queries, keys, values, out_weight, offsets, out_grad):
    index = lax.axis_index("seq")
    rank = jnp.stack([index >> 4, index >> 1 & 7, index & 1, lax.axis_index("head")]).astype(jnp.int32)
    far_groups = [[far * 16 + low for far in range(FAR)] for low in range(16)]
    line_groups = [[far * 16 + line * 2 + core for line in range(LINE)] for far in range(FAR) for core in range(CORE)]
    side_groups = [[far * 16 + line * 2 + core for far in range(FAR) for core in range(CORE)] for line in range(LINE)]
    queries, keys, values = (array.transpose(1, 0, 2) for array in (queries, keys, values))
    ordered, line_out, grad_out = start(offsets, keys, values, out_grad)
    line_in = trade(line_out, line_groups)
    far_out, partner_out = far_pieces(ordered, line_in)
    other_in = swap_cores(partner_out)
    far_in = trade(far_out, far_groups)
    other_far_in = swap_cores(far_in)
    grads = lax.all_to_all(grad_out, "head", 0, 0, tiled=True)
    output_keep, output_send, query_grad, send, keep_line, keep_far, keep_own, keep_weight = attention(
        rank, offsets, queries, out_weight, grads, ordered, line_in, far_in, other_in, other_far_in
    )
    first = swap_heads(output_send, 1)
    received = swap_cores(send)
    far_back = trade(far_return(rank, received, keep_far, keep_weight), far_groups)
    far_back, first = lax.optimization_barrier((far_back, first))
    output_sum = output_keep + first.astype(F32)
    second = swap_heads(output_sum[1].astype(BF16), 3)
    line_back = trade(line_return(received, keep_line, far_back), line_groups)
    line_back, second = lax.optimization_barrier((line_back, second))
    output = (output_sum[0] + second.astype(F32)).astype(BF16)
    near_sum, spread_out = spread_pieces(line_back)
    weight_grad = weight_rows(trade(spread_out, side_groups))
    key_grad, value_grad = finish(offsets, keep_own, received, near_sum)
    query_grad, key_grad, value_grad = (grad.transpose(1, 0, 2) for grad in (query_grad, key_grad, value_grad))
    return (output, query_grad, key_grad, value_grad, weight_grad)


def solution(mesh):
    return jax.shard_map(
        shards,
        mesh=mesh,
        in_specs=(
            P("seq", "head", None),
            P("seq", "head", None),
            P("seq", "head", None),
            P("head", None),
            P("head"),
            P("seq", "head"),
        ),
        out_specs=(
            P("seq", "head"),
            P("seq", "head", None),
            P("seq", "head", None),
            P("seq", "head", None),
            P("head", None),
        ),
        check_vma=False,
    )
```

```python
import math

import jax
import jax.numpy as jnp
import numpy as np
from jax import lax
from jax.experimental import pallas as pl
from jax.experimental.pallas import tpu as pltpu
from jax.sharding import PartitionSpec as P

FAR, LINE, CORE = 8, 8, 2
ROWS = 128
LOCAL = 3
SIZE = 64
LANES = LOCAL * 2 * SIZE
WIDTH = 768
HALF = WIDTH // 2
SCALE = SIZE**-0.5
NEAR = 32
EACH = 4
PICKED = 96
SLOTS = LINE * NEAR
LINE_AT = ROWS
FAR_AT = LINE_AT + SLOTS - NEAR
PARTNER_AT = FAR_AT + PICKED
OTHER_AT = PARTNER_AT + NEAR
OTHER_FAR_AT = OTHER_AT + SLOTS
KEYS = OTHER_FAR_AT + PICKED
SHARE = 192
PART = SHARE // FAR
SEND_FAR = SLOTS + NEAR
SEND_WEIGHT = SEND_FAR + PICKED
SEND = SEND_WEIGHT + SHARE

NT = (((1,), (1,)), ((), ()))
TN = (((0,), (0,)), ((), ()))
NN = (((1,), (0,)), ((), ()))
BF16 = jnp.bfloat16
F32 = jnp.float32


def dot(a, b, dims=NN):
    return lax.dot_general(a, b, dims, preferred_element_type=F32)


def depth_of(row):
    return 7 if row == 0 else 7 - row.bit_length()


def far_table():
    table = [(1, row) for line in range(LINE) for row in range(4)]
    table += [(far, row) for far in (2, 3) for line in range(LINE) for row in range(2)]
    return table + [(far, 0) for far in range(4, 8) for line in range(LINE)]


def key_table():
    table = [(-1, depth_of(row)) for row in range(ROWS)]
    for core in range(CORE):
        if core:
            table += [(0, depth_of(NEAR + row)) for row in range(NEAR)]
        for line in range(1 - core, LINE):
            table += [(line.bit_length(), depth_of(row)) for row in range(NEAR)]
        table += [(3 + far.bit_length(), depth_of(row)) for far, row in far_table()]
    return table


def shared_levels():
    table = key_table()
    bias = np.full((KEYS, ROWS), -1e30, np.float32)
    for key, entry in enumerate(table):
        for query in range(ROWS):
            count = min(entry[1], depth_of(query)) - entry[0]
            if count > 0:
                bias[key, query] = math.log(count)
    return bias


def reversed_bits(row):
    out = row * 0
    for bit in range(7):
        out = out | ((row >> bit) & 1) << (6 - bit)
    return out


def token_of(row):
    return jnp.where(row < SIZE, 2 * row, 2 * row - (ROWS - 1))


def one_hot(match):
    return jnp.where(match, 1.0, 0.0).astype(BF16)


def order_from(offset, row_axis):
    row = lax.broadcasted_iota(jnp.int32, (ROWS, ROWS), row_axis)
    token = token_of(lax.broadcasted_iota(jnp.int32, (ROWS, ROWS), 1 - row_axis))
    return one_hot(((reversed_bits(row) + offset) & (ROWS - 1)) == token)


def lane_iota(shape):
    return lax.broadcasted_iota(jnp.int32, shape, len(shape) - 1)


def beside(first, second):
    low = lane_iota(first.shape) < SIZE
    even = jnp.where(low, first, pltpu.roll(second, SIZE, 1))
    odd = jnp.where(low, pltpu.roll(first, SIZE, 1), second)
    return jnp.concatenate([even, odd], axis=0).astype(BF16)


def start_kernel(offsets, keys, values, ordered, line_out, keys_here, values_here, done):
    copies = [
        pltpu.make_async_copy(source, target, done.at[at])
        for at, (source, target) in enumerate(((keys, keys_here), (values, values_here)))
    ]
    for copy in copies:
        copy.start()
    orders = [order_from(offsets[head], 0) for head in range(LOCAL)]
    for copy in copies:
        copy.wait()
    for head in range(LOCAL):
        lanes = pl.ds(head * 2 * SIZE, 2 * SIZE)
        both = beside(keys_here[head].astype(F32), values_here[head].astype(F32))
        ordered[:, lanes] = dot(orders[head], both).astype(BF16)
    for slot in range(LINE):
        line_out[slot] = ordered[0:NEAR, :]


def far_place(row, far):
    second, third = row - 32, row - 64
    distance = jnp.where(row < 32, 1, jnp.where(row < 64, 2 + (second >> 4), 4 + (third >> 3)))
    line = jnp.where(row < 32, row >> 2, jnp.where(row < 64, (second >> 1) & 7, third & 7))
    index = jnp.where(row < 32, row & 3, jnp.where(row < 64, second & 1, 0))
    return ((far ^ distance) * LINE + line) * EACH + index


def far_choice(far, row_axis):
    shape = (PICKED, FAR * NEAR) if row_axis == 0 else (FAR * NEAR, PICKED)
    row = lax.broadcasted_iota(jnp.int32, shape, row_axis)
    return one_hot(far_place(row, far) == lax.broadcasted_iota(jnp.int32, shape, 1 - row_axis))


def table_kernel(rank, offsets, queries, to_order, to_token, query, choice, choice_back):
    for head in range(LOCAL):
        order = order_from(offsets[head], 0)
        pairs = queries[head].astype(F32)
        to_order[head] = order
        to_token[head] = order_from(offsets[head], 1)
        query[head] = dot(order, beside(pairs, jnp.zeros_like(pairs))).astype(BF16)
    choice[...] = far_choice(rank[0], 0)
    choice_back[...] = far_choice(rank[0], 1)


def far_kernel(ordered, line_in, grad, grad_in, far_out, partner_out, grads_out):
    grads_out[0] = grad[...]
    grads_out[1] = grad_in[...]
    for slot in range(LINE):
        partner_out[slot * NEAR : (slot + 1) * NEAR, :] = line_in[slot]
    partner_out[SLOTS:, :] = ordered[NEAR : 2 * NEAR, :]
    low = lax.broadcasted_iota(jnp.int32, (8, LANES), 0) < EACH
    for pair in range(LINE // 2):
        first, second = (line_in[2 * pair + slot, 0:16, :].astype(F32)[:8] for slot in range(2))
        rows = jnp.where(low, first, pltpu.roll(second, EACH, 0)).astype(BF16)
        for slot in range(FAR):
            far_out[slot, pair * 8 : (pair + 1) * 8, :] = rows


def main_kernel(
    rank, to_order, to_token, query, choice, weight, grads, other_grads, ordered, line_in, far_in, other_in, other_far_in, bias,
    output_keep, output_send, query_grad, send, keep_line, keep_far, keep_own, keep_weight,
    held, full_grad, attn, weight_term, parts, grad_parts,
):
    line, core, mine = rank[1], rank[2], rank[3]
    held[0:ROWS, :] = ordered[...]
    held[PARTNER_AT:OTHER_AT, :] = other_in[SLOTS:, :]
    held[FAR_AT:PARTNER_AT, :] = dot(choice[...], far_in[...].reshape(FAR * NEAR, LANES)).astype(BF16)
    held[OTHER_FAR_AT:, :] = dot(choice[...], other_far_in[...].reshape(FAR * NEAR, LANES)).astype(BF16)
    for step in range(LINE):
        slot = line ^ step
        if step:
            at = LINE_AT + (step - 1) * NEAR
            held[at : at + NEAR, :] = line_in[slot]
        at = OTHER_AT + step * NEAR
        held[at : at + NEAR, :] = other_in[pl.ds(pl.multiple_of(slot * NEAR, NEAR), NEAR), :]
    for way, piece in enumerate((grads[0], grads[1], other_grads[1], other_grads[0])):
        grad_parts[mine ^ way] = piece
    for parity in range(2):
        for half in range(2):
            place = (slice(parity * SIZE, (parity + 1) * SIZE), slice(half * HALF, (half + 1) * HALF))
            full_grad[place] = grad_parts[2 * parity + half]
    heads = range(LOCAL)
    lanes = [pl.ds(head * 2 * SIZE, 2 * SIZE) for head in heads]
    grad = dot(full_grad[...], weight[...], NT).astype(BF16)
    zeros = jnp.zeros((ROWS, SIZE), BF16)
    grad = [jnp.concatenate([zeros, grad[:, head * SIZE : (head + 1) * SIZE]], axis=1) for head in heads]
    grad = [dot(to_order[head], grad[head]).astype(BF16) for head in heads]
    blocks = [jnp.concatenate([query[head], grad[head]], axis=0) for head in heads]
    products = [dot(held[:, lanes[head]], blocks[head], NT) for head in heads]
    scores = [products[head][:, :ROWS] * SCALE + bias[...] for head in heads]
    top = [jnp.max(scores[head], axis=0, keepdims=True) for head in heads]
    expd = [jnp.exp(scores[head] - top[head]) for head in heads]
    share = [1.0 / jnp.sum(expd[head], axis=0, keepdims=True) for head in heads]
    probs = [expd[head] * share[head] for head in heads]
    rounded = [probs[head].astype(BF16) for head in heads]
    attn_head = [dot(held[:, lanes[head]], rounded[head], TN)[SIZE:, :].astype(BF16) for head in heads]
    grad_side = [grad[head].astype(F32).T[SIZE:, :] for head in heads]
    delta = [jnp.sum(grad_side[head] * attn_head[head].astype(F32), axis=0, keepdims=True) for head in heads]
    dscore = [(probs[head] * (products[head][:, ROWS:] - delta[head]) * SCALE).astype(BF16) for head in heads]
    dquery = [dot(held[:, lanes[head]], dscore[head], TN)[:SIZE, :].astype(BF16) for head in heads]
    dboth = [dot(jnp.concatenate([dscore[head], rounded[head]], axis=1), blocks[head]) for head in heads]
    for head in heads:
        attn[:, head * SIZE : (head + 1) * SIZE] = dot(to_token[head], attn_head[head], NT).astype(BF16)
        by_token = dot(to_token[head], jnp.concatenate([dquery[head], jnp.zeros_like(dquery[head])], axis=0), NT)
        query_grad[head] = (by_token[:SIZE] + pltpu.roll(by_token[SIZE:], SIZE, 1)).astype(BF16)
        keep_own[:, lanes[head]] = dboth[head][0:ROWS]
        keep_far[:, lanes[head]] = dboth[head][FAR_AT:PARTNER_AT]
        send[SLOTS:SEND_FAR, lanes[head]] = dboth[head][PARTNER_AT:OTHER_AT].astype(BF16)
        send[SEND_FAR:SEND_WEIGHT, lanes[head]] = dboth[head][OTHER_FAR_AT:].astype(BF16)
        for step in range(LINE):
            slot = line ^ step
            at = LINE_AT + (step - 1) * NEAR
            keep_line[slot, :, lanes[head]] = dboth[head][at : at + NEAR] if step else jnp.zeros((NEAR, 2 * SIZE), F32)
            at = OTHER_AT + step * NEAR
            rows = pl.ds(pl.multiple_of(slot * NEAR, NEAR), NEAR)
            send[rows, lanes[head]] = dboth[head][at : at + NEAR].astype(BF16)
    part = dot(attn[...], weight[...])
    for parity in range(2):
        for half in range(2):
            piece = part[parity * SIZE : (parity + 1) * SIZE, half * HALF : (half + 1) * HALF]
            parts[2 * parity + half] = piece
    for step, way in ((0, 0), (1, 3)):
        output_keep[step] = parts[mine ^ way]
        output_send[step] = parts[mine ^ way ^ 1].astype(BF16)
    weight_term[...] = dot(attn[...], full_grad[...], TN)
    rows = SHARE // 2
    mine = pl.ds(pl.multiple_of(core * rows, 8), rows)
    theirs = pl.ds(pl.multiple_of((1 - core) * rows, 8), rows)
    for half in range(2):
        columns = pl.ds(half * HALF, HALF)
        keep_weight[half * rows : (half + 1) * rows, :] = weight_term[mine, columns]
        at = SEND_WEIGHT + half * rows
        send[at : at + rows, :] = weight_term[theirs, columns].astype(BF16)


def far_return_kernel(choice_back, received, keep_far, keep_weight, far_out):
    picked = (keep_far[...] + received[SEND_FAR:SEND_WEIGHT, :].astype(F32)).astype(BF16)
    rows = dot(choice_back[...], picked).astype(BF16)
    weight = (keep_weight[...] + received[SEND_WEIGHT:, :].astype(F32)).astype(BF16)
    for slot in range(FAR):
        far_out[slot, 0:NEAR, :] = rows[slot * NEAR : (slot + 1) * NEAR]
        far_out[slot, NEAR:, :] = weight[slot * PART : (slot + 1) * PART]


def line_return_kernel(received, keep_line, far_in, line_out):
    total = far_in[0].astype(F32)
    for slot in range(1, FAR):
        total = total + far_in[slot].astype(F32)
    low = lax.broadcasted_iota(jnp.int32, (8, LANES), 0) < EACH
    for slot in range(LINE):
        rows = keep_line[slot] + received[slot * NEAR : (slot + 1) * NEAR, :].astype(F32)
        both = total[slot // 2 * 8 : slot // 2 * 8 + 8]
        first = jnp.where(low, pltpu.roll(both, EACH, 0) if slot % 2 else both, 0.0)
        line_out[slot, 0:NEAR, :] = jnp.concatenate([rows[:8] + first, rows[8:]], axis=0).astype(BF16)
        line_out[slot, NEAR:, :] = total[NEAR:].astype(BF16)


def spread_kernel(line_in, near_sum, spread_out):
    total = line_in[0].astype(F32)
    for slot in range(1, LINE):
        total = total + line_in[slot].astype(F32)
    near_sum[...] = total[:NEAR]
    part = total[NEAR:].astype(BF16)
    for slot in range(FAR * CORE):
        spread_out[slot] = part


def finish_kernel(to_token, keep_own, received, near_sum, key_grad, value_grad, own):
    own[...] = keep_own[...]
    own[NEAR : 2 * NEAR, :] += received[SLOTS:SEND_FAR, :].astype(F32)
    own[0:NEAR, :] += near_sum[...]
    for head in range(LOCAL):
        both = own[:, head * 2 * SIZE : (head + 1) * 2 * SIZE].astype(BF16)
        both = dot(to_token[head], both)
        even, odd = both[:SIZE], both[SIZE:]
        low = lane_iota(even.shape) < SIZE
        key_grad[head] = jnp.where(low, even, pltpu.roll(odd, SIZE, 1)).astype(BF16)
        value_grad[head] = jnp.where(low, pltpu.roll(even, SIZE, 1), odd).astype(BF16)


def weight_kernel(spread_in, weight_grad):
    for far in range(FAR):
        half, row = far // 4, far % 4 * PART
        for core in range(CORE):
            at = core * SHARE // 2 + row
            weight_grad[at : at + PART, half * HALF : (half + 1) * HALF] = spread_in[CORE * far + core].astype(F32)


def call(kernel, outs, args, scalars, scratch=(), space=pltpu.VMEM):
    return pl.pallas_call(
        kernel,
        out_shape=[jax.ShapeDtypeStruct(shape, dtype) for shape, dtype in outs],
        in_specs=[pl.BlockSpec(memory_space=pltpu.SMEM)] * scalars
        + [pl.BlockSpec(memory_space=space)] * (len(args) - scalars),
        out_specs=[pl.BlockSpec(memory_space=pltpu.VMEM)] * len(outs),
        scratch_shapes=list(scratch),
        compiler_params=pltpu.CompilerParams(vmem_limit_bytes=48 * 2**20),
    )(*args)


def start(offsets, keys, values):
    outs = [((ROWS, LANES), BF16), ((LINE, NEAR, LANES), BF16)]
    scratch = [pltpu.VMEM((LOCAL, SIZE, 2 * SIZE), BF16)] * 2 + [pltpu.SemaphoreType.DMA((2,))]
    args = (pltpu.with_memory_space_constraint(array, pltpu.HBM) for array in (offsets, keys, values))
    return call(start_kernel, outs, tuple(args), 1, scratch, pltpu.HBM)


def tables(rank, offsets, queries):
    square = (LOCAL, ROWS, ROWS)
    outs = [(square, BF16)] * 3 + [((PICKED, FAR * NEAR), BF16), ((FAR * NEAR, PICKED), BF16)]
    return call(table_kernel, outs, (rank, offsets, queries), 2)


def far_pieces(ordered, line_in, grad, grad_in):
    outs = [((FAR, NEAR, LANES), BF16), ((SLOTS + NEAR, LANES), BF16), ((2, SIZE, HALF), BF16)]
    return call(far_kernel, outs, (ordered, line_in, grad, grad_in), 0)


def attention(rank, *arrays):
    outs = [
        ((2, SIZE, HALF), F32),
        ((2, SIZE, HALF), BF16),
        ((LOCAL, SIZE, 2 * SIZE), BF16),
        ((SEND, LANES), BF16),
        ((LINE, NEAR, LANES), F32),
        ((PICKED, LANES), F32),
        ((ROWS, LANES), F32),
        ((SHARE, HALF), F32),
    ]
    scratch = [
        pltpu.VMEM((KEYS, LANES), BF16),
        pltpu.VMEM((ROWS, WIDTH), BF16),
        pltpu.VMEM((ROWS, LOCAL * SIZE), BF16),
        pltpu.VMEM((SHARE, WIDTH), F32),
        pltpu.VMEM((4, SIZE, HALF), F32),
        pltpu.VMEM((4, SIZE, HALF), BF16),
    ]
    return call(main_kernel, outs, (rank,) + arrays + (jnp.asarray(shared_levels()),), 1, scratch)


def far_return(choice_back, received, keep_far, keep_weight):
    args = (choice_back, received, keep_far, keep_weight)
    return call(far_return_kernel, [((FAR, NEAR + PART, LANES), BF16)], args, 0)[0]


def line_return(received, keep_line, far_in):
    return call(line_return_kernel, [((LINE, NEAR + PART, LANES), BF16)], (received, keep_line, far_in), 0)[0]


def spread_pieces(line_in):
    outs = [((NEAR, LANES), F32), ((FAR * CORE, PART, LANES), BF16)]
    return call(spread_kernel, outs, (line_in,), 0)


def finish(to_token, keep_own, received, near_sum):
    outs = [((LOCAL, SIZE, 2 * SIZE), BF16)] * 2
    return call(finish_kernel, outs, (to_token, keep_own, received, near_sum), 0, [pltpu.VMEM((ROWS, LANES), F32)])


def weight_rows(spread_in):
    return call(weight_kernel, [((SHARE, WIDTH), F32)], (spread_in,), 0)[0]


def trade(pieces, groups):
    return lax.all_to_all(pieces, "seq", 0, 0, axis_index_groups=groups, tiled=True)


def swap_cores(block):
    return lax.ppermute(block, "seq", [(i, i ^ 1) for i in range(FAR * LINE * CORE)])


def swap_heads(block, way):
    return lax.ppermute(block, "head", [(i, i ^ way) for i in range(4)])


def shards(queries, keys, values, out_weight, offsets, out_grad):
    index = lax.axis_index("seq")
    rank = jnp.stack([index >> 4, index >> 1 & 7, index & 1, lax.axis_index("head")]).astype(jnp.int32)
    far_groups = [[far * 16 + low for far in range(FAR)] for low in range(16)]
    line_groups = [[far * 16 + line * 2 + core for line in range(LINE)] for far in range(FAR) for core in range(CORE)]
    side_groups = [[far * 16 + line * 2 + core for far in range(FAR) for core in range(CORE)] for line in range(LINE)]
    queries, keys, values = (array.transpose(1, 0, 2) for array in (queries, keys, values))
    ordered, line_out = start(offsets, keys, values)
    grad_in = swap_heads(out_grad, 1)
    to_order, to_token, query, choice, choice_back = tables(rank, offsets, queries)
    line_in = trade(line_out, line_groups)
    far_out, partner_out, grads = far_pieces(ordered, line_in, out_grad, grad_in)
    other_grads = swap_heads(grads, 3)
    other_in = swap_cores(partner_out)
    far_in = trade(far_out, far_groups)
    other_far_in = swap_cores(far_in)
    output_keep, output_send, query_grad, send, keep_line, keep_far, keep_own, keep_weight = attention(
        rank, to_order, to_token, query, choice, out_weight, grads, other_grads,
        ordered, line_in, far_in, other_in, other_far_in,
    )
    first = swap_heads(output_send, 1)
    received = swap_cores(send)
    far_back = trade(far_return(choice_back, received, keep_far, keep_weight), far_groups)
    line_back = trade(line_return(received, keep_line, far_back), line_groups)
    line_back, first = lax.optimization_barrier((line_back, first))
    output_sum = output_keep + first.astype(F32)
    second = swap_heads(output_sum[1].astype(BF16), 3)
    near_sum, spread_out = spread_pieces(line_back)
    spread_in = trade(spread_out, side_groups)
    key_grad, value_grad = finish(to_token, keep_own, received, near_sum)
    output = (output_sum[0] + second.astype(F32)).astype(BF16)
    weight_grad = weight_rows(spread_in)
    query_grad, key_grad, value_grad = (grad.transpose(1, 0, 2) for grad in (query_grad, key_grad, value_grad))
    return (output, query_grad, key_grad, value_grad, weight_grad)


def solution(mesh):
    return jax.shard_map(
        shards,
        mesh=mesh,
        in_specs=(
            P("seq", "head", None),
            P("seq", "head", None),
            P("seq", "head", None),
            P("head", None),
            P("head"),
            P("seq", "head"),
        ),
        out_specs=(
            P("seq", "head"),
            P("seq", "head", None),
            P("seq", "head", None),
            P("seq", "head", None),
            P("head", None),
        ),
        check_vma=False,
    )
```

```python
import math

import jax
import jax.numpy as jnp
import numpy as np
from jax import lax
from jax.experimental import pallas as pl
from jax.experimental.pallas import tpu as pltpu
from jax.sharding import PartitionSpec as P

FAR, LINE, CORE = 8, 8, 2
ROWS = 128
LOCAL = 3
SIZE = 64
LANES = LOCAL * 2 * SIZE
WIDTH = 768
HALF = WIDTH // 2
SCALE = SIZE**-0.5
NEAR = 32
EACH = 4
PICKED = 96
SLOTS = LINE * NEAR
LINE_AT = ROWS
FAR_AT = LINE_AT + SLOTS - NEAR
PARTNER_AT = FAR_AT + PICKED
OTHER_AT = PARTNER_AT + NEAR
OTHER_FAR_AT = OTHER_AT + SLOTS
KEYS = OTHER_FAR_AT + PICKED
SHARE = 192
PART = SHARE // FAR
SEND_FAR = SLOTS + NEAR
SEND_WEIGHT = SEND_FAR + PICKED
SEND = SEND_WEIGHT + SHARE

NT = (((1,), (1,)), ((), ()))
TN = (((0,), (0,)), ((), ()))
NN = (((1,), (0,)), ((), ()))
BF16 = jnp.bfloat16
F32 = jnp.float32


def dot(a, b, dims=NN):
    return lax.dot_general(a, b, dims, preferred_element_type=F32)


def depth_of(row):
    return 7 if row == 0 else 7 - row.bit_length()


def far_table():
    table = [(1, row) for line in range(LINE) for row in range(4)]
    table += [(far, row) for far in (2, 3) for line in range(LINE) for row in range(2)]
    return table + [(far, 0) for far in range(4, 8) for line in range(LINE)]


def key_table():
    table = [(-1, depth_of(row)) for row in range(ROWS)]
    for core in range(CORE):
        if core:
            table += [(0, depth_of(NEAR + row)) for row in range(NEAR)]
        for line in range(1 - core, LINE):
            table += [(line.bit_length(), depth_of(row)) for row in range(NEAR)]
        table += [(3 + far.bit_length(), depth_of(row)) for far, row in far_table()]
    return table


def shared_levels():
    table = key_table()
    bias = np.full((KEYS, ROWS), -1e30, np.float32)
    for key, entry in enumerate(table):
        for query in range(ROWS):
            count = min(entry[1], depth_of(query)) - entry[0]
            if count > 0:
                bias[key, query] = math.log(count)
    return bias


def reversed_bits(row):
    out = row * 0
    for bit in range(7):
        out = out | ((row >> bit) & 1) << (6 - bit)
    return out


def token_of(row):
    return jnp.where(row < SIZE, 2 * row, 2 * row - (ROWS - 1))


def one_hot(match):
    return jnp.where(match, 1.0, 0.0).astype(BF16)


def order_from(offset, row_axis):
    row = lax.broadcasted_iota(jnp.int32, (ROWS, ROWS), row_axis)
    token = token_of(lax.broadcasted_iota(jnp.int32, (ROWS, ROWS), 1 - row_axis))
    return one_hot(((reversed_bits(row) + offset) & (ROWS - 1)) == token)


def lane_iota(shape):
    return lax.broadcasted_iota(jnp.int32, shape, len(shape) - 1)


def beside(first, second):
    low = lane_iota(first.shape) < SIZE
    even = jnp.where(low, first, pltpu.roll(second, SIZE, 1))
    odd = jnp.where(low, pltpu.roll(first, SIZE, 1), second)
    return jnp.concatenate([even, odd], axis=0).astype(BF16)


def start_kernel(offsets_far, keys, values, ordered, line_out, offsets, keys_here, values_here, done):
    copies = [
        pltpu.make_async_copy(source, target, done.at[at])
        for at, (source, target) in enumerate(((offsets_far, offsets), (keys, keys_here), (values, values_here)))
    ]
    for copy in copies:
        copy.start()
    copies[0].wait()
    orders = [order_from(offsets[head], 0) for head in range(LOCAL)]
    for copy in copies[1:]:
        copy.wait()
    for head in range(LOCAL):
        lanes = pl.ds(head * 2 * SIZE, 2 * SIZE)
        both = beside(keys_here[head].astype(F32), values_here[head].astype(F32))
        ordered[:, lanes] = dot(orders[head], both).astype(BF16)
    for slot in range(LINE):
        line_out[slot] = ordered[0:NEAR, :]


def far_place(row, far):
    second, third = row - 32, row - 64
    distance = jnp.where(row < 32, 1, jnp.where(row < 64, 2 + (second >> 4), 4 + (third >> 3)))
    line = jnp.where(row < 32, row >> 2, jnp.where(row < 64, (second >> 1) & 7, third & 7))
    index = jnp.where(row < 32, row & 3, jnp.where(row < 64, second & 1, 0))
    return ((far ^ distance) * LINE + line) * EACH + index


def far_choice(far, row_axis):
    shape = (PICKED, FAR * NEAR) if row_axis == 0 else (FAR * NEAR, PICKED)
    row = lax.broadcasted_iota(jnp.int32, shape, row_axis)
    return one_hot(far_place(row, far) == lax.broadcasted_iota(jnp.int32, shape, 1 - row_axis))


def table_kernel(rank, offsets, queries, grad, to_order, to_token, query, choice, choice_back, grads_out):
    for slot in range(4):
        grads_out[slot] = grad[...]
    for head in range(LOCAL):
        order = order_from(offsets[head], 0)
        pairs = queries[head].astype(F32)
        to_order[head] = order
        to_token[head] = order_from(offsets[head], 1)
        query[head] = dot(order, beside(pairs, jnp.zeros_like(pairs))).astype(BF16)
    choice[...] = far_choice(rank[0], 0)
    choice_back[...] = far_choice(rank[0], 1)


def far_kernel(ordered, line_in, far_out, partner_out):
    for slot in range(LINE):
        partner_out[slot * NEAR : (slot + 1) * NEAR, :] = line_in[slot]
    partner_out[SLOTS:, :] = ordered[NEAR : 2 * NEAR, :]
    low = lax.broadcasted_iota(jnp.int32, (8, LANES), 0) < EACH
    for pair in range(LINE // 2):
        first, second = (line_in[2 * pair + slot, 0:16, :].astype(F32)[:8] for slot in range(2))
        rows = jnp.where(low, first, pltpu.roll(second, EACH, 0)).astype(BF16)
        for slot in range(FAR):
            far_out[slot, pair * 8 : (pair + 1) * 8, :] = rows


def main_kernel(
    rank, to_order, to_token, query, choice, weight, grads, ordered, line_in, far_in, other_in, other_far_in, bias,
    output_keep, output_send, query_grad, send, keep_line, keep_far, keep_own, keep_weight,
    held, full_grad, attn, weight_term, parts,
):
    line, core, mine = rank[1], rank[2], rank[3]
    held[0:ROWS, :] = ordered[...]
    held[PARTNER_AT:OTHER_AT, :] = other_in[SLOTS:, :]
    held[FAR_AT:PARTNER_AT, :] = dot(choice[...], far_in[...].reshape(FAR * NEAR, LANES)).astype(BF16)
    held[OTHER_FAR_AT:, :] = dot(choice[...], other_far_in[...].reshape(FAR * NEAR, LANES)).astype(BF16)
    for step in range(LINE):
        slot = line ^ step
        if step:
            at = LINE_AT + (step - 1) * NEAR
            held[at : at + NEAR, :] = line_in[slot]
        at = OTHER_AT + step * NEAR
        held[at : at + NEAR, :] = other_in[pl.ds(pl.multiple_of(slot * NEAR, NEAR), NEAR), :]
    for parity in range(2):
        for half in range(2):
            place = (slice(parity * SIZE, (parity + 1) * SIZE), slice(half * HALF, (half + 1) * HALF))
            full_grad[place] = grads[2 * parity + half]
    heads = range(LOCAL)
    lanes = [pl.ds(head * 2 * SIZE, 2 * SIZE) for head in heads]
    grad = dot(full_grad[...], weight[...], NT).astype(BF16)
    zeros = jnp.zeros((ROWS, SIZE), BF16)
    grad = [jnp.concatenate([zeros, grad[:, head * SIZE : (head + 1) * SIZE]], axis=1) for head in heads]
    grad = [dot(to_order[head], grad[head]).astype(BF16) for head in heads]
    blocks = [jnp.concatenate([query[head], grad[head]], axis=0) for head in heads]
    products = [dot(held[:, lanes[head]], blocks[head], NT) for head in heads]
    scores = [products[head][:, :ROWS] * SCALE + bias[...] for head in heads]
    top = [jnp.max(scores[head], axis=0, keepdims=True) for head in heads]
    expd = [jnp.exp(scores[head] - top[head]) for head in heads]
    share = [1.0 / jnp.sum(expd[head], axis=0, keepdims=True) for head in heads]
    probs = [expd[head] * share[head] for head in heads]
    rounded = [probs[head].astype(BF16) for head in heads]
    attn_head = [dot(held[:, lanes[head]], rounded[head], TN)[SIZE:, :].astype(BF16) for head in heads]
    grad_side = [grad[head].astype(F32).T[SIZE:, :] for head in heads]
    delta = [jnp.sum(grad_side[head] * attn_head[head].astype(F32), axis=0, keepdims=True) for head in heads]
    dscore = [(probs[head] * (products[head][:, ROWS:] - delta[head]) * SCALE).astype(BF16) for head in heads]
    dquery = [dot(held[:, lanes[head]], dscore[head], TN)[:SIZE, :].astype(BF16) for head in heads]
    dboth = [dot(jnp.concatenate([dscore[head], rounded[head]], axis=1), blocks[head]) for head in heads]
    for head in heads:
        attn[:, head * SIZE : (head + 1) * SIZE] = dot(to_token[head], attn_head[head], NT).astype(BF16)
        by_token = dot(to_token[head], jnp.concatenate([dquery[head], jnp.zeros_like(dquery[head])], axis=0), NT)
        query_grad[head] = (by_token[:SIZE] + pltpu.roll(by_token[SIZE:], SIZE, 1)).astype(BF16)
        keep_own[:, lanes[head]] = dboth[head][0:ROWS]
        keep_far[:, lanes[head]] = dboth[head][FAR_AT:PARTNER_AT]
        send[SLOTS:SEND_FAR, lanes[head]] = dboth[head][PARTNER_AT:OTHER_AT].astype(BF16)
        send[SEND_FAR:SEND_WEIGHT, lanes[head]] = dboth[head][OTHER_FAR_AT:].astype(BF16)
        for step in range(LINE):
            slot = line ^ step
            at = LINE_AT + (step - 1) * NEAR
            keep_line[slot, :, lanes[head]] = dboth[head][at : at + NEAR] if step else jnp.zeros((NEAR, 2 * SIZE), F32)
            at = OTHER_AT + step * NEAR
            rows = pl.ds(pl.multiple_of(slot * NEAR, NEAR), NEAR)
            send[rows, lanes[head]] = dboth[head][at : at + NEAR].astype(BF16)
    part = dot(attn[...], weight[...])
    for parity in range(2):
        for half in range(2):
            piece = part[parity * SIZE : (parity + 1) * SIZE, half * HALF : (half + 1) * HALF]
            parts[2 * parity + half] = piece
    for step, way in ((0, 0), (1, 3)):
        output_keep[step] = parts[mine ^ way]
        output_send[step] = parts[mine ^ way ^ 1].astype(BF16)
    weight_term[...] = dot(attn[...], full_grad[...], TN)
    rows = SHARE // 2
    mine = pl.ds(pl.multiple_of(core * rows, 8), rows)
    theirs = pl.ds(pl.multiple_of((1 - core) * rows, 8), rows)
    for half in range(2):
        columns = pl.ds(half * HALF, HALF)
        keep_weight[half * rows : (half + 1) * rows, :] = weight_term[mine, columns]
        at = SEND_WEIGHT + half * rows
        send[at : at + rows, :] = weight_term[theirs, columns].astype(BF16)


def far_return_kernel(choice_back, received, keep_far, keep_weight, far_out):
    picked = (keep_far[...] + received[SEND_FAR:SEND_WEIGHT, :].astype(F32)).astype(BF16)
    rows = dot(choice_back[...], picked).astype(BF16)
    weight = (keep_weight[...] + received[SEND_WEIGHT:, :].astype(F32)).astype(BF16)
    for slot in range(FAR):
        far_out[slot, 0:NEAR, :] = rows[slot * NEAR : (slot + 1) * NEAR]
        far_out[slot, NEAR:, :] = weight[slot * PART : (slot + 1) * PART]


def line_return_kernel(received, keep_line, far_in, line_out):
    total = far_in[0].astype(F32)
    for slot in range(1, FAR):
        total = total + far_in[slot].astype(F32)
    low = lax.broadcasted_iota(jnp.int32, (8, LANES), 0) < EACH
    for slot in range(LINE):
        rows = keep_line[slot] + received[slot * NEAR : (slot + 1) * NEAR, :].astype(F32)
        both = total[slot // 2 * 8 : slot // 2 * 8 + 8]
        first = jnp.where(low, pltpu.roll(both, EACH, 0) if slot % 2 else both, 0.0)
        line_out[slot, 0:NEAR, :] = jnp.concatenate([rows[:8] + first, rows[8:]], axis=0).astype(BF16)
        line_out[slot, NEAR:, :] = total[NEAR:].astype(BF16)


def spread_kernel(line_in, near_sum, spread_out):
    total = line_in[0].astype(F32)
    for slot in range(1, LINE):
        total = total + line_in[slot].astype(F32)
    near_sum[...] = total[:NEAR]
    part = total[NEAR:].astype(BF16)
    for slot in range(FAR * CORE):
        spread_out[slot] = part


def finish_kernel(to_token, keep_own, received, near_sum, key_grad, value_grad, own):
    own[...] = keep_own[...]
    own[NEAR : 2 * NEAR, :] += received[SLOTS:SEND_FAR, :].astype(F32)
    own[0:NEAR, :] += near_sum[...]
    for head in range(LOCAL):
        both = own[:, head * 2 * SIZE : (head + 1) * 2 * SIZE].astype(BF16)
        both = dot(to_token[head], both)
        even, odd = both[:SIZE], both[SIZE:]
        low = lane_iota(even.shape) < SIZE
        key_grad[head] = jnp.where(low, even, pltpu.roll(odd, SIZE, 1)).astype(BF16)
        value_grad[head] = jnp.where(low, pltpu.roll(even, SIZE, 1), odd).astype(BF16)


def weight_kernel(spread_in, weight_grad):
    for far in range(FAR):
        half, row = far // 4, far % 4 * PART
        for core in range(CORE):
            at = core * SHARE // 2 + row
            weight_grad[at : at + PART, half * HALF : (half + 1) * HALF] = spread_in[CORE * far + core].astype(F32)


def call(kernel, outs, args, scalars, scratch=(), space=pltpu.VMEM):
    return pl.pallas_call(
        kernel,
        out_shape=[jax.ShapeDtypeStruct(shape, dtype) for shape, dtype in outs],
        in_specs=[pl.BlockSpec(memory_space=pltpu.SMEM)] * scalars
        + [pl.BlockSpec(memory_space=space)] * (len(args) - scalars),
        out_specs=[pl.BlockSpec(memory_space=pltpu.VMEM)] * len(outs),
        scratch_shapes=list(scratch),
        compiler_params=pltpu.CompilerParams(vmem_limit_bytes=48 * 2**20),
    )(*args)


def start(offsets, keys, values):
    outs = [((ROWS, LANES), BF16), ((LINE, NEAR, LANES), BF16)]
    here = pltpu.VMEM((LOCAL, SIZE, 2 * SIZE), BF16)
    scratch = [pltpu.SMEM((LOCAL,), jnp.int32), here, here, pltpu.SemaphoreType.DMA((3,))]
    args = (pltpu.with_memory_space_constraint(array, pltpu.HBM) for array in (offsets, keys, values))
    return call(start_kernel, outs, tuple(args), 0, scratch, pltpu.HBM)


def tables(rank, offsets, queries, grad):
    square = (LOCAL, ROWS, ROWS)
    outs = [(square, BF16)] * 3 + [((PICKED, FAR * NEAR), BF16), ((FAR * NEAR, PICKED), BF16)]
    return call(table_kernel, outs + [((4, SIZE, HALF), BF16)], (rank, offsets, queries, grad), 2)


def far_pieces(ordered, line_in):
    return call(far_kernel, [((FAR, NEAR, LANES), BF16), ((SLOTS + NEAR, LANES), BF16)], (ordered, line_in), 0)


def attention(rank, *arrays):
    outs = [
        ((2, SIZE, HALF), F32),
        ((2, SIZE, HALF), BF16),
        ((LOCAL, SIZE, 2 * SIZE), BF16),
        ((SEND, LANES), BF16),
        ((LINE, NEAR, LANES), F32),
        ((PICKED, LANES), F32),
        ((ROWS, LANES), F32),
        ((SHARE, HALF), F32),
    ]
    scratch = [
        pltpu.VMEM((KEYS, LANES), BF16),
        pltpu.VMEM((ROWS, WIDTH), BF16),
        pltpu.VMEM((ROWS, LOCAL * SIZE), BF16),
        pltpu.VMEM((SHARE, WIDTH), F32),
        pltpu.VMEM((4, SIZE, HALF), F32),
    ]
    return call(main_kernel, outs, (rank,) + arrays + (jnp.asarray(shared_levels()),), 1, scratch)


def far_return(choice_back, received, keep_far, keep_weight):
    args = (choice_back, received, keep_far, keep_weight)
    return call(far_return_kernel, [((FAR, NEAR + PART, LANES), BF16)], args, 0)[0]


def line_return(received, keep_line, far_in):
    return call(line_return_kernel, [((LINE, NEAR + PART, LANES), BF16)], (received, keep_line, far_in), 0)[0]


def spread_pieces(line_in):
    outs = [((NEAR, LANES), F32), ((FAR * CORE, PART, LANES), BF16)]
    return call(spread_kernel, outs, (line_in,), 0)


def finish(to_token, keep_own, received, near_sum):
    outs = [((LOCAL, SIZE, 2 * SIZE), BF16)] * 2
    return call(finish_kernel, outs, (to_token, keep_own, received, near_sum), 0, [pltpu.VMEM((ROWS, LANES), F32)])


def weight_rows(spread_in):
    return call(weight_kernel, [((SHARE, WIDTH), F32)], (spread_in,), 0)[0]


def trade(pieces, groups):
    return lax.all_to_all(pieces, "seq", 0, 0, axis_index_groups=groups, tiled=True)


def swap_cores(block):
    return lax.ppermute(block, "seq", [(i, i ^ 1) for i in range(FAR * LINE * CORE)])


def swap_heads(block, way):
    return lax.ppermute(block, "head", [(i, i ^ way) for i in range(4)])


def shards(queries, keys, values, out_weight, offsets, out_grad):
    index = lax.axis_index("seq")
    rank = jnp.stack([index >> 4, index >> 1 & 7, index & 1, lax.axis_index("head")]).astype(jnp.int32)
    far_groups = [[far * 16 + low for far in range(FAR)] for low in range(16)]
    line_groups = [[far * 16 + line * 2 + core for line in range(LINE)] for far in range(FAR) for core in range(CORE)]
    side_groups = [[far * 16 + line * 2 + core for far in range(FAR) for core in range(CORE)] for line in range(LINE)]
    queries, keys, values = (array.transpose(1, 0, 2) for array in (queries, keys, values))
    ordered, line_out = start(offsets, keys, values)
    to_order, to_token, query, choice, choice_back, grads_out = tables(rank, offsets, queries, out_grad)
    line_in = trade(line_out, line_groups)
    far_out, partner_out = far_pieces(ordered, line_in)
    other_in = swap_cores(partner_out)
    far_in = trade(far_out, far_groups)
    other_far_in = swap_cores(far_in)
    grads = lax.all_to_all(grads_out, "head", 0, 0, tiled=True)
    output_keep, output_send, query_grad, send, keep_line, keep_far, keep_own, keep_weight = attention(
        rank, to_order, to_token, query, choice, out_weight, grads, ordered, line_in, far_in, other_in, other_far_in
    )
    first = swap_heads(output_send, 1)
    received = swap_cores(send)
    far_back = trade(far_return(choice_back, received, keep_far, keep_weight), far_groups)
    line_back = trade(line_return(received, keep_line, far_back), line_groups)
    line_back, first = lax.optimization_barrier((line_back, first))
    output_sum = output_keep + first.astype(F32)
    second = swap_heads(output_sum[1].astype(BF16), 3)
    near_sum, spread_out = spread_pieces(line_back)
    spread_in = trade(spread_out, side_groups)
    key_grad, value_grad = finish(to_token, keep_own, received, near_sum)
    output = (output_sum[0] + second.astype(F32)).astype(BF16)
    weight_grad = weight_rows(spread_in)
    query_grad, key_grad, value_grad = (grad.transpose(1, 0, 2) for grad in (query_grad, key_grad, value_grad))
    return (output, query_grad, key_grad, value_grad, weight_grad)


def solution(mesh):
    return jax.shard_map(
        shards,
        mesh=mesh,
        in_specs=(
            P("seq", "head", None),
            P("seq", "head", None),
            P("seq", "head", None),
            P("head", None),
            P("head"),
            P("seq", "head"),
        ),
        out_specs=(
            P("seq", "head"),
            P("seq", "head", None),
            P("seq", "head", None),
            P("seq", "head", None),
            P("head", None),
        ),
        check_vma=False,
    )
```

```python
import math

import jax
import jax.numpy as jnp
import numpy as np
from jax import lax
from jax.experimental import pallas as pl
from jax.experimental.pallas import tpu as pltpu
from jax.sharding import PartitionSpec as P

FAR, LINE, CORE = 8, 8, 2
ROWS = 128
LOCAL = 3
SIZE = 64
LANES = LOCAL * 2 * SIZE
WIDTH = 768
HALF = WIDTH // 2
SCALE = SIZE**-0.5
NEAR = 32
EACH = 4
PICKED = 96
SLOTS = LINE * NEAR
LINE_AT = ROWS
FAR_AT = LINE_AT + SLOTS - NEAR
PARTNER_AT = FAR_AT + PICKED
OTHER_AT = PARTNER_AT + NEAR
OTHER_FAR_AT = OTHER_AT + SLOTS
KEYS = OTHER_FAR_AT + PICKED
SHARE = 192
PART = SHARE // FAR
SEND_FAR = SLOTS + NEAR
SEND_WEIGHT = SEND_FAR + PICKED
SEND = SEND_WEIGHT + SHARE

NT = (((1,), (1,)), ((), ()))
TN = (((0,), (0,)), ((), ()))
NN = (((1,), (0,)), ((), ()))
BF16 = jnp.bfloat16
F32 = jnp.float32


def dot(a, b, dims=NN):
    return lax.dot_general(a, b, dims, preferred_element_type=F32)


def depth_of(row):
    return 7 if row == 0 else 7 - row.bit_length()


def far_table():
    table = [(1, row) for line in range(LINE) for row in range(4)]
    table += [(far, row) for far in (2, 3) for line in range(LINE) for row in range(2)]
    return table + [(far, 0) for far in range(4, 8) for line in range(LINE)]


def key_table():
    table = [(-1, depth_of(row)) for row in range(ROWS)]
    for core in range(CORE):
        if core:
            table += [(0, depth_of(NEAR + row)) for row in range(NEAR)]
        for line in range(1 - core, LINE):
            table += [(line.bit_length(), depth_of(row)) for row in range(NEAR)]
        table += [(3 + far.bit_length(), depth_of(row)) for far, row in far_table()]
    return table


def shared_levels():
    table = key_table()
    bias = np.full((KEYS, ROWS), -1e30, np.float32)
    for key, entry in enumerate(table):
        for query in range(ROWS):
            count = min(entry[1], depth_of(query)) - entry[0]
            if count > 0:
                bias[key, query] = math.log(count)
    return bias


def reversed_bits(row):
    out = row * 0
    for bit in range(7):
        out = out | ((row >> bit) & 1) << (6 - bit)
    return out


def token_of(row):
    return jnp.where(row < SIZE, 2 * row, 2 * row - (ROWS - 1))


def one_hot(match):
    return jnp.where(match, 1.0, 0.0).astype(BF16)


def here():
    index = lax.axis_index("seq")
    return index >> 4, (index >> 1) & 7, index & 1, lax.axis_index("head")


def order_from(offset, row_axis):
    row = lax.broadcasted_iota(jnp.int32, (ROWS, ROWS), row_axis)
    token = token_of(lax.broadcasted_iota(jnp.int32, (ROWS, ROWS), 1 - row_axis))
    return one_hot(((reversed_bits(row) + offset) & (ROWS - 1)) == token)


def lane_iota(shape):
    return lax.broadcasted_iota(jnp.int32, shape, len(shape) - 1)


def beside(first, second):
    low = lane_iota(first.shape) < SIZE
    even = jnp.where(low, first, pltpu.roll(second, SIZE, 1))
    odd = jnp.where(low, pltpu.roll(first, SIZE, 1), second)
    return jnp.concatenate([even, odd], axis=0).astype(BF16)


def start_kernel(offsets_far, keys, values, ordered, line_out, offsets, keys_here, values_here, done):
    copies = [
        pltpu.make_async_copy(source, target, done.at[at])
        for at, (source, target) in enumerate(((offsets_far, offsets), (keys, keys_here), (values, values_here)))
    ]
    for copy in copies:
        copy.start()
    copies[0].wait()
    orders = [order_from(offsets[head], 0) for head in range(LOCAL)]
    for copy in copies[1:]:
        copy.wait()
    for head in range(LOCAL):
        lanes = pl.ds(head * 2 * SIZE, 2 * SIZE)
        both = beside(keys_here[head].astype(F32), values_here[head].astype(F32))
        ordered[:, lanes] = dot(orders[head], both).astype(BF16)
    for slot in range(LINE):
        line_out[slot] = ordered[0:NEAR, :]


def far_place(row, far):
    second, third = row - 32, row - 64
    distance = jnp.where(row < 32, 1, jnp.where(row < 64, 2 + (second >> 4), 4 + (third >> 3)))
    line = jnp.where(row < 32, row >> 2, jnp.where(row < 64, (second >> 1) & 7, third & 7))
    index = jnp.where(row < 32, row & 3, jnp.where(row < 64, second & 1, 0))
    return ((far ^ distance) * LINE + line) * EACH + index


def far_choice(far, row_axis):
    shape = (PICKED, FAR * NEAR) if row_axis == 0 else (FAR * NEAR, PICKED)
    row = lax.broadcasted_iota(jnp.int32, shape, row_axis)
    return one_hot(far_place(row, far) == lax.broadcasted_iota(jnp.int32, shape, 1 - row_axis))


def table_kernel(offsets, queries, grad, to_order, to_token, query, choice, choice_back, grads_out):
    for slot in range(4):
        grads_out[slot] = grad[...]
    for head in range(LOCAL):
        order = order_from(offsets[head], 0)
        pairs = queries[head].astype(F32)
        to_order[head] = order
        to_token[head] = order_from(offsets[head], 1)
        query[head] = dot(order, beside(pairs, jnp.zeros_like(pairs))).astype(BF16)
    far = here()[0]
    choice[...] = far_choice(far, 0)
    choice_back[...] = far_choice(far, 1)


def far_kernel(ordered, line_in, far_out):
    low = lax.broadcasted_iota(jnp.int32, (8, LANES), 0) < EACH
    for pair in range(LINE // 2):
        first, second = (line_in[2 * pair + slot, 0:16, :].astype(F32)[:8] for slot in range(2))
        rows = jnp.where(low, first, pltpu.roll(second, EACH, 0)).astype(BF16)
        for slot in range(FAR):
            far_out[slot, pair * 8 : (pair + 1) * 8, :] = rows
    far_out[here()[0]] = ordered[NEAR : 2 * NEAR, :]


def main_kernel(
    to_order, to_token, query, choice, weight, grads, ordered, line_in, far_in, other_in, other_far_in, bias,
    output_keep, output_send, query_grad, send, keep_line, keep_far, keep_own, keep_weight,
    held, full_grad, attn, weight_term, parts,
):
    far, line, core, mine = here()
    held[0:ROWS, :] = ordered[...]
    held[PARTNER_AT:OTHER_AT, :] = other_far_in[far]
    held[FAR_AT:PARTNER_AT, :] = dot(choice[...], far_in[...].reshape(FAR * NEAR, LANES)).astype(BF16)
    held[OTHER_FAR_AT:, :] = dot(choice[...], other_far_in[...].reshape(FAR * NEAR, LANES)).astype(BF16)
    for step in range(LINE):
        slot = line ^ step
        if step:
            at = LINE_AT + (step - 1) * NEAR
            held[at : at + NEAR, :] = line_in[slot]
        at = OTHER_AT + step * NEAR
        held[at : at + NEAR, :] = other_in[slot]
    for parity in range(2):
        for half in range(2):
            place = (slice(parity * SIZE, (parity + 1) * SIZE), slice(half * HALF, (half + 1) * HALF))
            full_grad[place] = grads[2 * parity + half]
    heads = range(LOCAL)
    lanes = [pl.ds(head * 2 * SIZE, 2 * SIZE) for head in heads]
    grad = dot(full_grad[...], weight[...], NT).astype(BF16)
    zeros = jnp.zeros((ROWS, SIZE), BF16)
    grad = [jnp.concatenate([zeros, grad[:, head * SIZE : (head + 1) * SIZE]], axis=1) for head in heads]
    grad = [dot(to_order[head], grad[head]).astype(BF16) for head in heads]
    blocks = [jnp.concatenate([query[head], grad[head]], axis=0) for head in heads]
    products = [dot(held[:, lanes[head]], blocks[head], NT) for head in heads]
    scores = [products[head][:, :ROWS] * SCALE + bias[...] for head in heads]
    top = [jnp.max(scores[head], axis=0, keepdims=True) for head in heads]
    expd = [jnp.exp(scores[head] - top[head]) for head in heads]
    share = [1.0 / jnp.sum(expd[head], axis=0, keepdims=True) for head in heads]
    probs = [expd[head] * share[head] for head in heads]
    rounded = [probs[head].astype(BF16) for head in heads]
    attn_head = [dot(held[:, lanes[head]], rounded[head], TN)[SIZE:, :].astype(BF16) for head in heads]
    grad_side = [grad[head].astype(F32).T[SIZE:, :] for head in heads]
    delta = [jnp.sum(grad_side[head] * attn_head[head].astype(F32), axis=0, keepdims=True) for head in heads]
    dscore = [(probs[head] * (products[head][:, ROWS:] - delta[head]) * SCALE).astype(BF16) for head in heads]
    dquery = [dot(held[:, lanes[head]], dscore[head], TN)[:SIZE, :].astype(BF16) for head in heads]
    dboth = [dot(jnp.concatenate([dscore[head], rounded[head]], axis=1), blocks[head]) for head in heads]
    for head in heads:
        attn[:, head * SIZE : (head + 1) * SIZE] = dot(to_token[head], attn_head[head], NT).astype(BF16)
        by_token = dot(to_token[head], jnp.concatenate([dquery[head], jnp.zeros_like(dquery[head])], axis=0), NT)
        query_grad[head] = (by_token[:SIZE] + pltpu.roll(by_token[SIZE:], SIZE, 1)).astype(BF16)
        keep_own[:, lanes[head]] = dboth[head][0:ROWS]
        keep_far[:, lanes[head]] = dboth[head][FAR_AT:PARTNER_AT]
        send[SLOTS:SEND_FAR, lanes[head]] = dboth[head][PARTNER_AT:OTHER_AT].astype(BF16)
        send[SEND_FAR:SEND_WEIGHT, lanes[head]] = dboth[head][OTHER_FAR_AT:].astype(BF16)
        for step in range(LINE):
            slot = line ^ step
            at = LINE_AT + (step - 1) * NEAR
            keep_line[slot, :, lanes[head]] = dboth[head][at : at + NEAR] if step else jnp.zeros((NEAR, 2 * SIZE), F32)
            at = OTHER_AT + step * NEAR
            rows = pl.ds(pl.multiple_of(slot * NEAR, NEAR), NEAR)
            send[rows, lanes[head]] = dboth[head][at : at + NEAR].astype(BF16)
    part = dot(attn[...], weight[...])
    for parity in range(2):
        for half in range(2):
            piece = part[parity * SIZE : (parity + 1) * SIZE, half * HALF : (half + 1) * HALF]
            parts[2 * parity + half] = piece
    for step, way in ((0, 0), (1, 3)):
        output_keep[step] = parts[mine ^ way]
        output_send[step] = parts[mine ^ way ^ 1].astype(BF16)
    weight_term[...] = dot(attn[...], full_grad[...], TN)
    rows = SHARE // 2
    mine = pl.ds(pl.multiple_of(core * rows, 8), rows)
    theirs = pl.ds(pl.multiple_of((1 - core) * rows, 8), rows)
    for half in range(2):
        columns = pl.ds(half * HALF, HALF)
        keep_weight[half * rows : (half + 1) * rows, :] = weight_term[mine, columns]
        at = SEND_WEIGHT + half * rows
        send[at : at + rows, :] = weight_term[theirs, columns].astype(BF16)


def far_return_kernel(choice_back, received, keep_far, keep_weight, far_out):
    picked = (keep_far[...] + received[SEND_FAR:SEND_WEIGHT, :].astype(F32)).astype(BF16)
    rows = dot(choice_back[...], picked).astype(BF16)
    weight = (keep_weight[...] + received[SEND_WEIGHT:, :].astype(F32)).astype(BF16)
    for slot in range(FAR):
        far_out[slot, 0:NEAR, :] = rows[slot * NEAR : (slot + 1) * NEAR]
        far_out[slot, NEAR:, :] = weight[slot * PART : (slot + 1) * PART]


def line_return_kernel(received, keep_line, far_in, line_out):
    total = far_in[0].astype(F32)
    for slot in range(1, FAR):
        total = total + far_in[slot].astype(F32)
    low = lax.broadcasted_iota(jnp.int32, (8, LANES), 0) < EACH
    for slot in range(LINE):
        rows = keep_line[slot] + received[slot * NEAR : (slot + 1) * NEAR, :].astype(F32)
        both = total[slot // 2 * 8 : slot // 2 * 8 + 8]
        first = jnp.where(low, pltpu.roll(both, EACH, 0) if slot % 2 else both, 0.0)
        line_out[slot, 0:NEAR, :] = jnp.concatenate([rows[:8] + first, rows[8:]], axis=0).astype(BF16)
        line_out[slot, NEAR:, :] = total[NEAR:].astype(BF16)


def spread_kernel(line_in, near_sum, spread_out):
    total = line_in[0].astype(F32)
    for slot in range(1, LINE):
        total = total + line_in[slot].astype(F32)
    near_sum[...] = total[:NEAR]
    part = total[NEAR:].astype(BF16)
    for slot in range(FAR * CORE):
        spread_out[slot] = part


def finish_kernel(to_token, keep_own, received, near_sum, key_grad, value_grad, own):
    own[...] = keep_own[...]
    own[NEAR : 2 * NEAR, :] += received[SLOTS:SEND_FAR, :].astype(F32)
    own[0:NEAR, :] += near_sum[...]
    for head in range(LOCAL):
        both = own[:, head * 2 * SIZE : (head + 1) * 2 * SIZE].astype(BF16)
        both = dot(to_token[head], both)
        even, odd = both[:SIZE], both[SIZE:]
        low = lane_iota(even.shape) < SIZE
        key_grad[head] = jnp.where(low, even, pltpu.roll(odd, SIZE, 1)).astype(BF16)
        value_grad[head] = jnp.where(low, pltpu.roll(even, SIZE, 1), odd).astype(BF16)


def weight_kernel(spread_in, output_sum, second, weight_grad, output):
    output[...] = (output_sum[0] + second[...].astype(F32)).astype(BF16)
    for far in range(FAR):
        half, row = far // 4, far % 4 * PART
        for core in range(CORE):
            at = core * SHARE // 2 + row
            weight_grad[at : at + PART, half * HALF : (half + 1) * HALF] = spread_in[CORE * far + core].astype(F32)


def call(kernel, outs, args, scalars, scratch=(), space=pltpu.VMEM):
    return pl.pallas_call(
        kernel,
        out_shape=[jax.ShapeDtypeStruct(shape, dtype) for shape, dtype in outs],
        in_specs=[pl.BlockSpec(memory_space=pltpu.SMEM)] * scalars
        + [pl.BlockSpec(memory_space=space)] * (len(args) - scalars),
        out_specs=[pl.BlockSpec(memory_space=pltpu.VMEM)] * len(outs),
        scratch_shapes=list(scratch),
        compiler_params=pltpu.CompilerParams(vmem_limit_bytes=48 * 2**20),
    )(*args)


def start(offsets, keys, values):
    outs = [((ROWS, LANES), BF16), ((LINE, NEAR, LANES), BF16)]
    here = pltpu.VMEM((LOCAL, SIZE, 2 * SIZE), BF16)
    scratch = [pltpu.SMEM((LOCAL,), jnp.int32), here, here, pltpu.SemaphoreType.DMA((3,))]
    args = (pltpu.with_memory_space_constraint(array, pltpu.HBM) for array in (offsets, keys, values))
    return call(start_kernel, outs, tuple(args), 0, scratch, pltpu.HBM)


def tables(offsets, queries, grad):
    square = (LOCAL, ROWS, ROWS)
    outs = [(square, BF16)] * 3 + [((PICKED, FAR * NEAR), BF16), ((FAR * NEAR, PICKED), BF16)]
    return call(table_kernel, outs + [((4, SIZE, HALF), BF16)], (offsets, queries, grad), 1)


def far_pieces(ordered, line_in):
    return call(far_kernel, [((FAR, NEAR, LANES), BF16)], (ordered, line_in), 0)[0]


def attention(*arrays):
    outs = [
        ((2, SIZE, HALF), F32),
        ((2, SIZE, HALF), BF16),
        ((LOCAL, SIZE, 2 * SIZE), BF16),
        ((SEND, LANES), BF16),
        ((LINE, NEAR, LANES), F32),
        ((PICKED, LANES), F32),
        ((ROWS, LANES), F32),
        ((SHARE, HALF), F32),
    ]
    scratch = [
        pltpu.VMEM((KEYS, LANES), BF16),
        pltpu.VMEM((ROWS, WIDTH), BF16),
        pltpu.VMEM((ROWS, LOCAL * SIZE), BF16),
        pltpu.VMEM((SHARE, WIDTH), F32),
        pltpu.VMEM((4, SIZE, HALF), F32),
    ]
    return call(main_kernel, outs, arrays + (jnp.asarray(shared_levels()),), 0, scratch)


def far_return(choice_back, received, keep_far, keep_weight):
    args = (choice_back, received, keep_far, keep_weight)
    return call(far_return_kernel, [((FAR, NEAR + PART, LANES), BF16)], args, 0)[0]


def line_return(received, keep_line, far_in):
    return call(line_return_kernel, [((LINE, NEAR + PART, LANES), BF16)], (received, keep_line, far_in), 0)[0]


def spread_pieces(line_in):
    outs = [((NEAR, LANES), F32), ((FAR * CORE, PART, LANES), BF16)]
    return call(spread_kernel, outs, (line_in,), 0)


def finish(to_token, keep_own, received, near_sum):
    outs = [((LOCAL, SIZE, 2 * SIZE), BF16)] * 2
    return call(finish_kernel, outs, (to_token, keep_own, received, near_sum), 0, [pltpu.VMEM((ROWS, LANES), F32)])


def weight_rows(spread_in, output_sum, second):
    return call(weight_kernel, [((SHARE, WIDTH), F32), ((SIZE, HALF), BF16)], (spread_in, output_sum, second), 0)


def trade(pieces, groups):
    return lax.all_to_all(pieces, "seq", 0, 0, axis_index_groups=groups, tiled=True)


def swap_cores(block):
    return lax.ppermute(block, "seq", [(i, i ^ 1) for i in range(FAR * LINE * CORE)])


def swap_heads(block, way):
    return lax.ppermute(block, "head", [(i, i ^ way) for i in range(4)])


def shards(queries, keys, values, out_weight, offsets, out_grad):
    far_groups = [[far * 16 + low for far in range(FAR)] for low in range(16)]
    line_groups = [[far * 16 + line * 2 + core for line in range(LINE)] for far in range(FAR) for core in range(CORE)]
    side_groups = [[far * 16 + line * 2 + core for far in range(FAR) for core in range(CORE)] for line in range(LINE)]
    queries, keys, values = (array.transpose(1, 0, 2) for array in (queries, keys, values))
    ordered, line_out = start(offsets, keys, values)
    to_order, to_token, query, choice, choice_back, grads_out = tables(offsets, queries, out_grad)
    line_in = trade(line_out, line_groups)
    far_out = far_pieces(ordered, line_in)
    other_in = swap_cores(line_in)
    far_in = trade(far_out, far_groups)
    other_far_in = swap_cores(far_in)
    grads = lax.all_to_all(grads_out, "head", 0, 0, tiled=True)
    output_keep, output_send, query_grad, send, keep_line, keep_far, keep_own, keep_weight = attention(
        to_order, to_token, query, choice, out_weight, grads, ordered, line_in, far_in, other_in, other_far_in
    )
    first = swap_heads(output_send, 1)
    received = swap_cores(send)
    far_back = trade(far_return(choice_back, received, keep_far, keep_weight), far_groups)
    line_back = trade(line_return(received, keep_line, far_back), line_groups)
    line_back, first = lax.optimization_barrier((line_back, first))
    output_sum = output_keep + first.astype(F32)
    second = swap_heads(output_sum[1].astype(BF16), 3)
    near_sum, spread_out = spread_pieces(line_back)
    spread_in = trade(spread_out, side_groups)
    key_grad, value_grad = finish(to_token, keep_own, received, near_sum)
    weight_grad, output = weight_rows(spread_in, output_sum, second)
    query_grad, key_grad, value_grad = (grad.transpose(1, 0, 2) for grad in (query_grad, key_grad, value_grad))
    return (output, query_grad, key_grad, value_grad, weight_grad)


def solution(mesh):
    return jax.shard_map(
        shards,
        mesh=mesh,
        in_specs=(
            P("seq", "head", None),
            P("seq", "head", None),
            P("seq", "head", None),
            P("head", None),
            P("head"),
            P("seq", "head"),
        ),
        out_specs=(
            P("seq", "head"),
            P("seq", "head", None),
            P("seq", "head", None),
            P("seq", "head", None),
            P("head", None),
        ),
        check_vma=False,
    )
```

```python
import math

import jax
import jax.numpy as jnp
import numpy as np
from jax import lax
from jax.experimental import pallas as pl
from jax.experimental.pallas import tpu as pltpu
from jax.sharding import PartitionSpec as P

FAR, LINE, CORE = 8, 8, 2
FAR_FIRST, LINE_FIRST, HEAD_FIRST = 3, 7, 3
FAR_BACK, LINE_BACK, SPREAD_FIRST, SPREAD_CORE = 3, 7, 3, 1
ROWS = 128
LOCAL = 3
SIZE = 64
LANES = LOCAL * 2 * SIZE
WIDTH = 768
HALF = WIDTH // 2
SCALE = SIZE**-0.5
NEAR = 32
EACH = 4
PICKED = 96
SLOTS = LINE * NEAR
LINE_AT = ROWS
FAR_AT = LINE_AT + SLOTS - NEAR
PARTNER_AT = FAR_AT + PICKED
OTHER_AT = PARTNER_AT + NEAR
OTHER_FAR_AT = OTHER_AT + SLOTS
KEYS = OTHER_FAR_AT + PICKED
SHARE = 192
PART = SHARE // FAR
SEND_FAR = SLOTS + NEAR
SEND_WEIGHT = SEND_FAR + PICKED
SEND = SEND_WEIGHT + SHARE

NT = (((1,), (1,)), ((), ()))
TN = (((0,), (0,)), ((), ()))
NN = (((1,), (0,)), ((), ()))
BF16 = jnp.bfloat16
F32 = jnp.float32


def dot(a, b, dims=NN):
    return lax.dot_general(a, b, dims, preferred_element_type=F32)


def depth_of(row):
    return 7 if row == 0 else 7 - row.bit_length()


def far_table():
    table = [(1, row) for line in range(LINE) for row in range(4)]
    table += [(far, row) for far in (2, 3) for line in range(LINE) for row in range(2)]
    return table + [(far, 0) for far in range(4, 8) for line in range(LINE)]


def key_table():
    table = [(-1, depth_of(row)) for row in range(ROWS)]
    for core in range(CORE):
        if core:
            table += [(0, depth_of(NEAR + row)) for row in range(NEAR)]
        for line in range(1 - core, LINE):
            table += [(line.bit_length(), depth_of(row)) for row in range(NEAR)]
        table += [(3 + far.bit_length(), depth_of(row)) for far, row in far_table()]
    return table


def shared_levels():
    table = key_table()
    bias = np.full((KEYS, ROWS), -1e30, np.float32)
    for key, entry in enumerate(table):
        for query in range(ROWS):
            count = min(entry[1], depth_of(query)) - entry[0]
            if count > 0:
                bias[key, query] = math.log(count)
    return bias


def reversed_bits(row):
    out = row * 0
    for bit in range(7):
        out = out | ((row >> bit) & 1) << (6 - bit)
    return out


def token_of(row):
    return jnp.where(row < SIZE, 2 * row, 2 * row - (ROWS - 1))


def one_hot(match):
    return jnp.where(match, 1.0, 0.0).astype(BF16)


def here():
    index = lax.axis_index("seq")
    return (index >> 4) ^ FAR_FIRST, ((index >> 1) & 7) ^ LINE_FIRST, index & 1, lax.axis_index("head")


def order_from(offset, row_axis):
    row = lax.broadcasted_iota(jnp.int32, (ROWS, ROWS), row_axis)
    token = token_of(lax.broadcasted_iota(jnp.int32, (ROWS, ROWS), 1 - row_axis))
    return one_hot(((reversed_bits(row) + offset) & (ROWS - 1)) == token)


def lane_iota(shape):
    return lax.broadcasted_iota(jnp.int32, shape, len(shape) - 1)


def beside(first, second):
    low = lane_iota(first.shape) < SIZE
    even = jnp.where(low, first, pltpu.roll(second, SIZE, 1))
    odd = jnp.where(low, pltpu.roll(first, SIZE, 1), second)
    return jnp.concatenate([even, odd], axis=0).astype(BF16)


def start_kernel(offsets_far, keys, values, ordered, line_out, offsets, keys_here, values_here, done):
    copies = [
        pltpu.make_async_copy(source, target, done.at[at])
        for at, (source, target) in enumerate(((offsets_far, offsets), (keys, keys_here), (values, values_here)))
    ]
    for copy in copies:
        copy.start()
    copies[0].wait()
    orders = [order_from(offsets[head], 0) for head in range(LOCAL)]
    for copy in copies[1:]:
        copy.wait()
    for head in range(LOCAL):
        lanes = pl.ds(head * 2 * SIZE, 2 * SIZE)
        both = beside(keys_here[head].astype(F32), values_here[head].astype(F32))
        ordered[:, lanes] = dot(orders[head], both).astype(BF16)
    for slot in range(LINE):
        line_out[slot] = ordered[0:NEAR, :]


def far_place(row, far):
    second, third = row - 32, row - 64
    distance = jnp.where(row < 32, 1, jnp.where(row < 64, 2 + (second >> 4), 4 + (third >> 3)))
    line = jnp.where(row < 32, row >> 2, jnp.where(row < 64, (second >> 1) & 7, third & 7))
    index = jnp.where(row < 32, row & 3, jnp.where(row < 64, second & 1, 0))
    return ((far ^ distance) * LINE + line) * EACH + index


def far_choice(far, row_axis):
    shape = (PICKED, FAR * NEAR) if row_axis == 0 else (FAR * NEAR, PICKED)
    row = lax.broadcasted_iota(jnp.int32, shape, row_axis)
    return one_hot(far_place(row, far) == lax.broadcasted_iota(jnp.int32, shape, 1 - row_axis))


def table_kernel(offsets, queries, grad, to_order, to_token, query, choice, choice_back, grads_out):
    for slot in range(4):
        grads_out[slot] = grad[...]
    for head in range(LOCAL):
        order = order_from(offsets[head], 0)
        pairs = queries[head].astype(F32)
        to_order[head] = order
        to_token[head] = order_from(offsets[head], 1)
        query[head] = (dot(order, beside(pairs, jnp.zeros_like(pairs))) * SCALE).astype(BF16)
    far = here()[0]
    choice[...] = far_choice(far, 0)
    choice_back[...] = far_choice(far ^ FAR_FIRST ^ FAR_BACK, 1)


def far_kernel(ordered, line_in, far_out):
    low = lax.broadcasted_iota(jnp.int32, (8, LANES), 0) < EACH
    for pair in range(LINE // 2):
        first, second = (line_in[2 * pair + slot, 0:16, :].astype(F32)[:8] for slot in range(2))
        rows = jnp.where(low, first, pltpu.roll(second, EACH, 0)).astype(BF16)
        for slot in range(FAR):
            far_out[slot, pair * 8 : (pair + 1) * 8, :] = rows
    far_out[here()[0]] = ordered[NEAR : 2 * NEAR, :]


def main_kernel(
    to_order, to_token, query, choice, weight, grads, ordered, line_in, far_in, other_in, other_far_in, bias,
    output_keep, output_send, query_grad, send, keep_line, keep_far, keep_own, keep_weight,
    held, full_grad, attn, weight_term, parts,
):
    far, line, core, mine = here()
    held[0:ROWS, :] = ordered[...]
    held[PARTNER_AT:OTHER_AT, :] = other_far_in[far]
    held[FAR_AT:PARTNER_AT, :] = dot(choice[...], far_in[...].reshape(FAR * NEAR, LANES)).astype(BF16)
    held[OTHER_FAR_AT:, :] = dot(choice[...], other_far_in[...].reshape(FAR * NEAR, LANES)).astype(BF16)
    for step in range(LINE):
        slot = line ^ step
        if step:
            at = LINE_AT + (step - 1) * NEAR
            held[at : at + NEAR, :] = line_in[slot]
        at = OTHER_AT + step * NEAR
        held[at : at + NEAR, :] = other_in[slot]
    for parity in range(2):
        for half in range(2):
            place = (slice(parity * SIZE, (parity + 1) * SIZE), slice(half * HALF, (half + 1) * HALF))
            full_grad[place] = grads[HEAD_FIRST ^ (2 * parity + half)]
    heads = range(LOCAL)
    lanes = [pl.ds(head * 2 * SIZE, 2 * SIZE) for head in heads]
    grad = dot(full_grad[...], weight[...], NT).astype(BF16)
    zeros = jnp.zeros((ROWS, SIZE), BF16)
    grad = [jnp.concatenate([zeros, grad[:, head * SIZE : (head + 1) * SIZE]], axis=1) for head in heads]
    grad = [dot(to_order[head], grad[head]).astype(BF16) for head in heads]
    blocks = [jnp.concatenate([query[head], grad[head]], axis=0) for head in heads]
    sides = [held[:, lanes[head]].T for head in heads]
    scores = [dot(held[:, lanes[head]], query[head], NT) + bias[...] for head in heads]
    top = [jnp.max(scores[head], axis=0, keepdims=True) for head in heads]
    expd = [jnp.exp(scores[head] - top[head]) for head in heads]
    share = [1.0 / jnp.sum(expd[head], axis=0, keepdims=True) for head in heads]
    probs = [expd[head] * share[head] for head in heads]
    rounded = [probs[head].astype(BF16) for head in heads]
    attn_head = [dot(sides[head][SIZE:], rounded[head]).astype(BF16) for head in heads]
    grad_side = [grad[head].astype(F32).T[SIZE:, :] for head in heads]
    delta = [jnp.sum(grad_side[head] * attn_head[head].astype(F32), axis=0, keepdims=True) for head in heads]
    dprob = [dot(held[:, lanes[head]], grad[head], NT) for head in heads]
    dscore = [(probs[head] * (dprob[head] - delta[head])).astype(BF16) for head in heads]
    dquery = [(dot(sides[head][:SIZE], dscore[head]) * SCALE).astype(BF16) for head in heads]
    dboth = [dot(jnp.concatenate([dscore[head], rounded[head]], axis=1), blocks[head]) for head in heads]
    for head in heads:
        attn[:, head * SIZE : (head + 1) * SIZE] = dot(to_token[head], attn_head[head], NT).astype(BF16)
        by_token = dot(to_token[head], jnp.concatenate([dquery[head], jnp.zeros_like(dquery[head])], axis=0), NT)
        query_grad[head] = (by_token[:SIZE] + pltpu.roll(by_token[SIZE:], SIZE, 1)).astype(BF16)
        keep_own[:, lanes[head]] = dboth[head][0:ROWS]
        keep_far[:, lanes[head]] = dboth[head][FAR_AT:PARTNER_AT]
        send[SLOTS:SEND_FAR, lanes[head]] = dboth[head][PARTNER_AT:OTHER_AT].astype(BF16)
        send[SEND_FAR:SEND_WEIGHT, lanes[head]] = dboth[head][OTHER_FAR_AT:].astype(BF16)
        for step in range(LINE):
            slot = line ^ step
            at = LINE_AT + (step - 1) * NEAR
            keep_line[slot, :, lanes[head]] = dboth[head][at : at + NEAR] if step else jnp.zeros((NEAR, 2 * SIZE), F32)
            at = OTHER_AT + step * NEAR
            rows = pl.ds(pl.multiple_of(slot * NEAR, NEAR), NEAR)
            send[rows, lanes[head]] = dboth[head][at : at + NEAR].astype(BF16)
    part = dot(attn[...], weight[...])
    for parity in range(2):
        for half in range(2):
            piece = part[parity * SIZE : (parity + 1) * SIZE, half * HALF : (half + 1) * HALF]
            parts[2 * parity + half] = piece
    for step, way in ((0, 0), (1, 3)):
        output_keep[step] = parts[mine ^ way]
        output_send[step] = parts[mine ^ way ^ 1].astype(BF16)
    weight_term[...] = dot(attn[...], full_grad[...], TN)
    rows = SHARE // 2
    mine = pl.ds(pl.multiple_of(core * rows, 8), rows)
    theirs = pl.ds(pl.multiple_of((1 - core) * rows, 8), rows)
    for half in range(2):
        columns = pl.ds(half * HALF, HALF)
        keep_weight[half * rows : (half + 1) * rows, :] = weight_term[mine, columns]
        at = SEND_WEIGHT + half * rows
        send[at : at + rows, :] = weight_term[theirs, columns].astype(BF16)


def far_return_kernel(choice_back, received, keep_far, keep_weight, far_out):
    picked = (keep_far[...] + received[SEND_FAR:SEND_WEIGHT, :].astype(F32)).astype(BF16)
    rows = dot(choice_back[...], picked).astype(BF16)
    weight = (keep_weight[...] + received[SEND_WEIGHT:, :].astype(F32)).astype(BF16)
    for slot in range(FAR):
        far_out[slot, 0:NEAR, :] = rows[slot * NEAR : (slot + 1) * NEAR]
        far_out[slot, NEAR:, :] = weight[slot * PART : (slot + 1) * PART]


def line_return_kernel(received, keep_line, far_in, line_out):
    total = far_in[0].astype(F32)
    for slot in range(1, FAR):
        total = total + far_in[slot].astype(F32)
    low = lax.broadcasted_iota(jnp.int32, (8, LANES), 0) < EACH
    for slot in range(LINE):
        rows = keep_line[slot] + received[slot * NEAR : (slot + 1) * NEAR, :].astype(F32)
        both = total[slot // 2 * 8 : slot // 2 * 8 + 8]
        first = jnp.where(low, pltpu.roll(both, EACH, 0) if slot % 2 else both, 0.0)
        back = slot ^ LINE_FIRST ^ LINE_BACK
        line_out[back, 0:NEAR, :] = jnp.concatenate([rows[:8] + first, rows[8:]], axis=0).astype(BF16)
        line_out[back, NEAR:, :] = total[NEAR:].astype(BF16)


def spread_kernel(line_in, output_keep, first, near_sum, spread_out, output_sum, second_out):
    output_sum[...] = output_keep[0] + first[0].astype(F32)
    second_out[...] = (output_keep[1] + first[1].astype(F32)).astype(BF16)
    total = line_in[0].astype(F32)
    for slot in range(1, LINE):
        total = total + line_in[slot].astype(F32)
    near_sum[...] = total[:NEAR]
    part = total[NEAR:].astype(BF16)
    for slot in range(FAR * CORE):
        spread_out[slot] = part


def finish_kernel(to_token, keep_own, received, near_sum, key_grad, value_grad, own):
    own[...] = keep_own[...]
    own[NEAR : 2 * NEAR, :] += received[SLOTS:SEND_FAR, :].astype(F32)
    own[0:NEAR, :] += near_sum[...]
    for head in range(LOCAL):
        both = own[:, head * 2 * SIZE : (head + 1) * 2 * SIZE].astype(BF16)
        both = dot(to_token[head], both)
        even, odd = both[:SIZE], both[SIZE:]
        low = lane_iota(even.shape) < SIZE
        key_grad[head] = jnp.where(low, even, pltpu.roll(odd, SIZE, 1)).astype(BF16)
        value_grad[head] = jnp.where(low, pltpu.roll(even, SIZE, 1), odd).astype(BF16)


def weight_kernel(spread_in, output_sum, second, weight_grad, output):
    output[...] = (output_sum[...] + second[...].astype(F32)).astype(BF16)
    for share in range(FAR):
        half, row = share // 4, share % 4 * PART
        for core in range(CORE):
            at = core * SHARE // 2 + row
            slot = CORE * (share ^ FAR_BACK ^ SPREAD_FIRST) + (core ^ SPREAD_CORE)
            weight_grad[at : at + PART, half * HALF : (half + 1) * HALF] = spread_in[slot].astype(F32)


def call(kernel, outs, args, scalars, scratch=(), space=pltpu.VMEM):
    return pl.pallas_call(
        kernel,
        out_shape=[jax.ShapeDtypeStruct(shape, dtype) for shape, dtype in outs],
        in_specs=[pl.BlockSpec(memory_space=pltpu.SMEM)] * scalars
        + [pl.BlockSpec(memory_space=space)] * (len(args) - scalars),
        out_specs=[pl.BlockSpec(memory_space=pltpu.VMEM)] * len(outs),
        scratch_shapes=list(scratch),
        compiler_params=pltpu.CompilerParams(vmem_limit_bytes=48 * 2**20),
    )(*args)


def start(offsets, keys, values):
    outs = [((ROWS, LANES), BF16), ((LINE, NEAR, LANES), BF16)]
    here = pltpu.VMEM((LOCAL, SIZE, 2 * SIZE), BF16)
    scratch = [pltpu.SMEM((LOCAL,), jnp.int32), here, here, pltpu.SemaphoreType.DMA((3,))]
    args = (pltpu.with_memory_space_constraint(array, pltpu.HBM) for array in (offsets, keys, values))
    return call(start_kernel, outs, tuple(args), 0, scratch, pltpu.HBM)


def tables(offsets, queries, grad):
    square = (LOCAL, ROWS, ROWS)
    outs = [(square, BF16)] * 3 + [((PICKED, FAR * NEAR), BF16), ((FAR * NEAR, PICKED), BF16)]
    return call(table_kernel, outs + [((4, SIZE, HALF), BF16)], (offsets, queries, grad), 1)


def far_pieces(ordered, line_in):
    return call(far_kernel, [((FAR, NEAR, LANES), BF16)], (ordered, line_in), 0)[0]


def attention(*arrays):
    outs = [
        ((2, SIZE, HALF), F32),
        ((2, SIZE, HALF), BF16),
        ((LOCAL, SIZE, 2 * SIZE), BF16),
        ((SEND, LANES), BF16),
        ((LINE, NEAR, LANES), F32),
        ((PICKED, LANES), F32),
        ((ROWS, LANES), F32),
        ((SHARE, HALF), F32),
    ]
    scratch = [
        pltpu.VMEM((KEYS, LANES), BF16),
        pltpu.VMEM((ROWS, WIDTH), BF16),
        pltpu.VMEM((ROWS, LOCAL * SIZE), BF16),
        pltpu.VMEM((SHARE, WIDTH), F32),
        pltpu.VMEM((4, SIZE, HALF), F32),
    ]
    return call(main_kernel, outs, arrays + (jnp.asarray(shared_levels()),), 0, scratch)


def far_return(choice_back, received, keep_far, keep_weight):
    args = (choice_back, received, keep_far, keep_weight)
    return call(far_return_kernel, [((FAR, NEAR + PART, LANES), BF16)], args, 0)[0]


def line_return(received, keep_line, far_in):
    return call(line_return_kernel, [((LINE, NEAR + PART, LANES), BF16)], (received, keep_line, far_in), 0)[0]


def spread_pieces(line_in, output_keep, first):
    outs = [((NEAR, LANES), F32), ((FAR * CORE, PART, LANES), BF16), ((SIZE, HALF), F32), ((SIZE, HALF), BF16)]
    return call(spread_kernel, outs, (line_in, output_keep, first), 0)


def finish(to_token, keep_own, received, near_sum):
    outs = [((LOCAL, SIZE, 2 * SIZE), BF16)] * 2
    return call(finish_kernel, outs, (to_token, keep_own, received, near_sum), 0, [pltpu.VMEM((ROWS, LANES), F32)])


def weight_rows(spread_in, output_sum, second):
    return call(weight_kernel, [((SHARE, WIDTH), F32), ((SIZE, HALF), BF16)], (spread_in, output_sum, second), 0)


def trade(pieces, groups):
    return lax.all_to_all(pieces, "seq", 0, 0, axis_index_groups=groups, tiled=True)


def swap_cores(block):
    return lax.ppermute(block, "seq", [(i, i ^ 1) for i in range(FAR * LINE * CORE)])


def swap_heads(block, way):
    return lax.ppermute(block, "head", [(i, i ^ way) for i in range(4)])


def shards(queries, keys, values, out_weight, offsets, out_grad):
    head_group = [HEAD_FIRST ^ slot for slot in range(4)]
    far_groups, far_back_groups = (
        [[(first ^ slot) * 16 + low for slot in range(FAR)] for low in range(16)] for first in (FAR_FIRST, FAR_BACK)
    )
    line_groups, line_back_groups = (
        [[far * 16 + (first ^ slot) * 2 + core for slot in range(LINE)] for far in range(FAR) for core in range(CORE)]
        for first in (LINE_FIRST, LINE_BACK)
    )
    spread_groups = [
        [(SPREAD_FIRST ^ slot) * 16 + line * 2 + (SPREAD_CORE ^ core) for slot in range(FAR) for core in range(CORE)]
        for line in range(LINE)
    ]
    queries, keys, values = (array.transpose(1, 0, 2) for array in (queries, keys, values))
    ordered, line_out = start(offsets, keys, values)
    to_order, to_token, query, choice, choice_back, grads_out = tables(offsets, queries, out_grad)
    line_in = trade(line_out, line_groups)
    far_out = far_pieces(ordered, line_in)
    other_in = swap_cores(line_in)
    far_in = trade(far_out, far_groups)
    other_far_in = swap_cores(far_in)
    grads = lax.all_to_all(grads_out, "head", 0, 0, axis_index_groups=[head_group], tiled=True)
    output_keep, output_send, query_grad, send, keep_line, keep_far, keep_own, keep_weight = attention(
        to_order, to_token, query, choice, out_weight, grads, ordered, line_in, far_in, other_in, other_far_in
    )
    first = swap_heads(output_send, 1)
    received = swap_cores(send)
    far_back = trade(far_return(choice_back, received, keep_far, keep_weight), far_back_groups)
    line_back = trade(line_return(received, keep_line, far_back), line_back_groups)
    near_sum, spread_out, output_sum, second_out = spread_pieces(line_back, output_keep, first)
    second = swap_heads(second_out, 3)
    spread_in = trade(spread_out, spread_groups)
    key_grad, value_grad = finish(to_token, keep_own, received, near_sum)
    weight_grad, output = weight_rows(spread_in, output_sum, second)
    query_grad, key_grad, value_grad = (grad.transpose(1, 0, 2) for grad in (query_grad, key_grad, value_grad))
    return (output, query_grad, key_grad, value_grad, weight_grad)


def solution(mesh):
    return jax.shard_map(
        shards,
        mesh=mesh,
        in_specs=(
            P("seq", "head", None),
            P("seq", "head", None),
            P("seq", "head", None),
            P("head", None),
            P("head"),
            P("seq", "head"),
        ),
        out_specs=(
            P("seq", "head"),
            P("seq", "head", None),
            P("seq", "head", None),
            P("seq", "head", None),
            P("head", None),
        ),
        check_vma=False,
    )
```

```python
import math

import jax
import jax.numpy as jnp
import numpy as np
from jax import lax
from jax.experimental import pallas as pl
from jax.experimental.pallas import tpu as pltpu
from jax.sharding import PartitionSpec as P

FAR, LINE, CORE = 8, 8, 2
FAR_FIRST, LINE_FIRST, HEAD_FIRST = 3, 6, 3
FAR_BACK, LINE_BACK, SPREAD_FIRST, SPREAD_CORE = 3, 7, 2, 1
ROWS = 128
LOCAL = 3
SIZE = 64
LANES = LOCAL * 2 * SIZE
WIDTH = 768
HALF = WIDTH // 2
SCALE = SIZE**-0.5
NEAR = 32
EACH = 4
PICKED = 96
SLOTS = LINE * NEAR
LINE_AT = ROWS
FAR_AT = LINE_AT + SLOTS - NEAR
PARTNER_AT = FAR_AT + PICKED
OTHER_AT = PARTNER_AT + NEAR
OTHER_FAR_AT = OTHER_AT + SLOTS
KEYS = OTHER_FAR_AT + PICKED
SHARE = 192
PART = SHARE // FAR
SEND_FAR = SLOTS + NEAR
SEND_WEIGHT = SEND_FAR + PICKED
SEND = SEND_WEIGHT + SHARE

NT = (((1,), (1,)), ((), ()))
TN = (((0,), (0,)), ((), ()))
NN = (((1,), (0,)), ((), ()))
BF16 = jnp.bfloat16
F32 = jnp.float32


def dot(a, b, dims=NN):
    return lax.dot_general(a, b, dims, preferred_element_type=F32)


def depth_of(row):
    return 7 if row == 0 else 7 - row.bit_length()


def far_table():
    table = [(1, row) for line in range(LINE) for row in range(4)]
    table += [(far, row) for far in (2, 3) for line in range(LINE) for row in range(2)]
    return table + [(far, 0) for far in range(4, 8) for line in range(LINE)]


def key_table():
    table = [(-1, depth_of(row)) for row in range(ROWS)]
    for core in range(CORE):
        if core:
            table += [(0, depth_of(NEAR + row)) for row in range(NEAR)]
        for line in range(1 - core, LINE):
            table += [(line.bit_length(), depth_of(row)) for row in range(NEAR)]
        table += [(3 + far.bit_length(), depth_of(row)) for far, row in far_table()]
    return table


def shared_levels():
    table = key_table()
    bias = np.full((KEYS, ROWS), -1e30, np.float32)
    for key, entry in enumerate(table):
        for query in range(ROWS):
            count = min(entry[1], depth_of(query)) - entry[0]
            if count > 0:
                bias[key, query] = math.log(count)
    return bias


def reversed_bits(row):
    out = row * 0
    for bit in range(7):
        out = out | ((row >> bit) & 1) << (6 - bit)
    return out


def token_of(row):
    return jnp.where(row < SIZE, 2 * row, 2 * row - (ROWS - 1))


def one_hot(match):
    return jnp.where(match, 1.0, 0.0).astype(BF16)


def here():
    index = lax.axis_index("seq")
    return (index >> 4) ^ FAR_FIRST, ((index >> 1) & 7) ^ LINE_FIRST, index & 1, lax.axis_index("head")


def order_from(offset, row_axis):
    row = lax.broadcasted_iota(jnp.int32, (ROWS, ROWS), row_axis)
    token = token_of(lax.broadcasted_iota(jnp.int32, (ROWS, ROWS), 1 - row_axis))
    return one_hot(((reversed_bits(row) + offset) & (ROWS - 1)) == token)


def lane_iota(shape):
    return lax.broadcasted_iota(jnp.int32, shape, len(shape) - 1)


def beside(first, second):
    low = lane_iota(first.shape) < SIZE
    even = jnp.where(low, first, pltpu.roll(second, SIZE, 1))
    odd = jnp.where(low, pltpu.roll(first, SIZE, 1), second)
    return jnp.concatenate([even, odd], axis=0).astype(BF16)


def start_kernel(offsets_far, keys, values, ordered, line_out, offsets, keys_here, values_here, done):
    copies = [
        pltpu.make_async_copy(source, target, done.at[at])
        for at, (source, target) in enumerate(((offsets_far, offsets), (keys, keys_here), (values, values_here)))
    ]
    for copy in copies:
        copy.start()
    copies[0].wait()
    orders = [order_from(offsets[head], 0) for head in range(LOCAL)]
    for copy in copies[1:]:
        copy.wait()
    for head in range(LOCAL):
        lanes = pl.ds(head * 2 * SIZE, 2 * SIZE)
        both = beside(keys_here[head].astype(F32), values_here[head].astype(F32))
        ordered[:, lanes] = dot(orders[head], both).astype(BF16)
    for slot in range(LINE):
        line_out[slot] = ordered[0:NEAR, :]


def far_place(row, far):
    second, third = row - 32, row - 64
    distance = jnp.where(row < 32, 1, jnp.where(row < 64, 2 + (second >> 4), 4 + (third >> 3)))
    line = jnp.where(row < 32, row >> 2, jnp.where(row < 64, (second >> 1) & 7, third & 7))
    index = jnp.where(row < 32, row & 3, jnp.where(row < 64, second & 1, 0))
    return ((far ^ distance) * LINE + line) * EACH + index


def far_choice(far, row_axis):
    shape = (PICKED, FAR * NEAR) if row_axis == 0 else (FAR * NEAR, PICKED)
    row = lax.broadcasted_iota(jnp.int32, shape, row_axis)
    return one_hot(far_place(row, far) == lax.broadcasted_iota(jnp.int32, shape, 1 - row_axis))


def table_kernel(offsets, queries, grad, to_order, to_token, query, choice, choice_back, grads_out):
    for slot in range(4):
        grads_out[slot] = grad[...]
    for head in range(LOCAL):
        order = order_from(offsets[head], 0)
        pairs = queries[head].astype(F32)
        to_order[head] = order
        to_token[head] = order_from(offsets[head], 1)
        query[head] = (dot(order, beside(pairs, jnp.zeros_like(pairs))) * SCALE).astype(BF16)
    far = here()[0]
    choice[...] = far_choice(far, 0)
    choice_back[...] = far_choice(far ^ FAR_FIRST ^ FAR_BACK, 1)


def far_kernel(ordered, line_in, far_out):
    low = lax.broadcasted_iota(jnp.int32, (8, LANES), 0) < EACH
    for pair in range(LINE // 2):
        first, second = (line_in[2 * pair + slot, 0:16, :].astype(F32)[:8] for slot in range(2))
        rows = jnp.where(low, first, pltpu.roll(second, EACH, 0)).astype(BF16)
        for slot in range(FAR):
            far_out[slot, pair * 8 : (pair + 1) * 8, :] = rows
    far_out[here()[0]] = ordered[NEAR : 2 * NEAR, :]


def main_kernel(
    to_order, to_token, query, choice, weight, grads, ordered, line_in, far_in, other_in, other_far_in, bias,
    output_keep, output_send, query_grad, send, keep_line, keep_far, keep_own, keep_weight,
    held, full_grad, attn, weight_term, parts,
):
    far, line, core, mine = here()
    held[0:ROWS, :] = ordered[...]
    held[PARTNER_AT:OTHER_AT, :] = other_far_in[far]
    held[FAR_AT:PARTNER_AT, :] = dot(choice[...], far_in[...].reshape(FAR * NEAR, LANES)).astype(BF16)
    held[OTHER_FAR_AT:, :] = dot(choice[...], other_far_in[...].reshape(FAR * NEAR, LANES)).astype(BF16)
    for step in range(LINE):
        slot = line ^ step
        if step:
            at = LINE_AT + (step - 1) * NEAR
            held[at : at + NEAR, :] = line_in[slot]
        at = OTHER_AT + step * NEAR
        held[at : at + NEAR, :] = other_in[slot]
    for parity in range(2):
        for half in range(2):
            place = (slice(parity * SIZE, (parity + 1) * SIZE), slice(half * HALF, (half + 1) * HALF))
            full_grad[place] = grads[HEAD_FIRST ^ (2 * parity + half)]
    heads = range(LOCAL)
    lanes = [pl.ds(head * 2 * SIZE, 2 * SIZE) for head in heads]
    grad = dot(full_grad[...], weight[...], NT).astype(BF16)
    zeros = jnp.zeros((ROWS, SIZE), BF16)
    grad = [jnp.concatenate([zeros, grad[:, head * SIZE : (head + 1) * SIZE]], axis=1) for head in heads]
    grad = [dot(to_order[head], grad[head]).astype(BF16) for head in heads]
    blocks = [jnp.concatenate([query[head], grad[head]], axis=0) for head in heads]
    sides = [held[:, lanes[head]].T for head in heads]
    scores = [dot(held[:, lanes[head]], query[head], NT) + bias[...] for head in heads]
    top = [jnp.max(scores[head], axis=0, keepdims=True) for head in heads]
    expd = [jnp.exp(scores[head] - top[head]) for head in heads]
    share = [1.0 / jnp.sum(expd[head], axis=0, keepdims=True) for head in heads]
    probs = [expd[head] * share[head] for head in heads]
    rounded = [probs[head].astype(BF16) for head in heads]
    attn_head = [dot(sides[head][SIZE:], rounded[head]).astype(BF16) for head in heads]
    grad_side = [grad[head].astype(F32).T[SIZE:, :] for head in heads]
    delta = [jnp.sum(grad_side[head] * attn_head[head].astype(F32), axis=0, keepdims=True) for head in heads]
    dprob = [dot(held[:, lanes[head]], grad[head], NT) for head in heads]
    dscore = [(probs[head] * (dprob[head] - delta[head])).astype(BF16) for head in heads]
    dquery = [(dot(sides[head][:SIZE], dscore[head]) * SCALE).astype(BF16) for head in heads]
    dboth = [dot(jnp.concatenate([dscore[head], rounded[head]], axis=1), blocks[head]) for head in heads]
    for head in heads:
        attn[:, head * SIZE : (head + 1) * SIZE] = dot(to_token[head], attn_head[head], NT).astype(BF16)
        by_token = dot(to_token[head], jnp.concatenate([dquery[head], jnp.zeros_like(dquery[head])], axis=0), NT)
        query_grad[head] = (by_token[:SIZE] + pltpu.roll(by_token[SIZE:], SIZE, 1)).astype(BF16)
        keep_own[:, lanes[head]] = dboth[head][0:ROWS]
        keep_far[:, lanes[head]] = dboth[head][FAR_AT:PARTNER_AT]
        send[SLOTS:SEND_FAR, lanes[head]] = dboth[head][PARTNER_AT:OTHER_AT].astype(BF16)
        send[SEND_FAR:SEND_WEIGHT, lanes[head]] = dboth[head][OTHER_FAR_AT:].astype(BF16)
        for step in range(LINE):
            slot = line ^ step
            at = LINE_AT + (step - 1) * NEAR
            keep_line[slot, :, lanes[head]] = dboth[head][at : at + NEAR] if step else jnp.zeros((NEAR, 2 * SIZE), F32)
            at = OTHER_AT + step * NEAR
            rows = pl.ds(pl.multiple_of(slot * NEAR, NEAR), NEAR)
            send[rows, lanes[head]] = dboth[head][at : at + NEAR].astype(BF16)
    part = dot(attn[...], weight[...])
    for parity in range(2):
        for half in range(2):
            piece = part[parity * SIZE : (parity + 1) * SIZE, half * HALF : (half + 1) * HALF]
            parts[2 * parity + half] = piece
    for step, way in ((0, 0), (1, 3)):
        output_keep[step] = parts[mine ^ way]
        output_send[step] = parts[mine ^ way ^ 1].astype(BF16)
    weight_term[...] = dot(attn[...], full_grad[...], TN)
    rows = SHARE // 2
    mine = pl.ds(pl.multiple_of(core * rows, 8), rows)
    theirs = pl.ds(pl.multiple_of((1 - core) * rows, 8), rows)
    for half in range(2):
        columns = pl.ds(half * HALF, HALF)
        keep_weight[half * rows : (half + 1) * rows, :] = weight_term[mine, columns]
        at = SEND_WEIGHT + half * rows
        send[at : at + rows, :] = weight_term[theirs, columns].astype(BF16)


def far_return_kernel(choice_back, received, keep_far, keep_weight, far_out):
    picked = (keep_far[...] + received[SEND_FAR:SEND_WEIGHT, :].astype(F32)).astype(BF16)
    rows = dot(choice_back[...], picked).astype(BF16)
    weight = (keep_weight[...] + received[SEND_WEIGHT:, :].astype(F32)).astype(BF16)
    for slot in range(FAR):
        far_out[slot, 0:NEAR, :] = rows[slot * NEAR : (slot + 1) * NEAR]
        far_out[slot, NEAR:, :] = weight[slot * PART : (slot + 1) * PART]


def line_return_kernel(received, keep_line, far_in, line_out):
    total = far_in[0].astype(F32)
    for slot in range(1, FAR):
        total = total + far_in[slot].astype(F32)
    low = lax.broadcasted_iota(jnp.int32, (8, LANES), 0) < EACH
    for slot in range(LINE):
        rows = keep_line[slot] + received[slot * NEAR : (slot + 1) * NEAR, :].astype(F32)
        both = total[slot // 2 * 8 : slot // 2 * 8 + 8]
        first = jnp.where(low, pltpu.roll(both, EACH, 0) if slot % 2 else both, 0.0)
        back = slot ^ LINE_FIRST ^ LINE_BACK
        line_out[back, 0:NEAR, :] = jnp.concatenate([rows[:8] + first, rows[8:]], axis=0).astype(BF16)
        line_out[back, NEAR:, :] = total[NEAR:].astype(BF16)


def spread_kernel(line_in, output_keep, first, near_sum, spread_out, output_sum, second_out):
    output_sum[...] = output_keep[0] + first[0].astype(F32)
    second_out[...] = (output_keep[1] + first[1].astype(F32)).astype(BF16)
    total = line_in[0].astype(F32)
    for slot in range(1, LINE):
        total = total + line_in[slot].astype(F32)
    near_sum[...] = total[:NEAR]
    part = total[NEAR:].astype(BF16)
    for slot in range(FAR * CORE):
        spread_out[slot] = part


def finish_kernel(to_token, keep_own, received, near_sum, key_grad, value_grad, own):
    own[...] = keep_own[...]
    own[NEAR : 2 * NEAR, :] += received[SLOTS:SEND_FAR, :].astype(F32)
    own[0:NEAR, :] += near_sum[...]
    for head in range(LOCAL):
        both = own[:, head * 2 * SIZE : (head + 1) * 2 * SIZE].astype(BF16)
        both = dot(to_token[head], both)
        even, odd = both[:SIZE], both[SIZE:]
        low = lane_iota(even.shape) < SIZE
        key_grad[head] = jnp.where(low, even, pltpu.roll(odd, SIZE, 1)).astype(BF16)
        value_grad[head] = jnp.where(low, pltpu.roll(even, SIZE, 1), odd).astype(BF16)


def weight_kernel(spread_in, output_sum, second, weight_grad, output):
    output[...] = (output_sum[...] + second[...].astype(F32)).astype(BF16)
    for share in range(FAR):
        half, row = share // 4, share % 4 * PART
        for core in range(CORE):
            at = core * SHARE // 2 + row
            slot = CORE * (share ^ FAR_BACK ^ SPREAD_FIRST) + (core ^ SPREAD_CORE)
            weight_grad[at : at + PART, half * HALF : (half + 1) * HALF] = spread_in[slot].astype(F32)


def call(kernel, outs, args, scalars, scratch=(), space=pltpu.VMEM):
    return pl.pallas_call(
        kernel,
        out_shape=[jax.ShapeDtypeStruct(shape, dtype) for shape, dtype in outs],
        in_specs=[pl.BlockSpec(memory_space=pltpu.SMEM)] * scalars
        + [pl.BlockSpec(memory_space=space)] * (len(args) - scalars),
        out_specs=[pl.BlockSpec(memory_space=pltpu.VMEM)] * len(outs),
        scratch_shapes=list(scratch),
        compiler_params=pltpu.CompilerParams(vmem_limit_bytes=48 * 2**20),
    )(*args)


def start(offsets, keys, values):
    outs = [((ROWS, LANES), BF16), ((LINE, NEAR, LANES), BF16)]
    here = pltpu.VMEM((LOCAL, SIZE, 2 * SIZE), BF16)
    scratch = [pltpu.SMEM((LOCAL,), jnp.int32), here, here, pltpu.SemaphoreType.DMA((3,))]
    args = (pltpu.with_memory_space_constraint(array, pltpu.HBM) for array in (offsets, keys, values))
    return call(start_kernel, outs, tuple(args), 0, scratch, pltpu.HBM)


def tables(offsets, queries, grad):
    square = (LOCAL, ROWS, ROWS)
    outs = [(square, BF16)] * 3 + [((PICKED, FAR * NEAR), BF16), ((FAR * NEAR, PICKED), BF16)]
    return call(table_kernel, outs + [((4, SIZE, HALF), BF16)], (offsets, queries, grad), 1)


def far_pieces(ordered, line_in):
    return call(far_kernel, [((FAR, NEAR, LANES), BF16)], (ordered, line_in), 0)[0]


def attention(*arrays):
    outs = [
        ((2, SIZE, HALF), F32),
        ((2, SIZE, HALF), BF16),
        ((LOCAL, SIZE, 2 * SIZE), BF16),
        ((SEND, LANES), BF16),
        ((LINE, NEAR, LANES), F32),
        ((PICKED, LANES), F32),
        ((ROWS, LANES), F32),
        ((SHARE, HALF), F32),
    ]
    scratch = [
        pltpu.VMEM((KEYS, LANES), BF16),
        pltpu.VMEM((ROWS, WIDTH), BF16),
        pltpu.VMEM((ROWS, LOCAL * SIZE), BF16),
        pltpu.VMEM((SHARE, WIDTH), F32),
        pltpu.VMEM((4, SIZE, HALF), F32),
    ]
    return call(main_kernel, outs, arrays + (jnp.asarray(shared_levels()),), 0, scratch)


def far_return(choice_back, received, keep_far, keep_weight):
    args = (choice_back, received, keep_far, keep_weight)
    return call(far_return_kernel, [((FAR, NEAR + PART, LANES), BF16)], args, 0)[0]


def line_return(received, keep_line, far_in):
    return call(line_return_kernel, [((LINE, NEAR + PART, LANES), BF16)], (received, keep_line, far_in), 0)[0]


def spread_pieces(line_in, output_keep, first):
    outs = [((NEAR, LANES), F32), ((FAR * CORE, PART, LANES), BF16), ((SIZE, HALF), F32), ((SIZE, HALF), BF16)]
    return call(spread_kernel, outs, (line_in, output_keep, first), 0)


def finish(to_token, keep_own, received, near_sum):
    outs = [((LOCAL, SIZE, 2 * SIZE), BF16)] * 2
    return call(finish_kernel, outs, (to_token, keep_own, received, near_sum), 0, [pltpu.VMEM((ROWS, LANES), F32)])


def weight_rows(spread_in, output_sum, second):
    return call(weight_kernel, [((SHARE, WIDTH), F32), ((SIZE, HALF), BF16)], (spread_in, output_sum, second), 0)


def trade(pieces, groups):
    return lax.all_to_all(pieces, "seq", 0, 0, axis_index_groups=groups, tiled=True)


def swap_cores(block):
    return lax.ppermute(block, "seq", [(i, i ^ 1) for i in range(FAR * LINE * CORE)])


def swap_heads(block, way):
    return lax.ppermute(block, "head", [(i, i ^ way) for i in range(4)])


def shards(queries, keys, values, out_weight, offsets, out_grad):
    head_group = [HEAD_FIRST ^ slot for slot in range(4)]
    far_groups, far_back_groups = (
        [[(first ^ slot) * 16 + low for slot in range(FAR)] for low in range(16)] for first in (FAR_FIRST, FAR_BACK)
    )
    line_groups, line_back_groups = (
        [[far * 16 + (first ^ slot) * 2 + core for slot in range(LINE)] for far in range(FAR) for core in range(CORE)]
        for first in (LINE_FIRST, LINE_BACK)
    )
    spread_groups = [
        [(SPREAD_FIRST ^ slot) * 16 + line * 2 + (SPREAD_CORE ^ core) for slot in range(FAR) for core in range(CORE)]
        for line in range(LINE)
    ]
    queries, keys, values = (array.transpose(1, 0, 2) for array in (queries, keys, values))
    ordered, line_out = start(offsets, keys, values)
    to_order, to_token, query, choice, choice_back, grads_out = tables(offsets, queries, out_grad)
    line_in = trade(line_out, line_groups)
    far_out = far_pieces(ordered, line_in)
    other_in = swap_cores(line_in)
    far_in = trade(far_out, far_groups)
    other_far_in = swap_cores(far_in)
    grads = lax.all_to_all(grads_out, "head", 0, 0, axis_index_groups=[head_group], tiled=True)
    output_keep, output_send, query_grad, send, keep_line, keep_far, keep_own, keep_weight = attention(
        to_order, to_token, query, choice, out_weight, grads, ordered, line_in, far_in, other_in, other_far_in
    )
    first = swap_heads(output_send, 1)
    received = swap_cores(send)
    far_back = trade(far_return(choice_back, received, keep_far, keep_weight), far_back_groups)
    line_back = trade(line_return(received, keep_line, far_back), line_back_groups)
    near_sum, spread_out, output_sum, second_out = spread_pieces(line_back, output_keep, first)
    second = swap_heads(second_out, 3)
    spread_in = trade(spread_out, spread_groups)
    key_grad, value_grad = finish(to_token, keep_own, received, near_sum)
    weight_grad, output = weight_rows(spread_in, output_sum, second)
    query_grad, key_grad, value_grad = (grad.transpose(1, 0, 2) for grad in (query_grad, key_grad, value_grad))
    return (output, query_grad, key_grad, value_grad, weight_grad)


def solution(mesh):
    return jax.shard_map(
        shards,
        mesh=mesh,
        in_specs=(
            P("seq", "head", None),
            P("seq", "head", None),
            P("seq", "head", None),
            P("head", None),
            P("head"),
            P("seq", "head"),
        ),
        out_specs=(
            P("seq", "head"),
            P("seq", "head", None),
            P("seq", "head", None),
            P("seq", "head", None),
            P("head", None),
        ),
        check_vma=False,
    )
```

```python
import math

import jax
import jax.numpy as jnp
import numpy as np
from jax import lax
from jax.experimental import pallas as pl
from jax.experimental.pallas import tpu as pltpu
from jax.sharding import PartitionSpec as P

FAR, LINE, CORE = 8, 8, 2
FAR_FIRST, LINE_FIRST, HEAD_FIRST = 3, 6, 3
FAR_BACK, LINE_BACK, SPREAD_FIRST, SPREAD_CORE = 3, 5, 1, 1
ROWS = 128
LOCAL = 3
SIZE = 64
LANES = LOCAL * 2 * SIZE
WIDTH = 768
HALF = WIDTH // 2
SCALE = SIZE**-0.5
NEAR = 32
EACH = 4
PICKED = 96
SLOTS = LINE * NEAR
LINE_AT = ROWS
FAR_AT = LINE_AT + SLOTS - NEAR
PARTNER_AT = FAR_AT + PICKED
OTHER_AT = PARTNER_AT + NEAR
OTHER_FAR_AT = OTHER_AT + SLOTS
KEYS = OTHER_FAR_AT + PICKED
SHARE = 192
PART = SHARE // FAR
SEND_FAR = SLOTS + NEAR
SEND_WEIGHT = SEND_FAR + PICKED
SEND = SEND_WEIGHT + SHARE

NT = (((1,), (1,)), ((), ()))
TN = (((0,), (0,)), ((), ()))
NN = (((1,), (0,)), ((), ()))
BF16 = jnp.bfloat16
F32 = jnp.float32


def dot(a, b, dims=NN):
    return lax.dot_general(a, b, dims, preferred_element_type=F32)


def depth_of(row):
    return 7 if row == 0 else 7 - row.bit_length()


def far_table():
    table = [(1, row) for line in range(LINE) for row in range(4)]
    table += [(far, row) for far in (2, 3) for line in range(LINE) for row in range(2)]
    return table + [(far, 0) for far in range(4, 8) for line in range(LINE)]


def key_table():
    table = [(-1, depth_of(row)) for row in range(ROWS)]
    for core in range(CORE):
        if core:
            table += [(0, depth_of(NEAR + row)) for row in range(NEAR)]
        for line in range(1 - core, LINE):
            table += [(line.bit_length(), depth_of(row)) for row in range(NEAR)]
        table += [(3 + far.bit_length(), depth_of(row)) for far, row in far_table()]
    return table


def shared_levels():
    table = key_table()
    bias = np.full((KEYS, ROWS), -1e30, np.float32)
    for key, entry in enumerate(table):
        for query in range(ROWS):
            count = min(entry[1], depth_of(query)) - entry[0]
            if count > 0:
                bias[key, query] = math.log(count)
    return bias


def reversed_bits(row):
    out = row * 0
    for bit in range(7):
        out = out | ((row >> bit) & 1) << (6 - bit)
    return out


def token_of(row):
    return jnp.where(row < SIZE, 2 * row, 2 * row - (ROWS - 1))


def one_hot(match):
    return jnp.where(match, 1.0, 0.0).astype(BF16)


def here():
    index = lax.axis_index("seq")
    return (index >> 4) ^ FAR_FIRST, ((index >> 1) & 7) ^ LINE_FIRST, index & 1, lax.axis_index("head")


def order_from(offset, row_axis):
    row = lax.broadcasted_iota(jnp.int32, (ROWS, ROWS), row_axis)
    token = token_of(lax.broadcasted_iota(jnp.int32, (ROWS, ROWS), 1 - row_axis))
    return one_hot(((reversed_bits(row) + offset) & (ROWS - 1)) == token)


def lane_iota(shape):
    return lax.broadcasted_iota(jnp.int32, shape, len(shape) - 1)


def beside(first, second):
    low = lane_iota(first.shape) < SIZE
    even = jnp.where(low, first, pltpu.roll(second, SIZE, 1))
    odd = jnp.where(low, pltpu.roll(first, SIZE, 1), second)
    return jnp.concatenate([even, odd], axis=0).astype(BF16)


def start_kernel(offsets_far, keys, values, ordered, line_out, offsets, keys_here, values_here, done):
    copies = [
        pltpu.make_async_copy(source, target, done.at[at])
        for at, (source, target) in enumerate(((offsets_far, offsets), (keys, keys_here), (values, values_here)))
    ]
    for copy in copies:
        copy.start()
    copies[0].wait()
    orders = [order_from(offsets[head], 0) for head in range(LOCAL)]
    for copy in copies[1:]:
        copy.wait()
    for head in range(LOCAL):
        lanes = pl.ds(head * 2 * SIZE, 2 * SIZE)
        both = beside(keys_here[head].astype(F32), values_here[head].astype(F32))
        ordered[:, lanes] = dot(orders[head], both).astype(BF16)
    for slot in range(LINE):
        line_out[slot] = ordered[0:NEAR, :]


def far_place(row, far):
    second, third = row - 32, row - 64
    distance = jnp.where(row < 32, 1, jnp.where(row < 64, 2 + (second >> 4), 4 + (third >> 3)))
    line = jnp.where(row < 32, row >> 2, jnp.where(row < 64, (second >> 1) & 7, third & 7))
    index = jnp.where(row < 32, row & 3, jnp.where(row < 64, second & 1, 0))
    return ((far ^ distance) * LINE + line) * EACH + index


def far_choice(far, row_axis):
    shape = (PICKED, FAR * NEAR) if row_axis == 0 else (FAR * NEAR, PICKED)
    row = lax.broadcasted_iota(jnp.int32, shape, row_axis)
    return one_hot(far_place(row, far) == lax.broadcasted_iota(jnp.int32, shape, 1 - row_axis))


def table_kernel(offsets, queries, grad, to_order, to_token, query, choice, choice_back, grads_out):
    for slot in range(4):
        grads_out[slot] = grad[...]
    for head in range(LOCAL):
        order = order_from(offsets[head], 0)
        pairs = queries[head].astype(F32)
        to_order[head] = order
        to_token[head] = order_from(offsets[head], 1)
        query[head] = (dot(order, beside(pairs, jnp.zeros_like(pairs))) * SCALE).astype(BF16)
    far = here()[0]
    choice[...] = far_choice(far, 0)
    choice_back[...] = far_choice(far ^ FAR_FIRST ^ FAR_BACK, 1)


def far_kernel(ordered, line_in, far_out):
    low = lax.broadcasted_iota(jnp.int32, (8, LANES), 0) < EACH
    for pair in range(LINE // 2):
        first, second = (line_in[2 * pair + slot, 0:16, :].astype(F32)[:8] for slot in range(2))
        rows = jnp.where(low, first, pltpu.roll(second, EACH, 0)).astype(BF16)
        for slot in range(FAR):
            far_out[slot, pair * 8 : (pair + 1) * 8, :] = rows
    far_out[here()[0]] = ordered[NEAR : 2 * NEAR, :]


def main_kernel(
    to_order, to_token, query, choice, weight, grads, ordered, line_in, far_in, other_in, other_far_in, bias,
    output_keep, output_send, query_grad, send, keep_line, keep_far, keep_own, keep_weight,
    held, full_grad, attn, weight_term, parts,
):
    far, line, core, mine = here()
    held[0:ROWS, :] = ordered[...]
    held[PARTNER_AT:OTHER_AT, :] = other_far_in[far]
    held[FAR_AT:PARTNER_AT, :] = dot(choice[...], far_in[...].reshape(FAR * NEAR, LANES)).astype(BF16)
    held[OTHER_FAR_AT:, :] = dot(choice[...], other_far_in[...].reshape(FAR * NEAR, LANES)).astype(BF16)
    for step in range(LINE):
        slot = line ^ step
        if step:
            at = LINE_AT + (step - 1) * NEAR
            held[at : at + NEAR, :] = line_in[slot]
        at = OTHER_AT + step * NEAR
        held[at : at + NEAR, :] = other_in[slot]
    for parity in range(2):
        for half in range(2):
            place = (slice(parity * SIZE, (parity + 1) * SIZE), slice(half * HALF, (half + 1) * HALF))
            full_grad[place] = grads[HEAD_FIRST ^ (2 * parity + half)]
    heads = range(LOCAL)
    lanes = [pl.ds(head * 2 * SIZE, 2 * SIZE) for head in heads]
    grad = dot(full_grad[...], weight[...], NT).astype(BF16)
    zeros = jnp.zeros((ROWS, SIZE), BF16)
    grad = [jnp.concatenate([zeros, grad[:, head * SIZE : (head + 1) * SIZE]], axis=1) for head in heads]
    grad = [dot(to_order[head], grad[head]).astype(BF16) for head in heads]
    blocks = [jnp.concatenate([query[head], grad[head]], axis=0) for head in heads]
    sides = [held[:, lanes[head]].T for head in heads]
    scores = [dot(held[:, lanes[head]], query[head], NT) + bias[...] for head in heads]
    top = [jnp.max(scores[head], axis=0, keepdims=True) for head in heads]
    expd = [jnp.exp(scores[head] - top[head]) for head in heads]
    share = [1.0 / jnp.sum(expd[head], axis=0, keepdims=True) for head in heads]
    probs = [expd[head] * share[head] for head in heads]
    rounded = [probs[head].astype(BF16) for head in heads]
    attn_head = [dot(sides[head][SIZE:], rounded[head]).astype(BF16) for head in heads]
    grad_side = [grad[head].astype(F32).T[SIZE:, :] for head in heads]
    delta = [jnp.sum(grad_side[head] * attn_head[head].astype(F32), axis=0, keepdims=True) for head in heads]
    dprob = [dot(held[:, lanes[head]], grad[head], NT) for head in heads]
    dscore = [(probs[head] * (dprob[head] - delta[head])).astype(BF16) for head in heads]
    dquery = [(dot(sides[head][:SIZE], dscore[head]) * SCALE).astype(BF16) for head in heads]
    dboth = [dot(jnp.concatenate([dscore[head], rounded[head]], axis=1), blocks[head]) for head in heads]
    for head in heads:
        attn[:, head * SIZE : (head + 1) * SIZE] = dot(to_token[head], attn_head[head], NT).astype(BF16)
        by_token = dot(to_token[head], jnp.concatenate([dquery[head], jnp.zeros_like(dquery[head])], axis=0), NT)
        query_grad[head] = (by_token[:SIZE] + pltpu.roll(by_token[SIZE:], SIZE, 1)).astype(BF16)
        keep_own[:, lanes[head]] = dboth[head][0:ROWS]
        keep_far[:, lanes[head]] = dboth[head][FAR_AT:PARTNER_AT]
        send[SLOTS:SEND_FAR, lanes[head]] = dboth[head][PARTNER_AT:OTHER_AT].astype(BF16)
        send[SEND_FAR:SEND_WEIGHT, lanes[head]] = dboth[head][OTHER_FAR_AT:].astype(BF16)
        for step in range(LINE):
            slot = line ^ step
            at = LINE_AT + (step - 1) * NEAR
            keep_line[slot, :, lanes[head]] = dboth[head][at : at + NEAR] if step else jnp.zeros((NEAR, 2 * SIZE), F32)
            at = OTHER_AT + step * NEAR
            rows = pl.ds(pl.multiple_of(slot * NEAR, NEAR), NEAR)
            send[rows, lanes[head]] = dboth[head][at : at + NEAR].astype(BF16)
    part = dot(attn[...], weight[...])
    for parity in range(2):
        for half in range(2):
            piece = part[parity * SIZE : (parity + 1) * SIZE, half * HALF : (half + 1) * HALF]
            parts[2 * parity + half] = piece
    for step, way in ((0, 0), (1, 3)):
        output_keep[step] = parts[mine ^ way]
        output_send[step] = parts[mine ^ way ^ 1].astype(BF16)
    weight_term[...] = dot(attn[...], full_grad[...], TN)
    rows = SHARE // 2
    mine = pl.ds(pl.multiple_of(core * rows, 8), rows)
    theirs = pl.ds(pl.multiple_of((1 - core) * rows, 8), rows)
    for half in range(2):
        columns = pl.ds(half * HALF, HALF)
        keep_weight[half * rows : (half + 1) * rows, :] = weight_term[mine, columns]
        at = SEND_WEIGHT + half * rows
        send[at : at + rows, :] = weight_term[theirs, columns].astype(BF16)


def far_return_kernel(choice_back, received, keep_far, keep_weight, far_out):
    picked = (keep_far[...] + received[SEND_FAR:SEND_WEIGHT, :].astype(F32)).astype(BF16)
    rows = dot(choice_back[...], picked).astype(BF16)
    weight = (keep_weight[...] + received[SEND_WEIGHT:, :].astype(F32)).astype(BF16)
    for slot in range(FAR):
        far_out[slot, 0:NEAR, :] = rows[slot * NEAR : (slot + 1) * NEAR]
        far_out[slot, NEAR:, :] = weight[slot * PART : (slot + 1) * PART]


def line_return_kernel(received, keep_line, far_in, line_out):
    total = far_in[0].astype(F32)
    for slot in range(1, FAR):
        total = total + far_in[slot].astype(F32)
    low = lax.broadcasted_iota(jnp.int32, (8, LANES), 0) < EACH
    for slot in range(LINE):
        rows = keep_line[slot] + received[slot * NEAR : (slot + 1) * NEAR, :].astype(F32)
        both = total[slot // 2 * 8 : slot // 2 * 8 + 8]
        first = jnp.where(low, pltpu.roll(both, EACH, 0) if slot % 2 else both, 0.0)
        back = slot ^ LINE_FIRST ^ LINE_BACK
        line_out[back, 0:NEAR, :] = jnp.concatenate([rows[:8] + first, rows[8:]], axis=0).astype(BF16)
        line_out[back, NEAR:, :] = total[NEAR:].astype(BF16)


def spread_kernel(line_in, output_keep, first, near_sum, spread_out, output_sum, second_out):
    output_sum[...] = output_keep[0] + first[0].astype(F32)
    second_out[...] = (output_keep[1] + first[1].astype(F32)).astype(BF16)
    total = line_in[0].astype(F32)
    for slot in range(1, LINE):
        total = total + line_in[slot].astype(F32)
    near_sum[...] = total[:NEAR]
    part = total[NEAR:].astype(BF16)
    for slot in range(FAR * CORE):
        spread_out[slot] = part


def finish_kernel(to_token, keep_own, received, near_sum, key_grad, value_grad, own):
    own[...] = keep_own[...]
    own[NEAR : 2 * NEAR, :] += received[SLOTS:SEND_FAR, :].astype(F32)
    own[0:NEAR, :] += near_sum[...]
    for head in range(LOCAL):
        both = own[:, head * 2 * SIZE : (head + 1) * 2 * SIZE].astype(BF16)
        both = dot(to_token[head], both)
        even, odd = both[:SIZE], both[SIZE:]
        low = lane_iota(even.shape) < SIZE
        key_grad[head] = jnp.where(low, even, pltpu.roll(odd, SIZE, 1)).astype(BF16)
        value_grad[head] = jnp.where(low, pltpu.roll(even, SIZE, 1), odd).astype(BF16)


def weight_kernel(spread_in, output_sum, second, weight_grad, output):
    output[...] = (output_sum[...] + second[...].astype(F32)).astype(BF16)
    for share in range(FAR):
        half, row = share // 4, share % 4 * PART
        for core in range(CORE):
            at = core * SHARE // 2 + row
            slot = CORE * (share ^ FAR_BACK ^ SPREAD_FIRST) + (core ^ SPREAD_CORE)
            weight_grad[at : at + PART, half * HALF : (half + 1) * HALF] = spread_in[slot].astype(F32)


def call(kernel, outs, args, scalars, scratch=(), space=pltpu.VMEM):
    return pl.pallas_call(
        kernel,
        out_shape=[jax.ShapeDtypeStruct(shape, dtype) for shape, dtype in outs],
        in_specs=[pl.BlockSpec(memory_space=pltpu.SMEM)] * scalars
        + [pl.BlockSpec(memory_space=space)] * (len(args) - scalars),
        out_specs=[pl.BlockSpec(memory_space=pltpu.VMEM)] * len(outs),
        scratch_shapes=list(scratch),
        compiler_params=pltpu.CompilerParams(vmem_limit_bytes=48 * 2**20),
    )(*args)


def start(offsets, keys, values):
    outs = [((ROWS, LANES), BF16), ((LINE, NEAR, LANES), BF16)]
    here = pltpu.VMEM((LOCAL, SIZE, 2 * SIZE), BF16)
    scratch = [pltpu.SMEM((LOCAL,), jnp.int32), here, here, pltpu.SemaphoreType.DMA((3,))]
    args = (pltpu.with_memory_space_constraint(array, pltpu.HBM) for array in (offsets, keys, values))
    return call(start_kernel, outs, tuple(args), 0, scratch, pltpu.HBM)


def tables(offsets, queries, grad):
    square = (LOCAL, ROWS, ROWS)
    outs = [(square, BF16)] * 3 + [((PICKED, FAR * NEAR), BF16), ((FAR * NEAR, PICKED), BF16)]
    return call(table_kernel, outs + [((4, SIZE, HALF), BF16)], (offsets, queries, grad), 1)


def far_pieces(ordered, line_in):
    return call(far_kernel, [((FAR, NEAR, LANES), BF16)], (ordered, line_in), 0)[0]


def attention(*arrays):
    outs = [
        ((2, SIZE, HALF), F32),
        ((2, SIZE, HALF), BF16),
        ((LOCAL, SIZE, 2 * SIZE), BF16),
        ((SEND, LANES), BF16),
        ((LINE, NEAR, LANES), F32),
        ((PICKED, LANES), F32),
        ((ROWS, LANES), F32),
        ((SHARE, HALF), F32),
    ]
    scratch = [
        pltpu.VMEM((KEYS, LANES), BF16),
        pltpu.VMEM((ROWS, WIDTH), BF16),
        pltpu.VMEM((ROWS, LOCAL * SIZE), BF16),
        pltpu.VMEM((SHARE, WIDTH), F32),
        pltpu.VMEM((4, SIZE, HALF), F32),
    ]
    return call(main_kernel, outs, arrays + (jnp.asarray(shared_levels()),), 0, scratch)


def far_return(choice_back, received, keep_far, keep_weight):
    args = (choice_back, received, keep_far, keep_weight)
    return call(far_return_kernel, [((FAR, NEAR + PART, LANES), BF16)], args, 0)[0]


def line_return(received, keep_line, far_in):
    return call(line_return_kernel, [((LINE, NEAR + PART, LANES), BF16)], (received, keep_line, far_in), 0)[0]


def spread_pieces(line_in, output_keep, first):
    outs = [((NEAR, LANES), F32), ((FAR * CORE, PART, LANES), BF16), ((SIZE, HALF), F32), ((SIZE, HALF), BF16)]
    return call(spread_kernel, outs, (line_in, output_keep, first), 0)


def finish(to_token, keep_own, received, near_sum):
    outs = [((LOCAL, SIZE, 2 * SIZE), BF16)] * 2
    return call(finish_kernel, outs, (to_token, keep_own, received, near_sum), 0, [pltpu.VMEM((ROWS, LANES), F32)])


def weight_rows(spread_in, output_sum, second):
    return call(weight_kernel, [((SHARE, WIDTH), F32), ((SIZE, HALF), BF16)], (spread_in, output_sum, second), 0)


def trade(pieces, groups):
    return lax.all_to_all(pieces, "seq", 0, 0, axis_index_groups=groups, tiled=True)


def swap_cores(block):
    return lax.ppermute(block, "seq", [(i, i ^ 1) for i in range(FAR * LINE * CORE)])


def swap_heads(block, way):
    return lax.ppermute(block, "head", [(i, i ^ way) for i in range(4)])


def shards(queries, keys, values, out_weight, offsets, out_grad):
    head_group = [HEAD_FIRST ^ slot for slot in range(4)]
    far_groups, far_back_groups = (
        [[(first ^ slot) * 16 + low for slot in range(FAR)] for low in range(16)] for first in (FAR_FIRST, FAR_BACK)
    )
    line_groups, line_back_groups = (
        [[far * 16 + (first ^ slot) * 2 + core for slot in range(LINE)] for far in range(FAR) for core in range(CORE)]
        for first in (LINE_FIRST, LINE_BACK)
    )
    spread_groups = [
        [(SPREAD_FIRST ^ slot) * 16 + line * 2 + (SPREAD_CORE ^ core) for slot in range(FAR) for core in range(CORE)]
        for line in range(LINE)
    ]
    queries, keys, values = (array.transpose(1, 0, 2) for array in (queries, keys, values))
    ordered, line_out = start(offsets, keys, values)
    to_order, to_token, query, choice, choice_back, grads_out = tables(offsets, queries, out_grad)
    line_in = trade(line_out, line_groups)
    far_out = far_pieces(ordered, line_in)
    other_in = swap_cores(line_in)
    far_in = trade(far_out, far_groups)
    other_far_in = swap_cores(far_in)
    grads = lax.all_to_all(grads_out, "head", 0, 0, axis_index_groups=[head_group], tiled=True)
    output_keep, output_send, query_grad, send, keep_line, keep_far, keep_own, keep_weight = attention(
        to_order, to_token, query, choice, out_weight, grads, ordered, line_in, far_in, other_in, other_far_in
    )
    first = swap_heads(output_send, 1)
    received = swap_cores(send)
    far_back = trade(far_return(choice_back, received, keep_far, keep_weight), far_back_groups)
    line_back = trade(line_return(received, keep_line, far_back), line_back_groups)
    near_sum, spread_out, output_sum, second_out = spread_pieces(line_back, output_keep, first)
    second = swap_heads(second_out, 3)
    spread_in = trade(spread_out, spread_groups)
    key_grad, value_grad = finish(to_token, keep_own, received, near_sum)
    weight_grad, output = weight_rows(spread_in, output_sum, second)
    query_grad, key_grad, value_grad = (grad.transpose(1, 0, 2) for grad in (query_grad, key_grad, value_grad))
    return (output, query_grad, key_grad, value_grad, weight_grad)


def solution(mesh):
    return jax.shard_map(
        shards,
        mesh=mesh,
        in_specs=(
            P("seq", "head", None),
            P("seq", "head", None),
            P("seq", "head", None),
            P("head", None),
            P("head"),
            P("seq", "head"),
        ),
        out_specs=(
            P("seq", "head"),
            P("seq", "head", None),
            P("seq", "head", None),
            P("seq", "head", None),
            P("head", None),
        ),
        check_vma=False,
    )
```
